32 devices in a mesh: expert: 16 (over z, y, x), ffn: 2 (over core).
Axes of the slice: x: 2, y: 2, z: 4, core: 2. Of those that a mesh axis runs over, the one named last changes fastest.
Arguments:
- tokens: bfloat16 [16384, 768], P(('expert', 'ffn')), may hold values from -6 to 6
- gain_attn: float32 [768], replicated, may hold values from 0.5 to 1.5
- query_weight: bfloat16 [768, 768], replicated, may hold values from -0.109375 to 0.109375
- key_weight: bfloat16 [768, 768], replicated, may hold values from -0.109375 to 0.109375
- value_weight: bfloat16 [768, 768], replicated, may hold values from -0.21875 to 0.21875
- out_weight: bfloat16 [768, 768], replicated, may hold values from -0.625 to 0.625
- rel_bias: float32 [32, 12], replicated, may hold values from -4 to 4
- gain_ffn: float32 [768], replicated, may hold values from 0.5 to 1.5
- router_weight: bfloat16 [768, 16], replicated, may hold values from -0.109375 to 0.109375
- expert_in: bfloat16 [16, 768, 3072], P('expert', None, 'ffn'), may hold values from -0.21875 to 0.21875
- expert_out: bfloat16 [16, 3072, 768], P('expert', 'ffn'), may hold values from -6 to 6
- routes: int32 [16384, 1], P(('expert', 'ffn')), may hold values from 0 to 15; in each aligned block of 512 rows (0 to 511, 512 to 1023, ...) at most 64 rows name the same one
- capacity: int32 [32], P(('expert', 'ffn')), may hold values from 1 to 2
- cotangent: bfloat16 [16384, 768], P(('expert', 'ffn')), may hold values from -6 to 6
Outputs:
- output: bfloat16 [16384, 768], P(('expert', 'ffn'))
- input_grad: float32 [16384, 768], P(('expert', 'ffn'))
- grad_gain_attn: float32 [768], replicated
- grad_query: float32 [768, 768], replicated
- grad_key: float32 [768, 768], replicated
- grad_value: float32 [768, 768], replicated
- grad_out: float32 [768, 768], replicated
- grad_rel_bias: float32 [32, 12], replicated
- grad_gain_ffn: float32 [768], replicated
- grad_router: float32 [768, 16], replicated
- grad_expert_in: float32 [16, 768, 3072], P('expert', None, 'ffn')
- grad_expert_out: float32 [16, 3072, 768], P('expert', 'ffn')
- rms_values: float32 [2, 16384], P(None, ('expert', 'ffn'))
The draws below stay inside these ranges and needn't reach their ends.
Inputs may be any that keep to these rules, and one draw needn't show every extreme that they name: routes[t, 0] is the expert of token t; among the rows of one device (aligned blocks of 512 rows) no expert is named more than 64 times, a bound that some block reaches. capacity[g] is the capacity factor of group g.
All inputs are finite; a program needn't handle non-finite values.
Results may differ from the reference program's by a relative error of at most 0.019.
Values may be sent and summed in bfloat16 or wider, within the bound.
A program may use at most 192 MiB of HBM per device.

```python
import math
from functools import partial
import jax
import jax.numpy as jnp
import numpy as np
from jax import lax

D = 768
HEADS = 12
HEAD_DIM = 64
FF = 3072
BUCKETS = 32
SEQ = 512
SEQS_DEV = 1
TOK_DEV = 512
EXPERTS = 16
TOKENS = 16384
GROUPS = 32
CAP = 64


def touch_ends(drawn, key, smallest, top_value):
    dims = drawn.shape
    place = [jax.random.randint(jax.random.fold_in(key, axis), (), 0, dims[axis]) for axis in range(len(dims))]
    drawn = drawn.at[tuple(place)].set(smallest)
    longest = dims.index(max(dims))
    place[longest] = (place[longest] + 1) % dims[longest]
    return drawn.at[tuple(place)].set(top_value)


def level_of(rng, shape, shards, least, high):
    loudness, own = 1.0, jax.random.fold_in(rng, 6)
    for dim, blocks in shards:
        steps = jnp.exp(jax.random.uniform(jax.random.fold_in(own, dim), (blocks,), jnp.float32, least / len(shards), high / len(shards)))
        loudness = loudness * jnp.repeat(steps, shape[dim] // blocks).reshape([-1 if axis == dim else 1 for axis in range(len(shape))])
    return loudness


def deal_out(key, own, number, rows, number_of, top, reach, lean):
    order = jax.random.permutation(key, number_of)
    packed, common = shares(number_of, rows * top, reach, lean, True), shares(number_of, rows * top, reach, lean, False)
    places = jnp.arange(number_of)

    def named(lengths, offset_by):
        used = int((lengths > 0).sum())
        fixed = max(1, used // 4)
        passed = fixed + (places - fixed + offset_by * (used - fixed)) % max(1, number_of - fixed)
        return jnp.zeros((number_of,), jnp.int32).at[order[jnp.where(places < fixed, places, passed)]].set(jnp.asarray(lengths, jnp.int32))

    lengths = jnp.where(number % 4 == 0, named(packed, number // 4), named(common, number - number // 4 - 1))
    mixed = jax.random.permutation(jax.random.fold_in(own, 3), number_of)
    donor, receiver = mixed[0:number_of // 2 * 2:2], mixed[1:number_of // 2 * 2:2]
    slack = jnp.minimum(lengths[donor] - 1, reach - lengths[receiver]) // 2
    slack = jnp.where((donor == order[0]) | (receiver == order[0]) | (lengths[receiver] == 0), 0, jnp.maximum(slack, 0))
    passed = jax.random.randint(jax.random.fold_in(own, 4), (number_of // 2,), 0, 1 << 20) % (slack + 1)
    lengths = lengths.at[donor].add(-passed).at[receiver].add(passed)
    items = jnp.searchsorted(jnp.cumsum(lengths), jnp.arange(rows * top), side="right").astype(jnp.int32)
    table = items.reshape(top, rows).T
    table = table[jax.random.permutation(jax.random.fold_in(own, 1), rows)]
    offset_by = jax.random.randint(jax.random.fold_in(own, 2), (rows, 1), 0, top)
    return jnp.take_along_axis(table, (jnp.arange(top)[None, :] + offset_by) % top, axis=1)


def shares(count, total, reach, slope, full):
    weights = [(1 << 20) // math.isqrt(rank ** slope) + 1 for rank in range(1, count + 1)]
    largest = reach if full else min(reach, max(-(-total // count), total * weights[0] // sum(weights)))
    least = 1 if total - largest >= count - 1 else 0
    holding, spare = [largest] + [least] * (count - 1), total - largest - least * (count - 1)
    while spare > 0:
        movable = [i for i in range(1, count) if holding[i] < largest] or [i for i in range(1, count) if holding[i] < reach]
        whole, budget = sum([weights[i] for i in movable]), spare
        for i in movable:
            addition = min(reach - holding[i], max(1, budget * weights[i] // whole), spare)
            holding[i] = holding[i] + addition
            spare = spare - addition
    return np.array(holding)


def scatter_about(own_key, shape, scale, bound, cuts=(), held_as=jnp.bfloat16):
    entries = jax.random.normal(own_key, shape, jnp.float32) * scale
    if len(cuts) > 0:
        entries = level_of(own_key, shape, cuts, -0.22, 0.18) * entries
    return jnp.clip(entries, min=-bound, max=bound).astype(held_as)


def setup_inputs(seed: int = 0) -> dict:
    key_list = jax.random.split(jax.random.key(seed), 15)
    tokens = scatter_about(key_list[0], (TOKENS, D), 1.0, 6.0, ((0, 32),))
    gain_attn = jnp.clip(1.0 + 0.1 * jax.random.normal(key_list[1], (D,), jnp.float32), 0.5, 1.5)
    query_weight = scatter_about(key_list[2], (D, D), (4 * D) ** -0.5, 0.109375)
    key_weight = scatter_about(key_list[3], (D, D), (4 * D) ** -0.5, 0.109375)
    value_weight = scatter_about(key_list[4], (D, D), D ** -0.5, 0.21875)
    out_weight = scatter_about(key_list[5], (D, D), (D // 8) ** -0.5, 0.625)
    rel_bias = scatter_about(key_list[6], (BUCKETS, HEADS), 1.0, 4.0, (), jnp.float32)
    gain_ffn = jnp.clip(1.0 + 0.1 * jax.random.normal(key_list[7], (D,), jnp.float32), 0.5, 1.5)
    router_weight = scatter_about(key_list[8], (D, EXPERTS), (4 * D) ** -0.5, 0.109375)
    expert_in = scatter_about(key_list[9], (EXPERTS, D, FF), D ** -0.5, 0.21875, ((0, 16), (2, 2)))
    expert_out = scatter_about(key_list[10], (EXPERTS, FF, D), (0.025 * EXPERTS), 6.0, ((0, 16), (1, 2)))
    routes_keys = jax.random.split(jax.random.fold_in(key_list[11], 1), TOKENS // TOK_DEV)
    routes_turns = jax.random.permutation(jax.random.fold_in(key_list[11], 3), TOKENS // TOK_DEV)
    routes = jax.vmap(lambda own, number: deal_out(jax.random.fold_in(key_list[11], 2), own, number, TOK_DEV, EXPERTS, 1, CAP, 2))(routes_keys, routes_turns).reshape((TOKENS, 1))
    capacity = touch_ends(jax.random.randint(key_list[12], (GROUPS,), 1, 3), jax.random.fold_in(key_list[12], 1), 1, 2).astype(jnp.int32)
    cotangent = scatter_about(key_list[13], (TOKENS, D), 1.0, 6.0, ((0, 32),))
    return {"tokens": tokens, "gain_attn": gain_attn, "query_weight": query_weight, "key_weight": key_weight, "value_weight": value_weight, "out_weight": out_weight, "rel_bias": rel_bias, "gain_ffn": gain_ffn, "router_weight": router_weight, "expert_in": expert_in, "expert_out": expert_out, "routes": routes, "capacity": capacity, "cotangent": cotangent}


EPSILON = 1e-06
THRESHOLDS = (12, 16, 23, 32, 46, 64, 91)
HIGH = lax.Precision.HIGHEST

@jax.custom_vjp
def low(v):
    return lax.optimization_barrier(v.astype(jnp.bfloat16)).astype(jnp.float32)

@jax.custom_vjp
def low_back(v):
    return v

def low_keep(v):
    return (low(v), None)

def low_pass(kept, grad):
    return (grad,)

def back_keep(v):
    return (v, None)

def back_low(kept, grad):
    return (low(grad),)
low.defvjp(low_keep, low_pass)
low_back.defvjp(back_keep, back_low)

def bucket_table(length):
    places = jnp.arange(length, dtype=jnp.int32)
    offset = places[None, :] - places[:, None]
    distance = jnp.abs(offset)
    larger = 8 + sum(((distance >= limit).astype(jnp.int32) for limit in THRESHOLDS))
    return jnp.where(distance < 8, distance, larger) + 16 * (offset > 0).astype(jnp.int32)

def attention_block(inputs, gain_attn, query_weight, key_weight, value_weight, out_weight, rel_bias, buckets):
    batch = inputs.shape[0]
    squares = lax.optimization_barrier(jnp.mean(inputs * inputs, axis=-1, keepdims=True))
    normed = low(inputs * lax.rsqrt(squares + EPSILON) * gain_attn)

    def project(weight):
        made = jnp.einsum('bsd,de->bse', normed, weight, precision=HIGH)
        return low(low_back(made)).reshape(batch, SEQ, HEADS, HEAD_DIM)
    queries = project(query_weight)
    key_rows = project(key_weight)
    value_rows = project(value_weight)
    bias = jnp.transpose(rel_bias[buckets], (2, 0, 1))
    scores = low_back(jnp.einsum('bqhd,bkhd->bhqk', queries, key_rows, precision=HIGH) + bias[None])
    weights = low(jax.nn.softmax(scores, axis=-1))
    mixed = jnp.einsum('bhqk,bkhd->bqhd', weights, value_rows, precision=HIGH).reshape(batch, SEQ, D)
    mixed = low(low_back(mixed))
    branch = low_back(jnp.einsum('bsd,de->bse', mixed, out_weight, precision=HIGH))
    return (inputs + branch, jnp.sqrt(squares[..., 0] + EPSILON))

def expert_apply(operands):
    rows, weight_in, weight_out = operands
    inner = low_back(jnp.einsum('gcd,df->gcf', rows, weight_in, precision=HIGH))
    activated = low(jax.nn.gelu(inner, approximate=False))
    return low(low_back(jnp.einsum('gcf,fd->gcd', activated, weight_out, precision=HIGH)))

def forward(routes, capacity, tokens, gain_attn, query_weight, key_weight, value_weight, out_weight, rel_bias, gain_ffn, router_weight, expert_in, expert_out):
    groups = TOKENS // TOK_DEV
    buckets = bucket_table(SEQ)
    grouped = tokens.reshape(groups, SEQS_DEV, SEQ, D)
    block = jax.checkpoint(lambda piece: attention_block(piece, gain_attn, query_weight, key_weight, value_weight, out_weight, rel_bias, buckets))
    hidden_state, rms_attn = lax.map(block, grouped)
    hidden_state = hidden_state.reshape(TOKENS, D)
    squares = lax.optimization_barrier(jnp.mean(hidden_state * hidden_state, axis=-1, keepdims=True))
    normed = low(hidden_state * lax.rsqrt(squares + EPSILON) * gain_ffn)
    logits = low_back(jnp.dot(normed, router_weight, precision=HIGH))
    probs = jax.nn.softmax(logits, axis=-1)
    expert_ids = routes[:, 0].astype(jnp.int32)
    chosen = expert_ids[:, None] == jnp.arange(EXPERTS, dtype=jnp.int32)[None, :]
    chosen_mask = chosen.astype(jnp.float32)
    gate = lax.optimization_barrier(jnp.sum(probs * chosen_mask, axis=-1))
    chosen_int = chosen.astype(jnp.int32).reshape(groups, TOK_DEV, EXPERTS)
    earlier = jnp.cumsum(chosen_int, axis=1, dtype=jnp.int32) - chosen_int
    position = lax.optimization_barrier(jnp.sum(earlier * chosen_int, axis=-1, dtype=jnp.int32)).reshape(TOKENS)
    group_ids = (jnp.arange(TOKENS, dtype=jnp.int32) // TOK_DEV).astype(jnp.int32)
    live = (capacity.astype(jnp.int32)[group_ids] * TOK_DEV // EXPERTS).astype(jnp.int32)
    slot = jnp.where(position < live, expert_ids * CAP + position, EXPERTS * CAP).astype(jnp.int32)
    buffer = jnp.zeros((groups, EXPERTS * CAP + 1, D), jnp.float32).at[group_ids, slot].add(normed)
    dispatched = low_back(buffer[:, :EXPERTS * CAP].reshape(groups, EXPERTS, CAP, D))
    returned = lax.map(jax.checkpoint(expert_apply), (jnp.transpose(dispatched, (1, 0, 2, 3)), expert_in, expert_out))
    returned = jnp.transpose(returned, (1, 0, 2, 3)).reshape(groups, EXPERTS * CAP, D)
    padded = jnp.concatenate([returned, jnp.zeros((groups, 1, D), jnp.float32)], axis=1)
    picked = padded[group_ids, slot]
    final = hidden_state + gate[:, None] * picked
    rms_values = jnp.stack([rms_attn.reshape(TOKENS), jnp.sqrt(squares[:, 0] + EPSILON)])
    return (final, rms_values)

def reference(tokens, gain_attn, query_weight, key_weight, value_weight, out_weight, rel_bias, gain_ffn, router_weight, expert_in, expert_out, routes, capacity, cotangent):
    primals = (tokens.astype(jnp.float32), gain_attn.astype(jnp.float32), query_weight.astype(jnp.float32), key_weight.astype(jnp.float32), value_weight.astype(jnp.float32), out_weight.astype(jnp.float32), rel_bias.astype(jnp.float32), gain_ffn.astype(jnp.float32), router_weight.astype(jnp.float32), expert_in.astype(jnp.float32), expert_out.astype(jnp.float32))
    results, pullback = jax.vjp(partial(forward, routes, capacity), *primals)
    final, rms_values = results
    seeds = (cotangent.astype(jnp.float32), jnp.zeros_like(rms_values))
    grads = pullback(seeds)
    return (final.astype(jnp.bfloat16), grads[0], grads[1], grads[2], grads[3], grads[4], grads[5], grads[6], grads[7], grads[8], grads[9], grads[10], rms_values)
```

```python
import functools
import jax
import jax.numpy as jnp
from jax import lax
from jax.experimental import pallas as pl
from jax.experimental.pallas import tpu as pltpu
from jax.sharding import PartitionSpec as P

HEADS = 12
HEAD_DIM = 64
BUCKETS = 32
SEQ = 512
EPSILON = 1e-06
THRESHOLDS = (12, 16, 23, 32, 46, 64, 91)
HIGH = lax.Precision.HIGHEST
F32 = jnp.float32
BF16 = jnp.bfloat16
MESH = pl.DeviceIdType.MESH
LANES = 128


def dot(a, b, ca=1, cb=0, precision=None):
    return lax.dot_general(
        a, b, (((ca,), (cb,)), ((), ())), precision=precision, preferred_element_type=F32
    )


def iota(shape, dim):
    return lax.broadcasted_iota(jnp.int32, shape, dim)


def each(n, body):
    if n <= 16:
        for k in range(1, n):
            body(k)
    else:

        def step(k, carry):
            body(k)
            return carry

        lax.fori_loop(1, n, step, 0)


def greet(n, me, core, sibling):
    barrier = pltpu.get_barrier_semaphore()

    def signal(k):
        pl.semaphore_signal(
            barrier, inc=1, device_id=(lax.rem(me + k, n), core), device_id_type=MESH
        )

    each(n, signal)
    if sibling:
        pl.semaphore_signal(barrier, inc=1, device_id=(me, 1 - core), device_id_type=MESH)
    return barrier


def band_onehot():
    place = iota((BUCKETS, 4 * LANES), 1)
    offset = jnp.where(place < 2 * LANES, -place, 4 * LANES - place)
    distance = jnp.abs(offset)
    larger = jnp.full(distance.shape, 8, jnp.int32)
    for limit in THRESHOLDS:
        larger = larger + (distance >= limit).astype(jnp.int32)
    bucket = jnp.where(distance < 8, distance, larger) + jnp.where(offset > 0, 16, 0)
    return (bucket == iota(bucket.shape, 0)).astype(F32)


def pieces(row):
    high = row.astype(BF16)
    rest = row - high.astype(F32)
    middle = rest.astype(BF16)
    low = (rest - middle.astype(F32)).astype(BF16)
    filler = jnp.zeros((5, row.shape[1]), BF16)
    return jnp.concatenate([high, middle, low, filler], axis=0)


def attend_kernel(
    n, slots, pad,
    tok_ref, ga_ref, wq_ref, wk_ref, wv_ref, wo_ref, rel_ref, gf_ref, wrt_ref, routes_ref, cap_ref, cot_ref, win_ref, wout_ref,
    cr_ref, wi2_ref, wo2_ref, xd_ref, gs_ref, st_ref, nat_ref, qt_ref, kt_ref, v_ref, p_ref, mixt_ref, hid_ref, nf_ref, pr_ref, gcol_ref, rms_ref,
    cd_ref, s_ref, k_ref, vt_ref, band_ref, send_sem, recv_sem, own_sem, w_send, w_recv,
):
    me = lax.axis_index("expert")
    core = lax.axis_index("ffn")
    count, width = tok_ref.shape
    rows_all = n * pad
    barrier = greet(n, me, core, True)

    routes = routes_ref[...]
    chosen = (iota((n, count), 0) == routes).astype(F32)
    upper = (iota((count, count), 0) < iota((count, count), 1)).astype(F32).astype(BF16)
    earlier = dot(chosen.astype(BF16), upper)
    position = jnp.sum(earlier * chosen, axis=0, keepdims=True)
    live = (cap_ref[0] * count // n).astype(F32)
    slot = jnp.where(position < live, routes * pad + position.astype(jnp.int32), rows_all)

    @pl.loop(0, rows_all // 256)
    def _(block):
        start = pl.multiple_of(block * 256, 256)
        hot = (iota((256, count), 0) + start == slot).astype(F32).astype(BF16)
        s_ref[pl.ds(start, 256), :] = hot
        cd_ref[pl.ds(start, 256), :] = dot(hot, cot_ref[...]).astype(BF16)

    pl.semaphore_wait(barrier, n)

    def rows_of(e):
        return pl.ds(pl.multiple_of(e * pad, pad), pad)

    def copy(k):
        target = lax.rem(me + k, n)
        return pltpu.make_async_remote_copy(
            src_ref=cd_ref.at[rows_of(target)],
            dst_ref=cr_ref.at[rows_of(me)],
            send_sem=send_sem.at[k],
            recv_sem=recv_sem.at[k],
            device_id=(target, core),
            device_id_type=MESH,
        )

    each(n, lambda k: copy(k).start())
    own = pltpu.make_async_copy(cd_ref.at[rows_of(me)], cr_ref.at[rows_of(me)], own_sem)
    own.start()
    halves = [
        pltpu.make_async_remote_copy(
            src_ref=src,
            dst_ref=dst,
            send_sem=w_send.at[i],
            recv_sem=w_recv.at[i],
            device_id=(me, 1 - core),
            device_id_type=MESH,
        )
        for i, (src, dst) in enumerate(((win_ref, wi2_ref), (wout_ref, wo2_ref)))
    ]
    for half in halves:
        half.start()

    x = tok_ref[...].astype(F32)
    ms1 = jnp.mean(x * x, axis=-1, keepdims=True)
    na = (x * lax.rsqrt(ms1 + EPSILON) * ga_ref[...]).astype(BF16)
    nat_ref[...] = na.T
    qt_ref[...] = dot(na, wq_ref[...]).astype(BF16).T
    keys = dot(na, wk_ref[...]).astype(BF16)
    k_ref[...] = keys
    kt_ref[...] = keys.T
    values = dot(na, wv_ref[...]).astype(BF16)
    v_ref[...] = values
    vt_ref[...] = values.T
    band_ref[...] = dot(rel_ref[...], band_onehot(), 0, 0, HIGH)
    lower_half = iota((LANES, count), 0) < HEAD_DIM
    blocks = count // LANES

    @pl.loop(0, HEADS // 2)
    def _(pair):
        lanes = pl.ds(pl.multiple_of(pair * LANES, LANES), LANES)
        both = qt_ref[lanes, :]
        for sub in range(2):
            head = 2 * pair + sub
            mask = lower_half if sub == 0 else jnp.logical_not(lower_half)
            query = jnp.where(mask, both, jnp.zeros_like(both))
            line = band_ref[pl.ds(head, 1), :]
            band = pltpu.roll(
                jnp.broadcast_to(line, (LANES, 4 * LANES)), 0, 1, stride=1, stride_axis=0
            )
            before = jnp.broadcast_to(line[:, 255:256], (LANES, LANES))
            after = jnp.broadcast_to(line[:, 257:258], (LANES, LANES))
            by_gap = {
                0: band[:, :LANES],
                -1: band[:, LANES : 2 * LANES],
                1: band[:, 3 * LANES :],
            }
            scores = []
            for row in range(blocks):
                bias = jnp.concatenate(
                    [
                        by_gap.get(row - col, after if row > col else before)
                        for col in range(blocks)
                    ],
                    axis=1,
                )
                made = dot(k_ref[row * LANES : (row + 1) * LANES, lanes], query)
                scores.append(made + bias)
            scores = jnp.concatenate(scores, axis=0)
            peak = jnp.max(scores, axis=0, keepdims=True)
            expo = jnp.exp(scores - peak)
            total = jnp.sum(expo, axis=0, keepdims=True)
            probs = (expo * (1.0 / total)).astype(BF16)
            p_ref[head] = probs
            features = pl.ds(pl.multiple_of(head * HEAD_DIM, HEAD_DIM), HEAD_DIM)
            mixt_ref[features, :] = dot(vt_ref[features, :], probs).astype(BF16)

    hidden = tok_ref[...].astype(F32) + dot(mixt_ref[...].T, wo_ref[...])
    hid_ref[...] = hidden
    ms2 = jnp.mean(hidden * hidden, axis=-1, keepdims=True)
    nf = (hidden * lax.rsqrt(ms2 + EPSILON) * gf_ref[...]).astype(BF16)
    nf_ref[...] = nf
    logits = dot(wrt_ref[...], nf, 1, 1)
    top = jnp.max(logits, axis=0, keepdims=True)
    raised = jnp.exp(logits - top)
    router = raised / jnp.sum(raised, axis=0, keepdims=True)
    pr_ref[...] = router
    gate = jnp.sum(router * chosen, axis=0, keepdims=True)
    gcol_ref[...] = jnp.broadcast_to(gate, (LANES, count)).T
    roots = jnp.concatenate(
        [
            jnp.broadcast_to(jnp.sqrt(ms + EPSILON), (count, LANES)).T[:4]
            for ms in (ms1, ms2)
        ],
        axis=0,
    )
    rms_ref[...] = roots
    parts = pieces(gate)

    @pl.loop(0, rows_all // 256)
    def _(block):
        start = pl.multiple_of(block * 256, 256)
        hot = s_ref[pl.ds(start, 256), :]
        xd_ref[pl.ds(start, 256), :] = dot(hot, nf_ref[...]).astype(BF16)
        split = dot(parts, hot, 1, 1)
        gs_ref[:, pl.ds(start, 256)] = jnp.broadcast_to(
            jnp.sum(split, axis=0, keepdims=True), split.shape
        )
        st_ref[:, pl.ds(start, 256)] = hot.T

    own.wait()
    for half in halves:
        half.wait()
    each(n, lambda k: copy(k).wait())


def attend(n, slots, pad, tokens, ga, wq, wk, wv, wo, rel, gf, wrt, routes, cap, cot, win, wout):
    count, width = tokens.shape
    rows = n * pad
    half = win.shape[-1]
    vmem = pl.BlockSpec(memory_space=pltpu.VMEM)
    anywhere = pl.BlockSpec(memory_space=pl.ANY)
    smem = pl.BlockSpec(memory_space=pltpu.SMEM)
    shapes = (
        ((rows, width), BF16, anywhere),
        ((width, half), BF16, anywhere),
        ((half, width), BF16, anywhere),
        ((rows, width), BF16, vmem),
        ((8, rows), F32, vmem),
        ((count, rows), BF16, vmem),
        ((width, count), BF16, vmem),
        ((width, count), BF16, vmem),
        ((width, count), BF16, vmem),
        ((count, width), BF16, vmem),
        ((HEADS, count, count), BF16, vmem),
        ((width, count), BF16, vmem),
        ((count, width), F32, vmem),
        ((count, width), BF16, vmem),
        ((n, count), F32, vmem),
        ((count, LANES), F32, vmem),
        ((8, count), F32, vmem),
    )
    return pl.pallas_call(
        functools.partial(attend_kernel, n, slots, pad),
        out_shape=[jax.ShapeDtypeStruct(shape, dtype) for shape, dtype, _ in shapes],
        in_specs=[vmem] * 10 + [smem, vmem, anywhere, anywhere],
        out_specs=[space for _, _, space in shapes],
        scratch_shapes=[
            pltpu.VMEM((rows, width), BF16),
            pltpu.VMEM((rows, count), BF16),
            pltpu.VMEM((count, width), BF16),
            pltpu.VMEM((width, count), BF16),
            pltpu.VMEM((HEADS, 4 * LANES), F32),
            pltpu.SemaphoreType.DMA((n,)),
            pltpu.SemaphoreType.DMA((n,)),
            pltpu.SemaphoreType.DMA,
            pltpu.SemaphoreType.DMA((2,)),
            pltpu.SemaphoreType.DMA((2,)),
        ],
        compiler_params=pltpu.CompilerParams(
            collective_id=0, has_side_effects=True, vmem_limit_bytes=60 * 1024 * 1024
        ),
        name="attend",
    )(tokens, ga, wq, wk, wv, wo, rel, gf, wrt, routes, cap, cot, win, wout)


def bucket_onehot(length, count):
    places = jnp.arange(length, dtype=jnp.int32)
    offset = places[None, :] - places[:, None]
    distance = jnp.abs(offset)
    larger = 8 + sum(((distance >= limit).astype(jnp.int32) for limit in THRESHOLDS))
    bucket = jnp.where(distance < 8, distance, larger) + 16 * (offset > 0).astype(jnp.int32)
    return (bucket[:, :, None] == jnp.arange(count, dtype=jnp.int32)).astype(jnp.float32)


def rms_forward(values, gain):
    squares = jnp.mean(values * values, axis=-1, keepdims=True)
    scale = lax.rsqrt(squares + EPSILON)
    return (values * scale * gain, scale, jnp.sqrt(squares[:, 0] + EPSILON))


def rms_backward(values, scale, gain, upstream):
    weighted = upstream * gain
    grad_gain = jnp.sum(upstream * values * scale, axis=0)
    inner_mean = jnp.mean(weighted * values, axis=-1, keepdims=True)
    return (scale * weighted - values * scale * scale * scale * inner_mean, grad_gain)


def gelu_slope(values):
    normal_cdf = 0.5 * (1.0 + lax.erf(values * 2.0 ** (-0.5)))
    density = jnp.exp(-0.5 * values * values) * (2.0 * jnp.pi) ** (-0.5)
    return normal_cdf + values * density


def per_device(
    tokens,
    gain_attn,
    query_weight,
    key_weight,
    value_weight,
    out_weight,
    rel_bias,
    gain_ffn,
    router_weight,
    expert_in,
    expert_out,
    routes,
    capacity,
    cotangent,
):
    tok_count, width = tokens.shape
    seq_count = tok_count // SEQ
    experts = router_weight.shape[1]
    n_expert = lax.axis_size("expert")
    local_experts = experts // n_expert
    slots = 2 * tok_count // experts
    n = n_expert
    pad = -(-slots // 16) * 16
    (
        cots, other_in, other_out, dispatched, slot_gates, slots_t, normed_t, query_t, key_t, values, probs_t, mixed_t,
        hidden_state, normed_ffn, router_t, gate_col, roots,
    ) = attend(
        n, slots, pad, tokens, gain_attn[None], query_weight, key_weight, value_weight, out_weight, rel_bias, gain_ffn[None],
        router_weight.T, routes.reshape(1, tok_count), capacity, cotangent, expert_in[0], expert_out[0],
    )
    inputs = tokens.astype(jnp.float32)
    normed_attn = normed_t.T
    queries = query_t.T.reshape(1, SEQ, HEADS, HEAD_DIM)
    key_rows = key_t.T.reshape(1, SEQ, HEADS, HEAD_DIM)
    value_rows = values.reshape(1, SEQ, HEADS, HEAD_DIM)
    mixed = mixed_t.T
    scale_attn = lax.rsqrt(jnp.mean(inputs * inputs, axis=-1, keepdims=True) + EPSILON)
    scale_ffn = lax.rsqrt(jnp.mean(hidden_state * hidden_state, axis=-1, keepdims=True) + EPSILON)
    root_attn, root_ffn = roots[0], roots[4]
    router_probs = router_t.T
    gate = gate_col[:, 0]
    onehot_table = bucket_onehot(SEQ, BUCKETS)
    expert_ids = routes[:, 0]
    chosen_mask = (expert_ids[:, None] == jnp.arange(experts, dtype=jnp.int32)[None, :]).astype(jnp.float32)
    chosen_int = chosen_mask.astype(jnp.int32)
    earlier = jnp.cumsum(chosen_int, axis=0, dtype=jnp.int32) - chosen_int
    position = jnp.sum(earlier * chosen_int, axis=-1, dtype=jnp.int32)
    live = capacity[0] * tok_count // experts
    slot = jnp.where(position < live, expert_ids * pad + position, experts * pad)
    received = lax.all_to_all(
        dispatched.reshape(n, 1, pad, width), "expert", split_axis=0, concat_axis=0, tiled=True
    )
    core = lax.axis_index("ffn")
    weight_in_all = jnp.where(
        core == 0,
        jnp.concatenate([expert_in[0], other_in], axis=1),
        jnp.concatenate([other_in, expert_in[0]], axis=1),
    )[None]
    weight_out_all = jnp.where(
        core == 0,
        jnp.concatenate([expert_out[0], other_out], axis=0),
        jnp.concatenate([other_out, expert_out[0]], axis=0),
    )[None]
    inner = jnp.einsum(
        "secd,edf->secf", received, weight_in_all, preferred_element_type=jnp.float32
    )
    activated = jax.nn.gelu(inner, approximate=False).astype(jnp.bfloat16)
    produced = jnp.einsum(
        "secf,efd->secd", activated, weight_out_all, preferred_element_type=jnp.float32
    )
    returned = lax.all_to_all(
        produced.astype(jnp.bfloat16), "expert", split_axis=0, concat_axis=0, tiled=True
    )
    padded = jnp.concatenate(
        [returned.reshape(experts * pad, width), jnp.zeros((1, width), jnp.bfloat16)], axis=0
    )
    picked = padded[slot].astype(jnp.float32)
    final = hidden_state + gate[:, None] * picked
    upstream = cotangent.astype(jnp.float32)
    grad_gate = jnp.sum(upstream * picked, axis=-1)
    gates = lax.all_to_all(slot_gates[0].reshape(n, 1, pad, 1), "expert", split_axis=0, concat_axis=0, tiled=True)
    grad_received = (gates * cots.reshape(n, 1, pad, width).astype(jnp.float32)).astype(jnp.bfloat16)
    grad_act = jnp.einsum(
        "secd,efd->secf", grad_received, weight_out_all, preferred_element_type=jnp.float32
    )
    grad_inner = (grad_act * gelu_slope(inner)).astype(jnp.bfloat16)
    full_out = jnp.einsum(
        "secf,secd->efd", activated, grad_received, preferred_element_type=jnp.float32
    )
    full_in = jnp.einsum("secd,secf->edf", received, grad_inner, preferred_element_type=jnp.float32)
    grad_expert_in, grad_expert_out = (
        lax.psum_scatter(
            full_in.astype(jnp.bfloat16), "ffn", scatter_dimension=2, tiled=True
        ).astype(jnp.float32),
        lax.psum_scatter(
            full_out.astype(jnp.bfloat16), "ffn", scatter_dimension=1, tiled=True
        ).astype(jnp.float32),
    )
    grad_sent = jnp.einsum(
        "secf,edf->secd", grad_inner, weight_in_all, preferred_element_type=jnp.float32
    )
    grad_back = lax.all_to_all(
        grad_sent.astype(jnp.bfloat16), "expert", split_axis=0, concat_axis=0, tiled=True
    )
    grad_padded = jnp.concatenate(
        [grad_back.reshape(experts * pad, width), jnp.zeros((1, width), jnp.bfloat16)], axis=0
    )
    grad_from_experts = grad_padded[slot].astype(jnp.float32)
    grad_probs = chosen_mask * grad_gate[:, None]
    grad_logits = router_probs * (
        grad_probs - jnp.sum(router_probs * grad_probs, axis=-1, keepdims=True)
    )
    grad_logits = grad_logits.astype(jnp.bfloat16)
    grad_router_part = jnp.einsum(
        "td,te->de", normed_ffn, grad_logits, preferred_element_type=jnp.float32
    )
    grad_normed_ffn = grad_from_experts + jnp.einsum(
        "te,de->td", grad_logits, router_weight, preferred_element_type=jnp.float32
    )
    grad_hidden_branch, grad_gain_ffn_part = rms_backward(
        hidden_state, scale_ffn, gain_ffn, grad_normed_ffn
    )
    grad_hidden = upstream + grad_hidden_branch
    grad_branch = grad_hidden.astype(jnp.bfloat16)
    grad_out_part = jnp.einsum("td,te->de", mixed, grad_branch, preferred_element_type=jnp.float32)
    grad_mixed = jnp.einsum(
        "te,de->td", grad_branch, out_weight, preferred_element_type=jnp.float32
    )
    grad_mixed = grad_mixed.astype(jnp.bfloat16).reshape(seq_count, SEQ, HEADS, HEAD_DIM)
    probs_full = jnp.swapaxes(probs_t, 1, 2)[None].astype(jnp.float32)
    probs_low = jnp.swapaxes(probs_t, 1, 2)[None]
    grad_value_rows = jnp.einsum(
        "bhqk,bqhd->bkhd", probs_low, grad_mixed, preferred_element_type=jnp.float32
    ).astype(jnp.bfloat16)
    grad_probs_attn = jnp.einsum(
        "bqhd,bkhd->bhqk", grad_mixed, value_rows, preferred_element_type=jnp.float32
    )
    grad_scores = probs_full * (
        grad_probs_attn - jnp.sum(grad_probs_attn * probs_full, axis=-1, keepdims=True)
    )
    grad_scores = grad_scores.astype(jnp.bfloat16)
    grad_queries = jnp.einsum(
        "bhqk,bkhd->bqhd", grad_scores, key_rows, preferred_element_type=jnp.float32
    ).astype(jnp.bfloat16)
    grad_key_rows = jnp.einsum(
        "bhqk,bqhd->bkhd", grad_scores, queries, preferred_element_type=jnp.float32
    ).astype(jnp.bfloat16)
    score_sums = jnp.sum(grad_scores.astype(jnp.float32), axis=0)
    grad_bias_part = jnp.einsum("hqk,qkn->nh", score_sums, onehot_table, precision=HIGH)
    flat_queries = grad_queries.reshape(tok_count, width)
    flat_keys = grad_key_rows.reshape(tok_count, width)
    flat_values = grad_value_rows.reshape(tok_count, width)
    grad_query_part = jnp.einsum(
        "td,te->de", normed_attn, flat_queries, preferred_element_type=jnp.float32
    )
    grad_key_part = jnp.einsum(
        "td,te->de", normed_attn, flat_keys, preferred_element_type=jnp.float32
    )
    grad_value_part = jnp.einsum(
        "td,te->de", normed_attn, flat_values, preferred_element_type=jnp.float32
    )
    grad_normed_attn = jnp.einsum(
        "te,de->td", flat_queries, query_weight, preferred_element_type=jnp.float32
    )
    grad_normed_attn = grad_normed_attn + jnp.einsum(
        "te,de->td", flat_keys, key_weight, preferred_element_type=jnp.float32
    )
    grad_normed_attn = grad_normed_attn + jnp.einsum(
        "te,de->td", flat_values, value_weight, preferred_element_type=jnp.float32
    )
    grad_input_branch, grad_gain_attn_part = rms_backward(
        inputs, scale_attn, gain_attn, grad_normed_attn
    )
    input_grad = grad_hidden + grad_input_branch
    summed = lax.psum(
        (
            grad_gain_attn_part,
            grad_query_part,
            grad_key_part,
            grad_value_part,
            grad_out_part,
            grad_bias_part,
            grad_gain_ffn_part,
            grad_router_part,
        ),
        ("expert", "ffn"),
    )
    rms_values = jnp.stack([root_attn, root_ffn])
    return (
        final.astype(jnp.bfloat16),
        input_grad,
        summed[0],
        summed[1],
        summed[2],
        summed[3],
        summed[4],
        summed[5],
        summed[6],
        summed[7],
        grad_expert_in,
        grad_expert_out,
        rms_values,
    )


def solution(mesh):
    placed = (
        P(("expert", "ffn"), None),
        P(),
        P(),
        P(),
        P(),
        P(),
        P(),
        P(),
        P(),
        P("expert", None, "ffn"),
        P("expert", "ffn", None),
        P(("expert", "ffn"), None),
        P(("expert", "ffn")),
        P(("expert", "ffn"), None),
    )
    return jax.shard_map(
        per_device,
        mesh=mesh,
        in_specs=placed,
        out_specs=(
            P(("expert", "ffn"), None),
            P(("expert", "ffn"), None),
            P(),
            P(),
            P(),
            P(),
            P(),
            P(),
            P(),
            P(),
            P("expert", None, "ffn"),
            P("expert", "ffn", None),
            P(None, ("expert", "ffn")),
        ),
        check_vma=False,
    )
```

```python
import functools
import jax
import jax.numpy as jnp
from jax import lax
from jax.experimental import pallas as pl
from jax.experimental.pallas import tpu as pltpu
from jax.sharding import PartitionSpec as P

HEADS = 12
HEAD_DIM = 64
BUCKETS = 32
SEQ = 512
EPSILON = 1e-06
THRESHOLDS = (12, 16, 23, 32, 46, 64, 91)
HIGH = lax.Precision.HIGHEST
F32 = jnp.float32
BF16 = jnp.bfloat16
MESH = pl.DeviceIdType.MESH
LANES = 128


def dot(a, b, ca=1, cb=0, precision=None):
    return lax.dot_general(
        a, b, (((ca,), (cb,)), ((), ())), precision=precision, preferred_element_type=F32
    )


def iota(shape, dim):
    return lax.broadcasted_iota(jnp.int32, shape, dim)


def each(n, body):
    if n <= 16:
        for k in range(1, n):
            body(k)
    else:

        def step(k, carry):
            body(k)
            return carry

        lax.fori_loop(1, n, step, 0)


def greet(n, me, core, sibling):
    barrier = pltpu.get_barrier_semaphore()

    def signal(k):
        pl.semaphore_signal(
            barrier, inc=1, device_id=(lax.rem(me + k, n), core), device_id_type=MESH
        )

    each(n, signal)
    if sibling:
        pl.semaphore_signal(barrier, inc=1, device_id=(me, 1 - core), device_id_type=MESH)
    return barrier


def band_onehot():
    place = iota((BUCKETS, 4 * LANES), 1)
    offset = jnp.where(place < 2 * LANES, -place, 4 * LANES - place)
    distance = jnp.abs(offset)
    larger = jnp.full(distance.shape, 8, jnp.int32)
    for limit in THRESHOLDS:
        larger = larger + (distance >= limit).astype(jnp.int32)
    bucket = jnp.where(distance < 8, distance, larger) + jnp.where(offset > 0, 16, 0)
    return (bucket == iota(bucket.shape, 0)).astype(F32)


def pieces(row):
    high = row.astype(BF16)
    rest = row - high.astype(F32)
    middle = rest.astype(BF16)
    low = (rest - middle.astype(F32)).astype(BF16)
    filler = jnp.zeros((5, row.shape[1]), BF16)
    return jnp.concatenate([high, middle, low, filler], axis=0)


def attend_kernel(
    n, slots, pad,
    tok_ref, ga_ref, wq_ref, wk_ref, wv_ref, wo_ref, rel_ref, gf_ref, wrt_ref, routes_ref, cap_ref, cot_ref, win_ref, wout_ref,
    cr_ref, wi2_ref, wo2_ref, xd_ref, gs_ref, st_ref, nat_ref, qt_ref, kt_ref, v_ref, p_ref, mixt_ref, hid_ref, nf_ref, pr_ref, gcol_ref, rms_ref,
    cd_ref, s_ref, k_ref, vt_ref, band_ref, send_sem, recv_sem, own_sem, w_send, w_recv,
):
    me = lax.axis_index("expert")
    core = lax.axis_index("ffn")
    count, width = tok_ref.shape
    rows_all = n * pad
    barrier = greet(n, me, core, True)

    routes = routes_ref[...]
    chosen = (iota((n, count), 0) == routes).astype(F32)
    upper = (iota((count, count), 0) < iota((count, count), 1)).astype(F32).astype(BF16)
    earlier = dot(chosen.astype(BF16), upper)
    position = jnp.sum(earlier * chosen, axis=0, keepdims=True)
    live = (cap_ref[0] * count // n).astype(F32)
    slot = jnp.where(position < live, routes * pad + position.astype(jnp.int32), rows_all)

    @pl.loop(0, rows_all // 256)
    def _(block):
        start = pl.multiple_of(block * 256, 256)
        hot = (iota((256, count), 0) + start == slot).astype(F32).astype(BF16)
        s_ref[pl.ds(start, 256), :] = hot
        cd_ref[pl.ds(start, 256), :] = dot(hot, cot_ref[...]).astype(BF16)

    pl.semaphore_wait(barrier, n)

    def rows_of(e):
        return pl.ds(pl.multiple_of(e * pad, pad), pad)

    def copy(k):
        target = lax.rem(me + k, n)
        return pltpu.make_async_remote_copy(
            src_ref=cd_ref.at[rows_of(target)],
            dst_ref=cr_ref.at[rows_of(me)],
            send_sem=send_sem.at[k],
            recv_sem=recv_sem.at[k],
            device_id=(target, core),
            device_id_type=MESH,
        )

    each(n, lambda k: copy(k).start())
    own = pltpu.make_async_copy(cd_ref.at[rows_of(me)], cr_ref.at[rows_of(me)], own_sem)
    own.start()
    halves = [
        pltpu.make_async_remote_copy(
            src_ref=src,
            dst_ref=dst,
            send_sem=w_send.at[i],
            recv_sem=w_recv.at[i],
            device_id=(me, 1 - core),
            device_id_type=MESH,
        )
        for i, (src, dst) in enumerate(((win_ref, wi2_ref), (wout_ref, wo2_ref)))
    ]
    for half in halves:
        half.start()

    x = tok_ref[...].astype(F32)
    ms1 = jnp.mean(x * x, axis=-1, keepdims=True)
    na = (x * lax.rsqrt(ms1 + EPSILON) * ga_ref[...]).astype(BF16)
    nat_ref[...] = na.T
    qt_ref[...] = dot(na, wq_ref[...]).astype(BF16).T
    keys = dot(na, wk_ref[...]).astype(BF16)
    k_ref[...] = keys
    kt_ref[...] = keys.T
    values = dot(na, wv_ref[...]).astype(BF16)
    v_ref[...] = values
    vt_ref[...] = values.T
    band_ref[...] = dot(rel_ref[...], band_onehot(), 0, 0, HIGH)
    lower_half = iota((LANES, count), 0) < HEAD_DIM
    blocks = count // LANES

    @pl.loop(0, HEADS // 2)
    def _(pair):
        lanes = pl.ds(pl.multiple_of(pair * LANES, LANES), LANES)
        both = qt_ref[lanes, :]
        for sub in range(2):
            head = 2 * pair + sub
            mask = lower_half if sub == 0 else jnp.logical_not(lower_half)
            query = jnp.where(mask, both, jnp.zeros_like(both))
            line = band_ref[pl.ds(head, 1), :]
            band = pltpu.roll(
                jnp.broadcast_to(line, (LANES, 4 * LANES)), 0, 1, stride=1, stride_axis=0
            )
            before = jnp.broadcast_to(line[:, 255:256], (LANES, LANES))
            after = jnp.broadcast_to(line[:, 257:258], (LANES, LANES))
            by_gap = {
                0: band[:, :LANES],
                -1: band[:, LANES : 2 * LANES],
                1: band[:, 3 * LANES :],
            }
            scores = []
            for row in range(blocks):
                bias = jnp.concatenate(
                    [
                        by_gap.get(row - col, after if row > col else before)
                        for col in range(blocks)
                    ],
                    axis=1,
                )
                made = dot(k_ref[row * LANES : (row + 1) * LANES, lanes], query)
                scores.append(made + bias)
            scores = jnp.concatenate(scores, axis=0)
            peak = jnp.max(scores, axis=0, keepdims=True)
            expo = jnp.exp(scores - peak)
            total = jnp.sum(expo, axis=0, keepdims=True)
            probs = (expo * (1.0 / total)).astype(BF16)
            p_ref[head] = probs
            features = pl.ds(pl.multiple_of(head * HEAD_DIM, HEAD_DIM), HEAD_DIM)
            mixt_ref[features, :] = dot(vt_ref[features, :], probs).astype(BF16)

    hidden = tok_ref[...].astype(F32) + dot(mixt_ref[...].T, wo_ref[...])
    hid_ref[...] = hidden
    ms2 = jnp.mean(hidden * hidden, axis=-1, keepdims=True)
    nf = (hidden * lax.rsqrt(ms2 + EPSILON) * gf_ref[...]).astype(BF16)
    nf_ref[...] = nf
    logits = dot(wrt_ref[...], nf, 1, 1)
    top = jnp.max(logits, axis=0, keepdims=True)
    raised = jnp.exp(logits - top)
    router = raised / jnp.sum(raised, axis=0, keepdims=True)
    pr_ref[...] = router
    gate = jnp.sum(router * chosen, axis=0, keepdims=True)
    gcol_ref[...] = jnp.broadcast_to(gate, (LANES, count)).T
    roots = jnp.concatenate(
        [
            jnp.broadcast_to(jnp.sqrt(ms + EPSILON), (count, LANES)).T[:4]
            for ms in (ms1, ms2)
        ],
        axis=0,
    )
    rms_ref[...] = roots
    parts = pieces(gate)

    @pl.loop(0, rows_all // 256)
    def _(block):
        start = pl.multiple_of(block * 256, 256)
        hot = s_ref[pl.ds(start, 256), :]
        xd_ref[pl.ds(start, 256), :] = dot(hot, nf_ref[...]).astype(BF16)
        split = dot(parts, hot, 1, 1)
        gs_ref[:, pl.ds(start, 256)] = jnp.broadcast_to(
            jnp.sum(split, axis=0, keepdims=True), split.shape
        )
        st_ref[:, pl.ds(start, 256)] = hot.T

    own.wait()
    for half in halves:
        half.wait()
    each(n, lambda k: copy(k).wait())


def attend(n, slots, pad, tokens, ga, wq, wk, wv, wo, rel, gf, wrt, routes, cap, cot, win, wout):
    count, width = tokens.shape
    rows = n * pad
    half = win.shape[-1]
    vmem = pl.BlockSpec(memory_space=pltpu.VMEM)
    anywhere = pl.BlockSpec(memory_space=pl.ANY)
    smem = pl.BlockSpec(memory_space=pltpu.SMEM)
    shapes = (
        ((rows, width), BF16, anywhere),
        ((width, half), BF16, anywhere),
        ((half, width), BF16, anywhere),
        ((rows, width), BF16, vmem),
        ((8, rows), F32, vmem),
        ((count, rows), BF16, vmem),
        ((width, count), BF16, vmem),
        ((width, count), BF16, vmem),
        ((width, count), BF16, vmem),
        ((count, width), BF16, vmem),
        ((HEADS, count, count), BF16, vmem),
        ((width, count), BF16, vmem),
        ((count, width), F32, vmem),
        ((count, width), BF16, vmem),
        ((n, count), F32, vmem),
        ((count, LANES), F32, vmem),
        ((8, count), F32, vmem),
    )
    return pl.pallas_call(
        functools.partial(attend_kernel, n, slots, pad),
        out_shape=[jax.ShapeDtypeStruct(shape, dtype) for shape, dtype, _ in shapes],
        in_specs=[vmem] * 10 + [smem, vmem, anywhere, anywhere],
        out_specs=[space for _, _, space in shapes],
        scratch_shapes=[
            pltpu.VMEM((rows, width), BF16),
            pltpu.VMEM((rows, count), BF16),
            pltpu.VMEM((count, width), BF16),
            pltpu.VMEM((width, count), BF16),
            pltpu.VMEM((HEADS, 4 * LANES), F32),
            pltpu.SemaphoreType.DMA((n,)),
            pltpu.SemaphoreType.DMA((n,)),
            pltpu.SemaphoreType.DMA,
            pltpu.SemaphoreType.DMA((2,)),
            pltpu.SemaphoreType.DMA((2,)),
        ],
        compiler_params=pltpu.CompilerParams(
            collective_id=0, has_side_effects=True, vmem_limit_bytes=60 * 1024 * 1024
        ),
        name="attend",
    )(tokens, ga, wq, wk, wv, wo, rel, gf, wrt, routes, cap, cot, win, wout)
RSQRT2 = 2.0 ** (-0.5)
RSQRT2PI = 0.3989422804014327
ROWS = 256
HIDDEN = 512


def lane_mask(pad, offset):
    return iota((pad, LANES), 1) == iota((pad, LANES), 0) + offset


def expert_kernel(
    n, pad,
    xd_ref, cr_ref, gs_ref, win_ref, wout_ref, win2_ref, wout2_ref,
    gx_ref, gg_ref, p_ref, own_in, own_out, got_in, got_out,
    xr_ref, gr_ref, gc_ref, wi_ref, wo_ref, act_ref, gi_ref, gxs_ref, ggs_ref, sum_gx, sum_p, sum_gg, gate_ref,
    x_send, x_recv, g_send, g_recv, gx_send, gx_recv, gg_send, gg_recv, w_sem, own_sem, dw_send, dw_recv, dw_sem,
):
    me = lax.axis_index("expert")
    core = lax.axis_index("ffn")
    half = win_ref.shape[1]
    parts = half // HIDDEN
    rows_all = n * pad
    barrier = greet(n, me, core, True)
    loads = []
    for j, (first, second) in enumerate(((win_ref, wout_ref), (win2_ref, wout2_ref))):
        for i in range(parts):
            at = j * parts + i
            cut = pl.ds(i * HIDDEN, HIDDEN)
            loads.append(pltpu.make_async_copy(first.at[:, cut], wi_ref.at[at], w_sem.at[2 * at]))
            loads.append(
                pltpu.make_async_copy(second.at[cut, :], wo_ref.at[at], w_sem.at[2 * at + 1])
            )
    for load in loads:
        load.start()

    def rows_of(e):
        return pl.ds(pl.multiple_of(e * pad, pad), pad)

    def tile_of(e):
        return pl.ds(pl.multiple_of(e * pad // LANES * LANES, LANES), LANES)

    def send(k, src, dst, sends, recvs):
        return pltpu.make_async_remote_copy(
            src_ref=src,
            dst_ref=dst,
            send_sem=sends.at[k],
            recv_sem=recvs.at[k],
            device_id=(lax.rem(me + k, n), core),
            device_id_type=MESH,
        )

    def token_copy(k):
        target = lax.rem(me + k, n)
        return send(k, xd_ref.at[rows_of(target)], xr_ref.at[rows_of(me)], x_send, x_recv)

    def gate_copy(k):
        target = lax.rem(me + k, n)
        return send(k, gs_ref.at[:, tile_of(target)], gr_ref.at[me], g_send, g_recv)

    def grad_copy(k):
        target = lax.rem(me + k, n)
        return send(k, gxs_ref.at[rows_of(target)], gx_ref.at[rows_of(me)], gx_send, gx_recv)

    def mark_copy(k):
        target = lax.rem(me + k, n)
        return send(k, ggs_ref.at[target], gg_ref.at[me], gg_send, gg_recv)

    pl.semaphore_wait(barrier, n)

    def start_tokens(k):
        gate_copy(k).start()
        token_copy(k).start()

    each(n, start_tokens)
    xr_ref[rows_of(me), :] = xd_ref[rows_of(me), :]
    gr_ref[me] = gs_ref[:, tile_of(me)]
    offset = lax.rem(me * pad, LANES)
    mask = lane_mask(pad, offset)
    for load in loads:
        load.wait()
    per = ROWS // pad
    row_blocks = rows_all // ROWS

    @pl.loop(0, row_blocks)
    def _(step):
        block = lax.rem(me // per + step, row_blocks)
        rows = pl.ds(pl.multiple_of(block * ROWS, ROWS), ROWS)
        columns = []
        for u in range(per):
            source = block * per + u
            k = lax.rem(me - source + n, n)

            @pl.when(k != 0)
            def _():
                gate_copy(k).wait_recv()
                token_copy(k).wait_recv()

            line = jnp.broadcast_to(gr_ref[source][:1], (pad, LANES))
            columns.append(jnp.sum(jnp.where(mask, line, 0.0), axis=1, keepdims=True))
        gates = jnp.concatenate(columns, axis=0)
        gate_ref[...] = jnp.broadcast_to(gates, gate_ref.shape)
        gc_ref[rows, :] = (gates * cr_ref[rows, :].astype(F32)).astype(BF16)
        sum_gx[...] = jnp.zeros_like(sum_gx)
        sum_p[...] = jnp.zeros_like(sum_p)
        sum_gg[...] = jnp.zeros_like(sum_gg)

        @pl.loop(0, 2 * parts)
        def _(i):
            inner = dot(xr_ref[rows, :], wi_ref[i])
            raw = dot(cr_ref[rows, :], wo_ref[i], 1, 1)
            normal = 0.5 * (1.0 + lax.erf(inner * RSQRT2))
            density = jnp.exp(-0.5 * inner * inner) * RSQRT2PI
            active = (inner * normal).astype(BF16)
            act_ref[i, rows, :] = active
            weighed = active.astype(F32) * raw
            folded = weighed[:, :LANES]
            for c in range(1, HIDDEN // LANES):
                folded = folded + weighed[:, c * LANES : (c + 1) * LANES]
            sum_gg[...] += folded
            grad = (gate_ref[:, :1] * raw * (normal + inner * density)).astype(BF16)
            gi_ref[i, rows, :] = grad
            sum_gx[...] += dot(grad, wi_ref[i], 1, 1)
            sum_p[...] += dot(active, wo_ref[i])

        gxs_ref[rows, :] = sum_gx[...].astype(BF16)
        p_ref[rows, :] = sum_p[...].astype(BF16)
        marks = jnp.sum(sum_gg[...], axis=1, keepdims=True)
        for u in range(per):
            source = block * per + u
            k = lax.rem(source - me + n, n)
            line = jnp.sum(
                jnp.where(mask, marks[u * pad : (u + 1) * pad], 0.0), axis=0, keepdims=True
            )
            ggs_ref[source] = jnp.broadcast_to(line, (8, LANES))

            @pl.when(k != 0)
            def _():
                mark_copy(k).start()
                grad_copy(k).start()

    own = pltpu.make_async_copy(gxs_ref.at[rows_of(me)], gx_ref.at[rows_of(me)], own_sem)
    own.start()
    gg_ref[me] = ggs_ref[me]

    def wait_sent(k):
        token_copy(k).wait_send()
        gate_copy(k).wait_send()

    each(n, wait_sent)

    moves = []
    for j in (1, 0):
        for i in range(parts):
            at = j * parts + i
            cut = pl.ds(i * HIDDEN, HIDDEN)
            wi_ref[at] = dot(xr_ref[...], gi_ref[at], 0, 0).astype(BF16)
            wo_ref[at] = dot(act_ref[at], gc_ref[...], 0, 0).astype(BF16)
            for q, (src, dst) in enumerate(
                (
                    (wi_ref.at[at], (got_in if j else own_in).at[:, cut]),
                    (wo_ref.at[at], (got_out if j else own_out).at[cut, :]),
                )
            ):
                if j:
                    moves.append(
                        pltpu.make_async_remote_copy(
                            src_ref=src,
                            dst_ref=dst,
                            send_sem=dw_send.at[2 * i + q],
                            recv_sem=dw_recv.at[2 * i + q],
                            device_id=(me, 1 - core),
                            device_id_type=MESH,
                        )
                    )
                else:
                    moves.append(pltpu.make_async_copy(src, dst, dw_sem.at[2 * i + q]))
                moves[-1].start()
    for move in moves:
        move.wait()
    own.wait()

    def finish(k):
        mark_copy(k).wait()
        grad_copy(k).wait()

    each(n, finish)


def run_experts(n, pad, xd, cr, gs, win, wout, win2, wout2):
    rows, width = xd.shape
    half = win.shape[1]
    parts = half // HIDDEN
    vmem = pl.BlockSpec(memory_space=pltpu.VMEM)
    anywhere = pl.BlockSpec(memory_space=pl.ANY)
    shapes = (
        ((rows, width), BF16, anywhere),
        ((n, 8, LANES), F32, vmem),
        ((rows, width), BF16, vmem),
        ((width, half), BF16, anywhere),
        ((half, width), BF16, anywhere),
        ((width, half), BF16, anywhere),
        ((half, width), BF16, anywhere),
    )
    return pl.pallas_call(
        functools.partial(expert_kernel, n, pad),
        out_shape=[jax.ShapeDtypeStruct(shape, dtype) for shape, dtype, _ in shapes],
        in_specs=[vmem] * 3 + [anywhere] * 4,
        out_specs=[space for _, _, space in shapes],
        scratch_shapes=[
            pltpu.VMEM((rows, width), BF16),
            pltpu.VMEM((n, 8, LANES), F32),
            pltpu.VMEM((rows, width), BF16),
            pltpu.VMEM((2 * parts, width, HIDDEN), BF16),
            pltpu.VMEM((2 * parts, HIDDEN, width), BF16),
            pltpu.VMEM((2 * parts, rows, HIDDEN), BF16),
            pltpu.VMEM((2 * parts, rows, HIDDEN), BF16),
            pltpu.VMEM((rows, width), BF16),
            pltpu.VMEM((n, 8, LANES), F32),
            pltpu.VMEM((ROWS, width), F32),
            pltpu.VMEM((ROWS, width), F32),
            pltpu.VMEM((ROWS, LANES), F32),
            pltpu.VMEM((ROWS, LANES), F32),
        ]
        + [pltpu.SemaphoreType.DMA((n,))] * 8
        + [
            pltpu.SemaphoreType.DMA((4 * parts,)),
            pltpu.SemaphoreType.DMA,
            pltpu.SemaphoreType.DMA((2 * parts,)),
            pltpu.SemaphoreType.DMA((2 * parts,)),
            pltpu.SemaphoreType.DMA((2 * parts,)),
        ],
        compiler_params=pltpu.CompilerParams(
            collective_id=1, has_side_effects=True, vmem_limit_bytes=60 * 1024 * 1024
        ),
        name="experts",
    )(xd, cr, gs, win, wout, win2, wout2)
def unit_rows(n, rows):
    return -(-rows // (n * 16)) * 16


def reduce_rows(n, width):
    first = 3 * width
    return [n * unit_rows(n, first)] * 3 + [n * unit_rows(n, first + 3 * n + 32)]


def reduce_shapes(n, width):
    stages = n.bit_length() - 1
    scratch = []
    for rows in reduce_rows(n, width):
        scratch.append(pltpu.VMEM((rows, LANES), BF16))
        scratch.append(pltpu.VMEM((rows, LANES), BF16))
        scratch += [pltpu.VMEM((rows >> (s + 1), LANES), BF16) for s in range(stages)]
    return scratch + [pltpu.SemaphoreType.DMA((4, 2 * stages + 2))] * 2


def greet_reducers(n, me, core, barrier):
    for s in range(n.bit_length() - 1):
        pl.semaphore_signal(
            barrier, inc=1, device_id=(reduce_peer(me, core, s)[0], core), device_id_type=MESH
        )
    pl.semaphore_signal(barrier, inc=1, device_id=(me, 1 - core), device_id_type=MESH)
    return n.bit_length()


def reduce_peer(me, core, s):
    distance = (1 + core, 2 - core)[s] if s < 2 else 2**s
    side = lax.rem(me // distance, 2)
    return me + distance * (1 - 2 * side), side


def reduce_steps(n, me, core, j, part, work, arrived, halves, total, sends, recvs):
    stages = n.bit_length() - 1
    unit = work.shape[0] // n
    sides, peers, starts = [], [], [0]
    for s in range(stages):
        peer, side = reduce_peer(me, core, s)
        peers.append(peer)
        sides.append(side)
        starts.append(starts[-1] + side * (n >> (s + 1)))

    def region(start, units):
        return pl.ds(pl.multiple_of(start * unit, unit), units * unit)

    def copy(step, src, dst, device):
        return pltpu.make_async_remote_copy(
            src_ref=src,
            dst_ref=dst,
            send_sem=sends.at[j, step],
            recv_sem=recvs.at[j, step],
            device_id=device,
            device_id_type=MESH,
        )

    def transfer(step):
        if step == 0:
            return copy(step, part.at[1 - core], arrived, (me, 1 - core))
        if step <= stages:
            s = step - 1
            size = n >> (s + 1)
            away = starts[s] + (1 - sides[s]) * size
            return copy(step, work.at[region(away, size)], halves[s], (peers[s], core))
        if step <= 2 * stages:
            s = 2 * stages - step
            held = total.at[core, region(starts[s + 1], n >> (s + 1))]
            return copy(step, held, held, (peers[s], core))
        return copy(step, total.at[core], total.at[core], (me, 1 - core))

    def add(step):
        if step == 0:
            work[...] = (part[core].astype(F32) + arrived[...].astype(F32)).astype(BF16)
        elif step <= stages:
            s = step - 1
            mine = region(starts[s + 1], n >> (s + 1))
            summed = (work[mine, :].astype(F32) + halves[s][...].astype(F32)).astype(BF16)
            if step == stages:
                total[core, mine, :] = summed
            else:
                work[mine, :] = summed

    last = 2 * stages + 1

    def run(step):
        if step > 0:
            transfer(step - 1).wait_recv()
            add(step - 1)
        if step <= last:
            transfer(step).start()
        else:
            for done in range(last + 1):
                transfer(done).wait_send()

    return [functools.partial(run, step) for step in range(last + 2)]


def reducers(n, me, core, parts, totals, scratch):
    stages = n.bit_length() - 1
    size = stages + 2
    sends, recvs = scratch[-2:]
    return [
        reduce_steps(
            n, me, core, j, parts[j], scratch[j * size], scratch[j * size + 1],
            scratch[j * size + 2 : (j + 1) * size], totals[j], sends, recvs,
        )
        for j in range(4)
    ]


def reduce_kernel(n, *refs):
    me = lax.axis_index("expert")
    core = lax.axis_index("ffn")
    barrier = pltpu.get_barrier_semaphore()
    pl.semaphore_wait(barrier, greet_reducers(n, me, core, barrier))
    chunks = reducers(n, me, core, refs[:4], refs[4:8], refs[8:])
    for time in range(len(chunks[0]) + 3):
        for j, steps in enumerate(chunks):
            if 0 <= time - j < len(steps):
                steps[time - j]()


def run_reduce(n, parts):
    vmem = pl.BlockSpec(memory_space=pltpu.VMEM)
    return pl.pallas_call(
        functools.partial(reduce_kernel, n),
        out_shape=[jax.ShapeDtypeStruct(part.shape, BF16) for part in parts],
        in_specs=[vmem] * 4,
        out_specs=[vmem] * 4,
        scratch_shapes=reduce_shapes(n, 768),
        compiler_params=pltpu.CompilerParams(
            collective_id=3, has_side_effects=True, vmem_limit_bytes=60 * 1024 * 1024
        ),
        name="sum_grads",
    )(*parts)


def unroll_band(band):
    wide = band.shape[1]
    folded = band[:8]
    for g in range(1, band.shape[0] // 8):
        folded = folded + pltpu.roll(band[8 * g : 8 * g + 8], wide - 8 * g, 1)
    line = folded[:1]
    for s in range(1, 8):
        line = line + pltpu.roll(folded, wide - s, 1)[s : s + 1]
    return line


def back_kernel(
    n, pad,
    tok_ref, ga_ref, wq_ref, wk_ref, wv_ref, wo_ref, gf_ref, wrt_ref, routes_ref, cot_ref, st_ref, gx_ref, gg_ref, p_ref,
    nat_ref, qt_ref, kt_ref, v_ref, probs_hbm, mixt_ref, hid_ref, nf_ref, pr_ref, gcol_ref,
    out_ref, dx_ref, part0, part1, part2, part3,
    got_ref, probs_ref, gmt_ref, gqt_ref, gkt_ref, gvt_ref, gh_ref, lines_ref,
    send_sem, recv_sem, probs_sem,
):
    me = lax.axis_index("expert")
    core = lax.axis_index("ffn")
    count, width = tok_ref.shape
    rows_all = n * pad
    barrier = greet(n, me, core, False)
    load = pltpu.make_async_copy(probs_hbm, probs_ref, probs_sem)
    load.start()

    def rows_of(e):
        return pl.ds(pl.multiple_of(e * pad, pad), pad)

    def copy(k):
        target = lax.rem(me + k, n)
        return pltpu.make_async_remote_copy(
            src_ref=p_ref.at[rows_of(target)],
            dst_ref=got_ref.at[rows_of(me)],
            send_sem=send_sem.at[k],
            recv_sem=recv_sem.at[k],
            device_id=(target, core),
            device_id_type=MESH,
        )

    pl.semaphore_wait(barrier, n - 1)
    each(n, lambda k: copy(k).start())
    got_ref[rows_of(me), :] = p_ref[rows_of(me), :]

    share = LANES // pad
    tiles = []
    for t in range(n // share):
        tile = gg_ref[t * share][:1]
        for u in range(1, share):
            tile = tile + gg_ref[t * share + u][:1]
        tiles.append(tile)
    marks = jnp.concatenate(tiles, axis=1)
    grad_gate = jnp.sum(dot(pieces(marks), st_ref[...], 1, 1), axis=0, keepdims=True)
    chosen = (iota((n, count), 0) == routes_ref[...]).astype(F32)
    router = pr_ref[...]
    grad_probs = chosen * grad_gate
    grad_logits = router * (grad_probs - jnp.sum(router * grad_probs, axis=0, keepdims=True))
    grad_logits = grad_logits.astype(BF16)
    grad_router = dot(nf_ref[...], grad_logits, 0, 1).T
    grad_nf = dot(st_ref[...], gx_ref[...]) + dot(grad_logits, wrt_ref[...], 0, 0)
    hidden = hid_ref[...]
    scale = lax.rsqrt(jnp.mean(hidden * hidden, axis=-1, keepdims=True) + EPSILON)
    weighted = grad_nf * gf_ref[...]
    grad_gain_ffn = jnp.sum(grad_nf * hidden * scale, axis=0, keepdims=True)
    inner = jnp.mean(weighted * hidden, axis=-1, keepdims=True)
    grad_hidden = (
        cot_ref[...].astype(F32) + scale * weighted - hidden * (scale * scale * scale * inner)
    )
    gh_ref[...] = grad_hidden
    branch = grad_hidden.astype(BF16)
    for t in range(width // LANES):
        cut = slice(t * LANES, (t + 1) * LANES)
        rows = slice(t % 3 * width, (t % 3 + 1) * width)
        part0[t // 3, rows, :] = dot(mixt_ref[...], branch[:, cut]).astype(BF16)
    gmt_ref[...] = dot(wo_ref[...], branch, 1, 1).astype(BF16)
    load.wait()
    lines_ref[...] = jnp.zeros_like(lines_ref)
    lower_half = iota((LANES, count), 0) < HEAD_DIM
    blocks = count // LANES
    place = iota((1, 4 * LANES), 1)

    @pl.loop(0, HEADS // 2)
    def _(pair):
        lanes = pl.ds(pl.multiple_of(pair * LANES, LANES), LANES)
        both = gmt_ref[lanes, :]
        for sub in range(2):
            head = 2 * pair + sub
            mask = lower_half if sub == 0 else jnp.logical_not(lower_half)
            chunk = jnp.where(mask, both, jnp.zeros_like(both))
            features = pl.ds(pl.multiple_of(head * HEAD_DIM, HEAD_DIM), HEAD_DIM)
            grad_mixed = gmt_ref[features, :]
            delta = jnp.sum(
                grad_mixed.astype(F32) * mixt_ref[features, :].astype(F32), axis=0, keepdims=True
            )
            probs = probs_ref[head]
            grad_probs = dot(v_ref[:, lanes], chunk)
            scores = probs.astype(F32) * (grad_probs - delta)
            low = scores.astype(BF16)
            gqt_ref[features, :] = dot(kt_ref[features, :], low).astype(BF16)
            gkt_ref[features, :] = dot(qt_ref[features, :], low, 1, 1).astype(BF16)
            gvt_ref[features, :] = dot(grad_mixed, probs, 1, 1).astype(BF16)
            near = {0: None, -1: None, 1: None}
            far = {-1: None, 1: None}
            for row in range(blocks):
                for col in range(blocks):
                    block = scores[
                        row * LANES : (row + 1) * LANES, col * LANES : (col + 1) * LANES
                    ]
                    gap = row - col
                    if gap in near:
                        near[gap] = block if near[gap] is None else near[gap] + block
                    else:
                        side = 1 if gap > 0 else -1
                        far[side] = block if far[side] is None else far[side] + block
            band = jnp.concatenate([near[0], near[-1], jnp.zeros_like(near[0]), near[1]], axis=1)
            line = unroll_band(band)
            for side, lane in ((-1, 255), (1, 257)):
                total = jnp.sum(jnp.sum(far[side], axis=0, keepdims=True), axis=1, keepdims=True)
                line = line + jnp.where(place == lane, total, 0.0)
            lines_ref[pl.ds(head, 1), :] = line

    for group, part in enumerate((part1, part2, part3)):
        for i, grad in enumerate((gqt_ref, gkt_ref, gvt_ref)):
            columns = grad[group * 2 * LANES : (group + 1) * 2 * LANES, :]
            made = dot(nat_ref[...], columns, 1, 1).astype(BF16)
            for c in range(2):
                part[c, i * width : (i + 1) * width, :] = made[:, c * LANES : (c + 1) * LANES]
    grad_na = (
        dot(wq_ref[...], gqt_ref[...])
        + dot(wk_ref[...], gkt_ref[...])
        + dot(wv_ref[...], gvt_ref[...])
    ).T
    x = tok_ref[...].astype(F32)
    scale = lax.rsqrt(jnp.mean(x * x, axis=-1, keepdims=True) + EPSILON)
    weighted = grad_na * ga_ref[...]
    grad_gain_attn = jnp.sum(grad_na * x * scale, axis=0, keepdims=True)
    inner = jnp.mean(weighted * x, axis=-1, keepdims=True)
    dx_ref[...] = gh_ref[...] + scale * weighted - x * (scale * scale * scale * inner)
    grad_bias = dot(band_onehot(), lines_ref[...], 1, 1, HIGH)
    gains = jnp.concatenate([grad_gain_attn, grad_gain_ffn, jnp.zeros((14, width), F32)], axis=0)
    base = 3 * width
    for c in range(2):
        for t in range(3):
            cut = slice((3 * c + t) * LANES, (3 * c + t + 1) * LANES)
            part3[c, base + t * n : base + (t + 1) * n, :] = grad_router[:, cut].astype(BF16)
        rows = slice(base + 3 * n, base + 3 * n + 16)
        sums = [gains[:, (3 * c + t) * LANES : (3 * c + t + 1) * LANES][:2] for t in range(3)]
        part3[c, rows, :] = jnp.concatenate(sums + [jnp.zeros((10, LANES), F32)], axis=0).astype(BF16)
        rows = slice(base + 3 * n + 16, base + 3 * n + 32)
        wide = jnp.concatenate(
            [grad_bias[16 * c : 16 * c + 16], jnp.zeros((16, LANES - 16), F32)], axis=1
        )
        part3[c, rows, :] = wide.astype(BF16)
    for part, used in ((part0, base), (part1, base), (part2, base), (part3, base + 3 * n + 32)):
        if part.shape[1] > used:
            part[:, used:, :] = jnp.zeros((2, part.shape[1] - used, LANES), BF16)

    each(n, lambda k: copy(k).wait())
    picked = dot(st_ref[...], got_ref[...])
    out_ref[...] = (hid_ref[...] + gcol_ref[:, :1] * picked).astype(BF16)


def run_back(n, pad, tokens, *rest):
    count, width = tokens.shape
    rows = n * pad
    vmem = pl.BlockSpec(memory_space=pltpu.VMEM)
    anywhere = pl.BlockSpec(memory_space=pl.ANY)
    shapes = (
        ((count, width), BF16, vmem),
        ((count, width), F32, vmem),
        *(((2, part, LANES), BF16, vmem) for part in reduce_rows(n, width)),
    )
    return pl.pallas_call(
        functools.partial(back_kernel, n, pad),
        out_shape=[jax.ShapeDtypeStruct(shape, dtype) for shape, dtype, _ in shapes],
        in_specs=[vmem] * 18 + [anywhere] + [vmem] * 5,
        out_specs=[space for _, _, space in shapes],
        scratch_shapes=[
            pltpu.VMEM((rows, width), BF16),
            pltpu.VMEM((HEADS, count, count), BF16),
            pltpu.VMEM((width, count), BF16),
            pltpu.VMEM((width, count), BF16),
            pltpu.VMEM((width, count), BF16),
            pltpu.VMEM((width, count), BF16),
            pltpu.VMEM((count, width), F32),
            pltpu.VMEM((16, 4 * LANES), F32),
            pltpu.SemaphoreType.DMA((n,)),
            pltpu.SemaphoreType.DMA((n,)),
            pltpu.SemaphoreType.DMA,
        ],
        compiler_params=pltpu.CompilerParams(
            collective_id=2, has_side_effects=True, vmem_limit_bytes=60 * 1024 * 1024
        ),
        name="attend_back",
    )(tokens, *rest)


def per_device(
    tokens, gain_attn, query_weight, key_weight, value_weight, out_weight, rel_bias, gain_ffn, router_weight,
    expert_in, expert_out, routes, capacity, cotangent,
):
    count, width = tokens.shape
    n = lax.axis_size("expert")
    experts = router_weight.shape[1]
    assert experts == n and count == SEQ
    slots = 2 * count // experts
    pad = -(-slots // 16) * 16
    gain_attn, gain_ffn = gain_attn[None], gain_ffn[None]
    router_rows = router_weight.T
    routes = routes.reshape(1, count)
    (
        cots, in_other, out_other, dispatched, gates, slots_t, normed_t, query_t, key_t, values, probs, mixed_t,
        hidden, normed_ffn, router_t, gate_col, roots,
    ) = attend(
        n, slots, pad, tokens, gain_attn, query_weight, key_weight, value_weight, out_weight, rel_bias, gain_ffn,
        router_rows, routes, capacity, cotangent, expert_in[0], expert_out[0],
    )
    grad_rows, marks, produced, own_in, own_out, got_in, got_out = run_experts(
        n, pad, dispatched, cots, gates, expert_in[0], expert_out[0], in_other, out_other
    )
    output, input_grad, *grad_parts = run_back(
        n, pad, tokens, gain_attn, query_weight, key_weight, value_weight, out_weight, gain_ffn, router_rows, routes,
        cotangent, slots_t, grad_rows, marks, produced, normed_t, query_t, key_t, values, probs, mixed_t, hidden,
        normed_ffn, router_t, gate_col,
    )
    first, *groups = run_reduce(n, grad_parts)
    grad_out = jnp.concatenate(
        [first[t // 3, t % 3 * width : (t % 3 + 1) * width] for t in range(6)], axis=1
    ).astype(F32)
    grads = [
        jnp.concatenate(
            [group[c, i * width : (i + 1) * width] for group in groups for c in range(2)], axis=1
        ).astype(F32)
        for i in range(3)
    ]
    base = 3 * width
    small = groups[2][:, base : base + 3 * n + 32].astype(F32)
    grad_router = small[:, : 3 * n].reshape(6, n, LANES)
    grad_router = jnp.swapaxes(grad_router, 0, 1).reshape(n, width).T
    gains = small[:, 3 * n : 3 * n + 6].reshape(6, 2, LANES)
    grad_bias = small[:, 3 * n + 16 :, :HEADS].reshape(BUCKETS, HEADS)
    grad_expert_in = own_in.astype(F32) + got_in.astype(F32)
    grad_expert_out = own_out.astype(F32) + got_out.astype(F32)
    rms_values = jnp.stack([roots[0], roots[4]])
    return (
        output,
        input_grad,
        gains[:, 0].reshape(width),
        grads[0],
        grads[1],
        grads[2],
        grad_out,
        grad_bias,
        gains[:, 1].reshape(width),
        grad_router,
        grad_expert_in[None],
        grad_expert_out[None],
        rms_values,
    )


def solution(mesh):
    placed = (
        P(("expert", "ffn"), None),
        P(),
        P(),
        P(),
        P(),
        P(),
        P(),
        P(),
        P(),
        P("expert", None, "ffn"),
        P("expert", "ffn", None),
        P(("expert", "ffn"), None),
        P(("expert", "ffn")),
        P(("expert", "ffn"), None),
    )
    return jax.shard_map(
        per_device,
        mesh=mesh,
        in_specs=placed,
        out_specs=(
            P(("expert", "ffn"), None),
            P(("expert", "ffn"), None),
            P(),
            P(),
            P(),
            P(),
            P(),
            P(),
            P(),
            P(),
            P("expert", None, "ffn"),
            P("expert", "ffn", None),
            P(None, ("expert", "ffn")),
        ),
        check_vma=False,
    )
```

```python
import functools
import jax
import jax.numpy as jnp
from jax import lax
from jax.experimental import pallas as pl
from jax.experimental.pallas import tpu as pltpu
from jax.sharding import PartitionSpec as P

HEADS = 12
HEAD_DIM = 64
BUCKETS = 32
SEQ = 512
EPSILON = 1e-06
THRESHOLDS = (12, 16, 23, 32, 46, 64, 91)
HIGH = lax.Precision.HIGHEST
F32 = jnp.float32
BF16 = jnp.bfloat16
MESH = pl.DeviceIdType.MESH
LANES = 128


def dot(a, b, ca=1, cb=0, precision=None):
    return lax.dot_general(
        a, b, (((ca,), (cb,)), ((), ())), precision=precision, preferred_element_type=F32
    )


def iota(shape, dim):
    return lax.broadcasted_iota(jnp.int32, shape, dim)


def div(a, b):
    return a // b if isinstance(a, int) else lax.div(a, jnp.int32(b))


def rem(a, b):
    return a % b if isinstance(a, int) else lax.rem(a, jnp.int32(b))


def block_at(n, me, step, per, blocks):
    if n != 16:
        return rem(div(me, per) + step, blocks)
    layer = div(me, 4)
    low = rem(rem(layer, 2) + div(step + 1, 2), 2)
    return 2 * rem(div(layer, 2) + 1 - div(step, 2), 2) + low


def partner(n, me, k):
    if n != 16:
        return rem(me + k, n)
    return 4 * block_at(n, me, div(k, 4), 4, 4) + rem(rem(me, 4) + rem(k, 4), 4)


def index_between(n, sender, receiver, step):
    if n != 16:
        return rem(receiver - sender + n, n)
    return 4 * step + rem(rem(receiver, 4) - rem(sender, 4) + 4, 4)


def each(n, body):
    if n == 16:
        for k in range(n):
            if k != 12:
                body(k)
    else:

        def step(k, carry):
            body(k)
            return carry

        lax.fori_loop(1, n, step, 0)


def greet(n, me, core, sibling):
    barrier = pltpu.get_barrier_semaphore()

    def signal(k):
        pl.semaphore_signal(
            barrier, inc=1, device_id=(partner(n, me, k), core), device_id_type=MESH
        )

    each(n, signal)
    if sibling:
        pl.semaphore_signal(barrier, inc=1, device_id=(me, 1 - core), device_id_type=MESH)
    return barrier


def band_onehot():
    place = iota((BUCKETS, 4 * LANES), 1)
    offset = jnp.where(place < 2 * LANES, -place, 4 * LANES - place)
    distance = jnp.abs(offset)
    larger = jnp.full(distance.shape, 8, jnp.int32)
    for limit in THRESHOLDS:
        larger = larger + (distance >= limit).astype(jnp.int32)
    bucket = jnp.where(distance < 8, distance, larger) + jnp.where(offset > 0, 16, 0)
    return (bucket == iota(bucket.shape, 0)).astype(F32)


def pieces(row):
    high = row.astype(BF16)
    rest = row - high.astype(F32)
    middle = rest.astype(BF16)
    low = (rest - middle.astype(F32)).astype(BF16)
    filler = jnp.zeros((5, row.shape[1]), BF16)
    return jnp.concatenate([high, middle, low, filler], axis=0)


def attend_kernel(
    n, slots, pad,
    tok_ref, ga_ref, wq_ref, wk_ref, wv_ref, wo_ref, rel_ref, gf_ref, wrt_ref, routes_ref, cap_ref, cot_ref, win_ref, wout_ref,
    cr_ref, wi2_ref, wo2_ref, xd_ref, gs_ref, st_ref, nat_ref, qt_ref, kt_ref, v_ref, p_ref, mixt_ref, hid_ref, nf_ref, pr_ref, gcol_ref, rms_ref,
    cd_ref, s_ref, k_ref, vt_ref, band_ref, send_sem, recv_sem, own_sem, w_send, w_recv,
):
    me = lax.axis_index("expert")
    core = lax.axis_index("ffn")
    count, width = tok_ref.shape
    rows_all = n * pad
    barrier = greet(n, me, core, True)

    routes = routes_ref[...]
    chosen = (iota((n, count), 0) == routes).astype(F32)
    upper = (iota((count, count), 0) < iota((count, count), 1)).astype(F32).astype(BF16)
    earlier = dot(chosen.astype(BF16), upper)
    position = jnp.sum(earlier * chosen, axis=0, keepdims=True)
    live = (cap_ref[0] * count // n).astype(F32)
    slot = jnp.where(position < live, routes * pad + position.astype(jnp.int32), rows_all)

    @pl.loop(0, rows_all // 256)
    def _(block):
        start = pl.multiple_of(block * 256, 256)
        hot = (iota((256, count), 0) + start == slot).astype(F32).astype(BF16)
        s_ref[pl.ds(start, 256), :] = hot
        cd_ref[pl.ds(start, 256), :] = dot(hot, cot_ref[...]).astype(BF16)

    pl.semaphore_wait(barrier, n)

    def rows_of(e):
        return pl.ds(pl.multiple_of(e * pad, pad), pad)

    def copy(k):
        target = partner(n, me, k)
        return pltpu.make_async_remote_copy(
            src_ref=cd_ref.at[rows_of(target)],
            dst_ref=cr_ref.at[rows_of(me)],
            send_sem=send_sem.at[k],
            recv_sem=recv_sem.at[k],
            device_id=(target, core),
            device_id_type=MESH,
        )

    each(n, lambda k: copy(k).start())
    own = pltpu.make_async_copy(cd_ref.at[rows_of(me)], cr_ref.at[rows_of(me)], own_sem)
    own.start()
    halves = [
        pltpu.make_async_remote_copy(
            src_ref=src,
            dst_ref=dst,
            send_sem=w_send.at[i],
            recv_sem=w_recv.at[i],
            device_id=(me, 1 - core),
            device_id_type=MESH,
        )
        for i, (src, dst) in enumerate(((win_ref, wi2_ref), (wout_ref, wo2_ref)))
    ]
    for half in halves:
        half.start()

    x = tok_ref[...].astype(F32)
    ms1 = jnp.mean(x * x, axis=-1, keepdims=True)
    na = (x * lax.rsqrt(ms1 + EPSILON) * ga_ref[...][None]).astype(BF16)
    nat_ref[...] = na.T
    qt_ref[...] = dot(na, wq_ref[...]).astype(BF16).T
    keys = dot(na, wk_ref[...]).astype(BF16)
    k_ref[...] = keys
    kt_ref[...] = keys.T
    values = dot(na, wv_ref[...]).astype(BF16)
    v_ref[...] = values
    vt_ref[...] = values.T
    band_ref[...] = dot(rel_ref[...], band_onehot(), 1, 0, HIGH)
    lower_half = iota((LANES, count), 0) < HEAD_DIM
    blocks = count // LANES

    @pl.loop(0, HEADS // 2)
    def _(pair):
        lanes = pl.ds(pl.multiple_of(pair * LANES, LANES), LANES)
        both = qt_ref[lanes, :]
        for sub in range(2):
            head = 2 * pair + sub
            mask = lower_half if sub == 0 else jnp.logical_not(lower_half)
            query = jnp.where(mask, both, jnp.zeros_like(both))
            line = band_ref[pl.ds(head, 1), :]
            band = pltpu.roll(
                jnp.broadcast_to(line, (LANES, 4 * LANES)), 0, 1, stride=1, stride_axis=0
            )
            before = jnp.broadcast_to(line[:, 255:256], (LANES, LANES))
            after = jnp.broadcast_to(line[:, 257:258], (LANES, LANES))
            by_gap = {
                0: band[:, :LANES],
                -1: band[:, LANES : 2 * LANES],
                1: band[:, 3 * LANES :],
            }
            scores = []
            for row in range(blocks):
                bias = jnp.concatenate(
                    [
                        by_gap.get(row - col, after if row > col else before)
                        for col in range(blocks)
                    ],
                    axis=1,
                )
                made = dot(k_ref[row * LANES : (row + 1) * LANES, lanes], query)
                scores.append(made + bias)
            scores = jnp.concatenate(scores, axis=0)
            peak = jnp.max(scores, axis=0, keepdims=True)
            expo = jnp.exp(scores - peak)
            total = jnp.sum(expo, axis=0, keepdims=True)
            probs = (expo * (1.0 / total)).astype(BF16)
            p_ref[head] = probs
            features = pl.ds(pl.multiple_of(head * HEAD_DIM, HEAD_DIM), HEAD_DIM)
            mixt_ref[features, :] = dot(vt_ref[features, :], probs).astype(BF16)

    hidden = tok_ref[...].astype(F32) + dot(mixt_ref[...].T, wo_ref[...])
    hid_ref[...] = hidden
    ms2 = jnp.mean(hidden * hidden, axis=-1, keepdims=True)
    nf = (hidden * lax.rsqrt(ms2 + EPSILON) * gf_ref[...][None]).astype(BF16)
    nf_ref[...] = nf
    logits = dot(wrt_ref[...], nf, 1, 1)
    top = jnp.max(logits, axis=0, keepdims=True)
    raised = jnp.exp(logits - top)
    router = raised / jnp.sum(raised, axis=0, keepdims=True)
    pr_ref[...] = router
    gate = jnp.sum(router * chosen, axis=0, keepdims=True)
    gcol_ref[...] = jnp.broadcast_to(gate, (LANES, count)).T
    roots = jnp.concatenate(
        [
            jnp.broadcast_to(jnp.sqrt(ms + EPSILON), (count, LANES)).T[:4]
            for ms in (ms1, ms2)
        ],
        axis=0,
    )
    rms_ref[...] = roots
    parts = pieces(gate)

    @pl.loop(0, rows_all // 256)
    def _(block):
        start = pl.multiple_of(block * 256, 256)
        hot = s_ref[pl.ds(start, 256), :]
        xd_ref[pl.ds(start, 256), :] = dot(hot, nf_ref[...]).astype(BF16)
        split = dot(parts, hot, 1, 1)
        gs_ref[:, pl.ds(start, 256)] = jnp.broadcast_to(
            jnp.sum(split, axis=0, keepdims=True), split.shape
        )
        st_ref[:, pl.ds(start, 256)] = hot.T

    own.wait()
    for half in halves:
        half.wait()
    each(n, lambda k: copy(k).wait())


def attend(n, slots, pad, tokens, ga, wq, wk, wv, wo, rel, gf, wrt, routes, cap, cot, win, wout):
    count, width = tokens.shape
    rows = n * pad
    half = win.shape[-1]
    vmem = pl.BlockSpec(memory_space=pltpu.VMEM)
    anywhere = pl.BlockSpec(memory_space=pl.ANY)
    smem = pl.BlockSpec(memory_space=pltpu.SMEM)
    shapes = (
        ((rows, width), BF16, anywhere),
        ((width, half), BF16, anywhere),
        ((half, width), BF16, anywhere),
        ((rows, width), BF16, vmem),
        ((8, rows), F32, vmem),
        ((count, rows), BF16, vmem),
        ((width, count), BF16, vmem),
        ((width, count), BF16, vmem),
        ((width, count), BF16, vmem),
        ((count, width), BF16, vmem),
        ((HEADS, count, count), BF16, vmem),
        ((width, count), BF16, vmem),
        ((count, width), F32, vmem),
        ((count, width), BF16, vmem),
        ((n, count), F32, vmem),
        ((count, LANES), F32, vmem),
        ((8, count), F32, vmem),
    )
    return pl.pallas_call(
        functools.partial(attend_kernel, n, slots, pad),
        out_shape=[jax.ShapeDtypeStruct(shape, dtype) for shape, dtype, _ in shapes],
        in_specs=[vmem] * 10 + [smem, vmem, anywhere, anywhere],
        out_specs=[space for _, _, space in shapes],
        scratch_shapes=[
            pltpu.VMEM((rows, width), BF16),
            pltpu.VMEM((rows, count), BF16),
            pltpu.VMEM((count, width), BF16),
            pltpu.VMEM((width, count), BF16),
            pltpu.VMEM((HEADS, 4 * LANES), F32),
            pltpu.SemaphoreType.DMA((n,)),
            pltpu.SemaphoreType.DMA((n,)),
            pltpu.SemaphoreType.DMA,
            pltpu.SemaphoreType.DMA((2,)),
            pltpu.SemaphoreType.DMA((2,)),
        ],
        compiler_params=pltpu.CompilerParams(
            collective_id=0, has_side_effects=True, vmem_limit_bytes=60 * 1024 * 1024
        ),
        name="attend",
    )(tokens, ga, wq, wk, wv, wo, rel, gf, wrt, routes, cap, cot, win, wout)
RSQRT2 = 2.0 ** (-0.5)
RSQRT2PI = 0.3989422804014327
ROWS = 256
HIDDEN = 512


def lane_mask(pad, offset):
    return iota((pad, LANES), 1) == iota((pad, LANES), 0) + offset


def expert_kernel(
    n, pad,
    xd_ref, cr_ref, gs_ref, win_ref, wout_ref, win2_ref, wout2_ref,
    gx_ref, gg_ref, p_ref, own_in, own_out, got_in, got_out,
    xr_ref, gr_ref, gc_ref, wi_ref, wo_ref, act_ref, gi_ref, gxs_ref, ggs_ref, sum_gx, sum_p, sum_gg, gate_ref,
    x_send, x_recv, g_send, g_recv, gx_send, gx_recv, gg_send, gg_recv, w_sem, own_sem, dw_send, dw_recv, dw_sem,
):
    me = lax.axis_index("expert")
    core = lax.axis_index("ffn")
    half = win_ref.shape[1]
    parts = half // HIDDEN
    rows_all = n * pad
    barrier = greet(n, me, core, True)
    loads = []
    for j, (first, second) in enumerate(((win_ref, wout_ref), (win2_ref, wout2_ref))):
        for i in range(parts):
            at = j * parts + i
            cut = pl.ds(i * HIDDEN, HIDDEN)
            loads.append(pltpu.make_async_copy(first.at[:, cut], wi_ref.at[at], w_sem.at[2 * at]))
            loads.append(
                pltpu.make_async_copy(second.at[cut, :], wo_ref.at[at], w_sem.at[2 * at + 1])
            )
    for load in loads:
        load.start()

    def rows_of(e):
        return pl.ds(pl.multiple_of(e * pad, pad), pad)

    def tile_of(e):
        return pl.ds(pl.multiple_of(e * pad // LANES * LANES, LANES), LANES)

    def send(k, src, dst, sends, recvs):
        return pltpu.make_async_remote_copy(
            src_ref=src,
            dst_ref=dst,
            send_sem=sends.at[k],
            recv_sem=recvs.at[k],
            device_id=(partner(n, me, k), core),
            device_id_type=MESH,
        )

    def token_copy(k):
        target = partner(n, me, k)
        return send(k, xd_ref.at[rows_of(target)], xr_ref.at[rows_of(me)], x_send, x_recv)

    def gate_copy(k):
        target = partner(n, me, k)
        return send(k, gs_ref.at[:, tile_of(target)], gr_ref.at[me], g_send, g_recv)

    def grad_copy(k):
        target = partner(n, me, k)
        return send(k, gxs_ref.at[rows_of(target)], gx_ref.at[rows_of(me)], gx_send, gx_recv)

    def mark_copy(k):
        target = partner(n, me, k)
        return send(k, ggs_ref.at[target], gg_ref.at[me], gg_send, gg_recv)

    pl.semaphore_wait(barrier, n)

    def start_tokens(k):
        gate_copy(k).start()
        token_copy(k).start()

    each(n, start_tokens)
    xr_ref[rows_of(me), :] = xd_ref[rows_of(me), :]
    gr_ref[me] = gs_ref[:, tile_of(me)]
    offset = lax.rem(me * pad, LANES)
    mask = lane_mask(pad, offset)
    for load in loads:
        load.wait()
    per = ROWS // pad
    row_blocks = rows_all // ROWS

    @pl.loop(0, row_blocks)
    def _(step):
        block = block_at(n, me, step, per, row_blocks)
        rows = pl.ds(pl.multiple_of(block * ROWS, ROWS), ROWS)
        columns = []
        for u in range(per):
            source = block * per + u
            k = index_between(n, source, me, step)

            @pl.when(source != me)
            def _():
                gate_copy(k).wait_recv()
                token_copy(k).wait_recv()

            line = jnp.broadcast_to(gr_ref[source][:1], (pad, LANES))
            columns.append(jnp.sum(jnp.where(mask, line, 0.0), axis=1, keepdims=True))
        gates = jnp.concatenate(columns, axis=0)
        gate_ref[...] = jnp.broadcast_to(gates, gate_ref.shape)
        gc_ref[rows, :] = (gates * cr_ref[rows, :].astype(F32)).astype(BF16)
        sum_gx[...] = jnp.zeros_like(sum_gx)
        sum_p[...] = jnp.zeros_like(sum_p)
        sum_gg[...] = jnp.zeros_like(sum_gg)

        @pl.loop(0, 2 * parts)
        def _(i):
            inner = dot(xr_ref[rows, :], wi_ref[i])
            raw = dot(cr_ref[rows, :], wo_ref[i], 1, 1)
            normal = 0.5 * (1.0 + lax.erf(inner * RSQRT2))
            density = jnp.exp(-0.5 * inner * inner) * RSQRT2PI
            active = (inner * normal).astype(BF16)
            act_ref[i, rows, :] = active
            weighed = active.astype(F32) * raw
            folded = weighed[:, :LANES]
            for c in range(1, HIDDEN // LANES):
                folded = folded + weighed[:, c * LANES : (c + 1) * LANES]
            sum_gg[...] += folded
            grad = (gate_ref[:, :1] * raw * (normal + inner * density)).astype(BF16)
            gi_ref[i, rows, :] = grad
            sum_gx[...] += dot(grad, wi_ref[i], 1, 1)
            sum_p[...] += dot(active, wo_ref[i])

        gxs_ref[rows, :] = sum_gx[...].astype(BF16)
        p_ref[rows, :] = sum_p[...].astype(BF16)
        marks = jnp.sum(sum_gg[...], axis=1, keepdims=True)
        for u in range(per):
            source = block * per + u
            k = index_between(n, me, source, step)
            line = jnp.sum(
                jnp.where(mask, marks[u * pad : (u + 1) * pad], 0.0), axis=0, keepdims=True
            )
            ggs_ref[source] = jnp.broadcast_to(line, (8, LANES))

            @pl.when(source != me)
            def _():
                mark_copy(k).start()
                grad_copy(k).start()

    own = pltpu.make_async_copy(gxs_ref.at[rows_of(me)], gx_ref.at[rows_of(me)], own_sem)
    own.start()
    gg_ref[me] = ggs_ref[me]

    def wait_sent(k):
        token_copy(k).wait_send()
        gate_copy(k).wait_send()

    each(n, wait_sent)

    moves = []
    for j in (1, 0):
        for i in range(parts):
            at = j * parts + i
            cut = pl.ds(i * HIDDEN, HIDDEN)
            wi_ref[at] = dot(xr_ref[...], gi_ref[at], 0, 0).astype(BF16)
            wo_ref[at] = dot(act_ref[at], gc_ref[...], 0, 0).astype(BF16)
            for q, (src, dst) in enumerate(
                (
                    (wi_ref.at[at], (got_in if j else own_in).at[:, cut]),
                    (wo_ref.at[at], (got_out if j else own_out).at[cut, :]),
                )
            ):
                if j:
                    moves.append(
                        pltpu.make_async_remote_copy(
                            src_ref=src,
                            dst_ref=dst,
                            send_sem=dw_send.at[2 * i + q],
                            recv_sem=dw_recv.at[2 * i + q],
                            device_id=(me, 1 - core),
                            device_id_type=MESH,
                        )
                    )
                else:
                    moves.append(pltpu.make_async_copy(src, dst, dw_sem.at[2 * i + q]))
                moves[-1].start()
    for move in moves:
        move.wait()
    own.wait()

    def finish(k):
        mark_copy(k).wait()
        grad_copy(k).wait()

    each(n, finish)


def run_experts(n, pad, xd, cr, gs, win, wout, win2, wout2):
    rows, width = xd.shape
    half = win.shape[1]
    parts = half // HIDDEN
    vmem = pl.BlockSpec(memory_space=pltpu.VMEM)
    anywhere = pl.BlockSpec(memory_space=pl.ANY)
    shapes = (
        ((rows, width), BF16, anywhere),
        ((n, 8, LANES), F32, vmem),
        ((rows, width), BF16, vmem),
        ((width, half), BF16, anywhere),
        ((half, width), BF16, anywhere),
        ((width, half), BF16, anywhere),
        ((half, width), BF16, anywhere),
    )
    return pl.pallas_call(
        functools.partial(expert_kernel, n, pad),
        out_shape=[jax.ShapeDtypeStruct(shape, dtype) for shape, dtype, _ in shapes],
        in_specs=[vmem] * 3 + [anywhere] * 4,
        out_specs=[space for _, _, space in shapes],
        scratch_shapes=[
            pltpu.VMEM((rows, width), BF16),
            pltpu.VMEM((n, 8, LANES), F32),
            pltpu.VMEM((rows, width), BF16),
            pltpu.VMEM((2 * parts, width, HIDDEN), BF16),
            pltpu.VMEM((2 * parts, HIDDEN, width), BF16),
            pltpu.VMEM((2 * parts, rows, HIDDEN), BF16),
            pltpu.VMEM((2 * parts, rows, HIDDEN), BF16),
            pltpu.VMEM((rows, width), BF16),
            pltpu.VMEM((n, 8, LANES), F32),
            pltpu.VMEM((ROWS, width), F32),
            pltpu.VMEM((ROWS, width), F32),
            pltpu.VMEM((ROWS, LANES), F32),
            pltpu.VMEM((ROWS, LANES), F32),
        ]
        + [pltpu.SemaphoreType.DMA((n,))] * 8
        + [
            pltpu.SemaphoreType.DMA((4 * parts,)),
            pltpu.SemaphoreType.DMA,
            pltpu.SemaphoreType.DMA((2 * parts,)),
            pltpu.SemaphoreType.DMA((2 * parts,)),
            pltpu.SemaphoreType.DMA((2 * parts,)),
        ],
        compiler_params=pltpu.CompilerParams(
            collective_id=1, has_side_effects=True, vmem_limit_bytes=60 * 1024 * 1024
        ),
        name="experts",
    )(xd, cr, gs, win, wout, win2, wout2)
def unit_rows(n, rows):
    return -(-rows // (n * 16)) * 16


def reduce_rows(n, width):
    return [n * unit_rows(n, 3 * width)] * 4 + [n * unit_rows(n, 3 * n + 32)]


def reduce_shapes(n, width):
    stages = n.bit_length() - 1
    scratch = []
    for rows in reduce_rows(n, width):
        scratch.append(pltpu.VMEM((rows, LANES), BF16))
        scratch += [pltpu.VMEM((rows >> (s + 1), LANES), BF16) for s in range(stages)]
    return scratch + [pltpu.SemaphoreType.DMA((5, 2 * stages + 2))] * 2


def reduce_peer(me, core, s):
    distance = (1 + core, 2 - core)[s] if s < 2 else 2**s
    side = lax.rem(me // distance, 2)
    return me + distance * (1 - 2 * side), side


def reduce_steps(n, me, core, j, part, arrived, halves, total, sends, recvs):
    stages = n.bit_length() - 1
    unit = part.shape[1] // n
    sides, peers, starts = [], [], [0]
    for s in range(stages):
        peer, side = reduce_peer(me, core, s)
        peers.append(peer)
        sides.append(side)
        starts.append(starts[-1] + side * (n >> (s + 1)))

    def region(start, units):
        return pl.ds(pl.multiple_of(start * unit, unit), units * unit)

    def copy(step, src, dst, device):
        return pltpu.make_async_remote_copy(
            src_ref=src,
            dst_ref=dst,
            send_sem=sends.at[j, step],
            recv_sem=recvs.at[j, step],
            device_id=device,
            device_id_type=MESH,
        )

    def transfer(step):
        if step == 0:
            return copy(step, part.at[1 - core], arrived, (me, 1 - core))
        if step <= stages:
            s = step - 1
            size = n >> (s + 1)
            away = starts[s] + (1 - sides[s]) * size
            return copy(step, part.at[core, region(away, size)], halves[s], (peers[s], core))
        if step <= 2 * stages:
            s = 2 * stages - step
            held = total.at[core, region(starts[s + 1], n >> (s + 1))]
            return copy(step, held, held, (peers[s], core))
        return copy(step, total.at[core], total.at[core], (me, 1 - core))

    def add(step):
        if step == 0:
            part[core] = (part[core].astype(F32) + arrived[...].astype(F32)).astype(BF16)
        elif step <= stages:
            s = step - 1
            mine = region(starts[s + 1], n >> (s + 1))
            summed = (part[core, mine, :].astype(F32) + halves[s][...].astype(F32)).astype(BF16)
            if step == stages:
                total[core, mine, :] = summed
            else:
                part[core, mine, :] = summed

    last = 2 * stages + 1

    def run(step):
        if step > 0:
            transfer(step - 1).wait_recv()
            add(step - 1)
        if step <= last:
            transfer(step).start()
        else:
            for done in range(last + 1):
                transfer(done).wait_send()

    return [functools.partial(run, step) for step in range(last + 2)]


def reducers(n, me, core, parts, totals, scratch):
    stages = n.bit_length() - 1
    size = stages + 1
    sends, recvs = scratch[-2:]
    return [
        reduce_steps(
            n, me, core, j, parts[j], scratch[j * size],
            scratch[j * size + 1 : (j + 1) * size], totals[j], sends, recvs,
        )
        for j in range(5)
    ]


def unroll_band(band):
    wide = band.shape[1]
    folded = band[:8]
    for g in range(1, band.shape[0] // 8):
        folded = folded + pltpu.roll(band[8 * g : 8 * g + 8], wide - 8 * g, 1)
    line = folded[:1]
    for s in range(1, 8):
        line = line + pltpu.roll(folded, wide - s, 1)[s : s + 1]
    return line


PLAN = (
    (0,),
    ((), (), (), (), (), ()),
    ((1, 0), (2, 1, 0), (3, 2, 1, 0)),
    (0, 1, 2, 3),
    (0, 1, 2, 3, 4),
)


def back_kernel(
    n, pad,
    tok_ref, ga_ref, wq_ref, wk_ref, wv_ref, wo_ref, gf_ref, wrt_ref, routes_ref, cot_ref, st_ref, gx_ref, gg_ref, p_ref,
    nat_ref, qt_ref, kt_ref, v_ref, probs_hbm, mixt_ref, hid_ref, nf_ref, pr_ref, gcol_ref,
    out_ref, dx_ref, total0, totals, total4,
    got_ref, probs_ref, gmt_ref, gqt_ref, gkt_ref, gvt_ref, lines_ref,
    send_sem, recv_sem, probs_sem, own_sem, part0, part1, part2, part3, part4, *reduce_scratch,
):
    me = lax.axis_index("expert")
    core = lax.axis_index("ffn")
    count, width = tok_ref.shape
    rows_all = n * pad
    barrier = greet(n, me, core, True)

    def load(pair):
        return pltpu.make_async_copy(
            probs_hbm.at[pl.ds(2 * pair, 2)], probs_ref.at[pair % 2], probs_sem.at[pair % 2]
        )

    load(0).start()
    load(1).start()

    def rows_of(e):
        return pl.ds(pl.multiple_of(e * pad, pad), pad)

    def copy(k):
        target = partner(n, me, k)
        return pltpu.make_async_remote_copy(
            src_ref=p_ref.at[rows_of(target)],
            dst_ref=got_ref.at[rows_of(me)],
            send_sem=send_sem.at[k],
            recv_sem=recv_sem.at[k],
            device_id=(target, core),
            device_id_type=MESH,
        )

    pl.semaphore_wait(barrier, n)
    each(n, lambda k: copy(k).start())
    own = pltpu.make_async_copy(p_ref.at[rows_of(me)], got_ref.at[rows_of(me)], own_sem)
    own.start()
    parts = (part0, part1, part2, part3, part4)
    queue = reducers(
        n, me, core, parts, [total0, totals.at[0], totals.at[1], totals.at[2], total4], reduce_scratch
    )
    done = [0] * 5

    def tick(*chosen):
        for j in chosen:
            if done[j] < len(queue[j]):
                queue[j][done[j]]()
                done[j] += 1

    base = 3 * width
    for part, filled in zip(parts, [base] * 4 + [3 * n + 32]):
        if part.shape[1] > filled:
            part[:, filled:, :] = jnp.zeros((2, part.shape[1] - filled, LANES), BF16)

    share = LANES // pad
    tiles = []
    for t in range(n // share):
        tile = gg_ref[t * share][:1]
        for u in range(1, share):
            tile = tile + gg_ref[t * share + u][:1]
        tiles.append(tile)
    marks = jnp.concatenate(tiles, axis=1)
    grad_gate = jnp.sum(dot(pieces(marks), st_ref[...], 1, 1), axis=0, keepdims=True)
    chosen = (iota((n, count), 0) == routes_ref[...]).astype(F32)
    router = pr_ref[...]
    grad_probs = chosen * grad_gate
    grad_logits = router * (grad_probs - jnp.sum(router * grad_probs, axis=0, keepdims=True))
    grad_logits = grad_logits.astype(BF16)
    grad_router = dot(nf_ref[...], grad_logits, 0, 1).T
    grad_nf = dot(st_ref[...], gx_ref[...]) + dot(grad_logits, wrt_ref[...], 0, 0)
    hidden = hid_ref[...]
    scale = lax.rsqrt(jnp.mean(hidden * hidden, axis=-1, keepdims=True) + EPSILON)
    weighted = grad_nf * gf_ref[...][None]
    grad_gain_ffn = jnp.sum(grad_nf * hidden * scale, axis=0, keepdims=True)
    inner = jnp.mean(weighted * hidden, axis=-1, keepdims=True)
    grad_hidden = (
        cot_ref[...].astype(F32) + scale * weighted - hidden * (scale * scale * scale * inner)
    )
    dx_ref[...] = grad_hidden
    branch = grad_hidden.astype(BF16)
    for t in range(width // LANES):
        cut = slice(t * LANES, (t + 1) * LANES)
        rows = slice(t % 3 * width, (t % 3 + 1) * width)
        part0[t // 3, rows, :] = dot(mixt_ref[...], branch[:, cut]).astype(BF16)
    tick(*PLAN[0])
    gmt_ref[...] = dot(wo_ref[...], branch, 1, 1).astype(BF16)
    lines_ref[...] = jnp.zeros_like(lines_ref)
    lower_half = iota((LANES, count), 0) < HEAD_DIM
    blocks = count // LANES
    place = iota((1, 4 * LANES), 1)

    def run_pair(pair):
        load(pair).wait()
        lanes = pl.ds(pair * LANES, LANES)
        both = gmt_ref[lanes, :]
        for sub in range(2):
            head = 2 * pair + sub
            mask = lower_half if sub == 0 else jnp.logical_not(lower_half)
            chunk = jnp.where(mask, both, jnp.zeros_like(both))
            features = pl.ds(head * HEAD_DIM, HEAD_DIM)
            grad_mixed = gmt_ref[features, :]
            delta = jnp.sum(
                grad_mixed.astype(F32) * mixt_ref[features, :].astype(F32), axis=0, keepdims=True
            )
            probs = probs_ref[pair % 2, sub]
            grad_probs = dot(v_ref[:, lanes], chunk)
            scores = probs.astype(F32) * (grad_probs - delta)
            low = scores.astype(BF16)
            gqt_ref[features, :] = dot(kt_ref[features, :], low).astype(BF16)
            gkt_ref[features, :] = dot(qt_ref[features, :], low, 1, 1).astype(BF16)
            gvt_ref[features, :] = dot(grad_mixed, probs, 1, 1).astype(BF16)
            near = {0: None, -1: None, 1: None}
            far = {-1: None, 1: None}
            for row in range(blocks):
                for col in range(blocks):
                    block = scores[
                        row * LANES : (row + 1) * LANES, col * LANES : (col + 1) * LANES
                    ]
                    gap = row - col
                    if gap in near:
                        near[gap] = block if near[gap] is None else near[gap] + block
                    else:
                        side = 1 if gap > 0 else -1
                        far[side] = block if far[side] is None else far[side] + block
            band = jnp.concatenate([near[0], near[-1], jnp.zeros_like(near[0]), near[1]], axis=1)
            line = unroll_band(band)
            for side, lane in ((-1, 255), (1, 257)):
                total = jnp.sum(jnp.sum(far[side], axis=0, keepdims=True), axis=1, keepdims=True)
                line = line + jnp.where(place == lane, total, 0.0)
            lines_ref[pl.ds(head, 1), :] = line
        if pair + 2 < HEADS // 2:
            load(pair + 2).start()

    for group, part in enumerate((part1, part2, part3)):
        for pair in (2 * group, 2 * group + 1):
            run_pair(pair)
            tick(*PLAN[1][pair])
        for i, grad in enumerate((gqt_ref, gkt_ref, gvt_ref)):
            columns = grad[group * 2 * LANES : (group + 1) * 2 * LANES, :]
            made = dot(nat_ref[...], columns, 1, 1).astype(BF16)
            for c in range(2):
                part[c, i * width : (i + 1) * width, :] = made[:, c * LANES : (c + 1) * LANES]
        tick(*PLAN[2][group])
    grad_na = (
        dot(wq_ref[...], gqt_ref[...])
        + dot(wk_ref[...], gkt_ref[...])
        + dot(wv_ref[...], gvt_ref[...])
    ).T
    x = tok_ref[...].astype(F32)
    scale = lax.rsqrt(jnp.mean(x * x, axis=-1, keepdims=True) + EPSILON)
    weighted = grad_na * ga_ref[...][None]
    grad_gain_attn = jnp.sum(grad_na * x * scale, axis=0, keepdims=True)
    inner = jnp.mean(weighted * x, axis=-1, keepdims=True)
    tick(*PLAN[3])
    dx_ref[...] = dx_ref[...] + scale * weighted - x * (scale * scale * scale * inner)
    grad_bias = dot(band_onehot(), lines_ref[...], 1, 1, HIGH)
    gains = jnp.concatenate([grad_gain_attn, grad_gain_ffn, jnp.zeros((14, width), F32)], axis=0)
    for c in range(2):
        for t in range(3):
            cut = slice((3 * c + t) * LANES, (3 * c + t + 1) * LANES)
            part4[c, t * n : (t + 1) * n, :] = grad_router[:, cut].astype(BF16)
        rows = slice(3 * n, 3 * n + 16)
        sums = [gains[:, (3 * c + t) * LANES : (3 * c + t + 1) * LANES][:2] for t in range(3)]
        part4[c, rows, :] = jnp.concatenate(sums + [jnp.zeros((10, LANES), F32)], axis=0).astype(BF16)
        rows = slice(3 * n + 16, 3 * n + 32)
        wide = jnp.concatenate(
            [grad_bias[16 * c : 16 * c + 16], jnp.zeros((16, LANES - 16), F32)], axis=1
        )
        part4[c, rows, :] = wide.astype(BF16)
    tick(*PLAN[4])
    own.wait()
    each(n, lambda k: copy(k).wait())
    picked = dot(st_ref[...], got_ref[...])
    out_ref[...] = (hid_ref[...] + gcol_ref[:, :1] * picked).astype(BF16)
    while any(done[j] < len(queue[j]) for j in range(5)):
        tick(0, 1, 2, 3, 4)


def run_back(n, pad, tokens, *rest):
    count, width = tokens.shape
    rows = n * pad
    vmem = pl.BlockSpec(memory_space=pltpu.VMEM)
    anywhere = pl.BlockSpec(memory_space=pl.ANY)
    shapes = (
        ((count, width), BF16, vmem),
        ((count, width), F32, vmem),
        ((2, reduce_rows(n, width)[0], LANES), BF16, vmem),
        ((3, 2, reduce_rows(n, width)[0], LANES), BF16, vmem),
        ((2, reduce_rows(n, width)[4], LANES), BF16, vmem),
    )
    return pl.pallas_call(
        functools.partial(back_kernel, n, pad),
        out_shape=[jax.ShapeDtypeStruct(shape, dtype) for shape, dtype, _ in shapes],
        in_specs=[vmem] * 13 + [anywhere] + [vmem] * 4 + [anywhere] + [vmem] * 5,
        out_specs=[space for _, _, space in shapes],
        scratch_shapes=[
            pltpu.VMEM((rows, width), BF16),
            pltpu.VMEM((2, 2, count, count), BF16),
            pltpu.VMEM((width, count), BF16),
            pltpu.VMEM((width, count), BF16),
            pltpu.VMEM((width, count), BF16),
            pltpu.VMEM((width, count), BF16),
            pltpu.VMEM((16, 4 * LANES), F32),
            pltpu.SemaphoreType.DMA((n,)),
            pltpu.SemaphoreType.DMA((n,)),
            pltpu.SemaphoreType.DMA((2,)),
            pltpu.SemaphoreType.DMA,
            *(pltpu.VMEM((2, part, LANES), BF16) for part in reduce_rows(n, width)),
            *reduce_shapes(n, width),
        ],
        compiler_params=pltpu.CompilerParams(
            collective_id=2, has_side_effects=True, vmem_limit_bytes=63 * 1024 * 1024
        ),
        name="attend_back",
    )(tokens, *rest)


def finish_kernel(
    n,
    first0, first1, first2, q_ref, k_ref, v_ref, small_ref, own_in, got_in, own_out, got_out, out_ref, dx_ref, rms_ref,
    go_ref, gq_ref, gk_ref, gv_ref, gi_ref, gw_ref, router_ref, gain_a, gain_f, bias_ref, output_ref, grad_ref, roots_ref,
):
    for t in range(6):
        cut = slice(t * LANES, (t + 1) * LANES)
        go_ref[:, cut] = (first0, first1, first2)[t % 3][t // 3].astype(F32)
        for made, grad in ((gq_ref, q_ref), (gk_ref, k_ref), (gv_ref, v_ref)):
            made[:, cut] = grad[t // 2, t % 2].astype(F32)
    gi_ref[...] = own_in[...].astype(F32) + got_in[...].astype(F32)
    gw_ref[...] = own_out[...].astype(F32) + got_out[...].astype(F32)
    output_ref[...] = out_ref[...]
    grad_ref[...] = dx_ref[...]

    @pl.when(pl.program_id(0) == 0)
    def _():
        roots_ref[...] = rms_ref[3:5, :]
        small = small_ref[...].astype(F32)
        for t in range(6):
            c, at = t // 3, t % 3
            cut = slice(t * LANES, (t + 1) * LANES)
            router_ref[:, cut] = small[c, at * n : (at + 1) * n]
            gain_a[cut] = small[c, 3 * n + 2 * at]
            gain_f[cut] = small[c, 3 * n + 2 * at + 1]
        bias = jnp.concatenate([small[c, 3 * n + 16 : 3 * n + 32] for c in range(2)], axis=0)
        bias_ref[...] = bias.T[:HEADS]


def run_finish(n, first, groups, smalls, own_in, got_in, own_out, got_out, out, dx, rms):
    width, half = own_in.shape
    count = out.shape[0]
    steps = width // LANES
    whole = lambda *shape: pl.BlockSpec(shape, lambda t: (0,) * len(shape))
    by_rows = lambda rows, columns: pl.BlockSpec((rows, columns), lambda t: (t, 0))
    out_part = lambda i: pl.BlockSpec((2, LANES, LANES), lambda t: (0, i * steps + t, 0))
    weight = lambda i: pl.BlockSpec((3, 2, LANES, LANES), lambda t: (0, 0, i * steps + t, 0))
    grad_shape = jax.ShapeDtypeStruct((width, width), F32)
    some = pl.BlockSpec((count // 4, width), lambda t: (jnp.minimum(t, 3), 0))
    rows_in, rows_out = by_rows(LANES, half), by_rows(half // steps, width)
    return pl.pallas_call(
        functools.partial(finish_kernel, n),
        grid=(steps,),
        out_shape=[
            grad_shape,
            grad_shape,
            grad_shape,
            grad_shape,
            jax.ShapeDtypeStruct((width, half), F32),
            jax.ShapeDtypeStruct((half, width), F32),
            jax.ShapeDtypeStruct((n, width), F32),
            jax.ShapeDtypeStruct((width,), F32),
            jax.ShapeDtypeStruct((width,), F32),
            jax.ShapeDtypeStruct((HEADS, BUCKETS), F32),
            jax.ShapeDtypeStruct((count, width), BF16),
            jax.ShapeDtypeStruct((count, width), F32),
            jax.ShapeDtypeStruct((2, count), F32),
        ],
        in_specs=[out_part(i) for i in range(3)]
        + [weight(i) for i in range(3)]
        + [whole(*smalls.shape), rows_in, rows_in, rows_out, rows_out, some, some, whole(8, count)],
        out_specs=[by_rows(LANES, width)] * 4
        + [rows_in, rows_out]
        + [whole(n, width), whole(width), whole(width), whole(HEADS, BUCKETS)]
        + [some, some, whole(2, count)],
        compiler_params=pltpu.CompilerParams(vmem_limit_bytes=60 * 1024 * 1024),
        name="finish",
    )(first, first, first, groups, groups, groups, smalls, own_in, got_in, own_out, got_out, out, dx, rms)


def per_device(
    tokens, gain_attn, query_weight, key_weight, value_weight, out_weight, rel_bias, gain_ffn, router_weight,
    expert_in, expert_out, routes, capacity, cotangent,
):
    count, width = tokens.shape
    n = lax.axis_size("expert")
    experts = router_weight.shape[1]
    assert experts == n and count == SEQ
    slots = 2 * count // experts
    pad = -(-slots // 16) * 16
    router_rows = router_weight.T
    routes = routes.reshape(1, count)
    (
        cots, in_other, out_other, dispatched, gates, slots_t, normed_t, query_t, key_t, values, probs, mixed_t,
        hidden, normed_ffn, router_t, gate_col, roots,
    ) = attend(
        n, slots, pad, tokens, gain_attn, query_weight, key_weight, value_weight, out_weight, rel_bias.T, gain_ffn,
        router_rows, routes, capacity, cotangent, expert_in[0], expert_out[0],
    )
    grad_rows, marks, produced, own_in, own_out, got_in, got_out = run_experts(
        n, pad, dispatched, cots, gates, expert_in[0], expert_out[0], in_other, out_other
    )
    output, input_grad, first, groups, smalls = run_back(
        n, pad, tokens, gain_attn, query_weight, key_weight, value_weight, out_weight, gain_ffn, router_rows, routes,
        cotangent, slots_t, grad_rows, marks, produced, normed_t, query_t, key_t, values, probs, mixed_t, hidden,
        normed_ffn, router_t, gate_col,
    )
    (
        grad_out, grad_query, grad_key, grad_value, grad_in, grad_expert, grad_router, grad_gain_attn, grad_gain_ffn,
        grad_bias, output, input_grad, rms_values,
    ) = run_finish(n, first, groups, smalls, own_in, got_in, own_out, got_out, output, input_grad, roots)
    return (
        output,
        input_grad,
        grad_gain_attn,
        grad_query,
        grad_key,
        grad_value,
        grad_out,
        grad_bias.T,
        grad_gain_ffn,
        grad_router.T,
        grad_in[None],
        grad_expert[None],
        rms_values,
    )


def solution(mesh):
    placed = (
        P(("expert", "ffn"), None),
        P(),
        P(),
        P(),
        P(),
        P(),
        P(),
        P(),
        P(),
        P("expert", None, "ffn"),
        P("expert", "ffn", None),
        P(("expert", "ffn"), None),
        P(("expert", "ffn")),
        P(("expert", "ffn"), None),
    )
    return jax.shard_map(
        per_device,
        mesh=mesh,
        in_specs=placed,
        out_specs=(
            P(("expert", "ffn"), None),
            P(("expert", "ffn"), None),
            P(),
            P(),
            P(),
            P(),
            P(),
            P(),
            P(),
            P(),
            P("expert", None, "ffn"),
            P("expert", "ffn", None),
            P(None, ("expert", "ffn")),
        ),
        check_vma=False,
    )
```

```python
import functools
import jax
import jax.numpy as jnp
from jax import lax
from jax.experimental import pallas as pl
from jax.experimental.pallas import tpu as pltpu
from jax.sharding import PartitionSpec as P

HEADS = 12
HEAD_DIM = 64
BUCKETS = 32
SEQ = 512
EPSILON = 1e-06
THRESHOLDS = (12, 16, 23, 32, 46, 64, 91)
HIGH = lax.Precision.HIGHEST
F32 = jnp.float32
BF16 = jnp.bfloat16
MESH = pl.DeviceIdType.MESH
LANES = 128


def dot(a, b, ca=1, cb=0, precision=None):
    return lax.dot_general(
        a, b, (((ca,), (cb,)), ((), ())), precision=precision, preferred_element_type=F32
    )


def iota(shape, dim):
    return lax.broadcasted_iota(jnp.int32, shape, dim)


def div(a, b):
    return a // b if isinstance(a, int) else lax.div(a, jnp.int32(b))


def rem(a, b):
    return a % b if isinstance(a, int) else lax.rem(a, jnp.int32(b))


def block_at(n, me, step, per, blocks):
    if n != 16:
        return rem(div(me, per) + step, blocks)
    layer = div(me, 4)
    low = rem(rem(layer, 2) + div(step + 1, 2), 2)
    return 2 * rem(div(layer, 2) + 1 - div(step, 2), 2) + low


def partner(n, me, k):
    if n != 16:
        return rem(me + k, n)
    return 4 * block_at(n, me, div(k, 4), 4, 4) + rem(rem(me, 4) + rem(k, 4), 4)


def index_between(n, sender, receiver, step):
    if n != 16:
        return rem(receiver - sender + n, n)
    return 4 * step + rem(rem(receiver, 4) - rem(sender, 4) + 4, 4)


def each(n, body):
    if n == 16:
        for k in range(n):
            if k != 12:
                body(k)
    else:

        def step(k, carry):
            body(k)
            return carry

        lax.fori_loop(1, n, step, 0)


def greet(n, me, core, sibling):
    barrier = pltpu.get_barrier_semaphore()

    def signal(k):
        pl.semaphore_signal(
            barrier, inc=1, device_id=(partner(n, me, k), core), device_id_type=MESH
        )

    each(n, signal)
    if sibling:
        pl.semaphore_signal(barrier, inc=1, device_id=(me, 1 - core), device_id_type=MESH)
    return barrier


def band_onehot():
    place = iota((BUCKETS, 4 * LANES), 1)
    offset = jnp.where(place < 2 * LANES, -place, 4 * LANES - place)
    distance = jnp.abs(offset)
    larger = jnp.full(distance.shape, 8, jnp.int32)
    for limit in THRESHOLDS:
        larger = larger + (distance >= limit).astype(jnp.int32)
    bucket = jnp.where(distance < 8, distance, larger) + jnp.where(offset > 0, 16, 0)
    return (bucket == iota(bucket.shape, 0)).astype(F32)


def pieces(row):
    high = row.astype(BF16)
    rest = row - high.astype(F32)
    middle = rest.astype(BF16)
    low = (rest - middle.astype(F32)).astype(BF16)
    filler = jnp.zeros((5, row.shape[1]), BF16)
    return jnp.concatenate([high, middle, low, filler], axis=0)


def fetch(sem, *pairs):
    copies = [pltpu.make_async_copy(src, dst, sem.at[i]) for i, (src, dst) in enumerate(pairs)]
    for copy in copies:
        copy.start()

    def need(*which):
        for i in which:
            copies[i].wait()

    return need


def attend_kernel(
    n, slots, pad,
    tok_hbm, ga_ref, wq_hbm, wk_hbm, wv_hbm, wo_hbm, rel_ref, gf_ref, wrt_ref, routes_ref, cap_ref, cot_ref, win_ref, wout_ref,
    cr_ref, wi2_ref, wo2_ref, xd_hbm, gs_ref, st_hbm, nat_hbm, qt_hbm, kt_hbm, v_hbm, p_hbm, mixt_hbm, hid_hbm, nf_hbm, pr_ref, gcol_ref, rms_ref,
    cd_ref, s_ref, k_ref, vt_ref, band_ref, send_sem, recv_sem, own_sem, w_send, w_recv,
    tok_ref, wq_ref, wk_ref, wv_ref, wo_ref, xd_ref, st_ref, nat_ref, qt_ref, kt_ref, v_ref, p_ref, mixt_ref, hid_ref, nf_ref,
    load_sem, save_sem, probs_sem,
):
    me = lax.axis_index("expert")
    core = lax.axis_index("ffn")
    count, width = tok_ref.shape
    rows_all = n * pad
    barrier = greet(n, me, core, True)
    need = fetch(
        load_sem,
        (tok_hbm, tok_ref), (wq_hbm, wq_ref), (wk_hbm, wk_ref), (wv_hbm, wv_ref), (wo_hbm, wo_ref),
    )
    saves = []

    def save(src, dst):
        saves.append(pltpu.make_async_copy(src, dst, save_sem.at[len(saves)]))
        saves[-1].start()


    routes = routes_ref[...]
    chosen = (iota((n, count), 0) == routes).astype(F32)
    upper = (iota((count, count), 0) < iota((count, count), 1)).astype(F32).astype(BF16)
    earlier = dot(chosen.astype(BF16), upper)
    position = jnp.sum(earlier * chosen, axis=0, keepdims=True)
    live = (cap_ref[0] * count // n).astype(F32)
    slot = jnp.where(position < live, routes * pad + position.astype(jnp.int32), rows_all)

    @pl.loop(0, rows_all // 256)
    def _(block):
        start = pl.multiple_of(block * 256, 256)
        hot = (iota((256, count), 0) + start == slot).astype(F32).astype(BF16)
        s_ref[pl.ds(start, 256), :] = hot
        cd_ref[pl.ds(start, 256), :] = dot(hot, cot_ref[...]).astype(BF16)

    pl.semaphore_wait(barrier, n)

    def rows_of(e):
        return pl.ds(pl.multiple_of(e * pad, pad), pad)

    def copy(k):
        target = partner(n, me, k)
        return pltpu.make_async_remote_copy(
            src_ref=cd_ref.at[rows_of(target)],
            dst_ref=cr_ref.at[rows_of(me)],
            send_sem=send_sem.at[k],
            recv_sem=recv_sem.at[k],
            device_id=(target, core),
            device_id_type=MESH,
        )

    each(n, lambda k: copy(k).start())
    own = pltpu.make_async_copy(cd_ref.at[rows_of(me)], cr_ref.at[rows_of(me)], own_sem)
    own.start()
    halves = [
        pltpu.make_async_remote_copy(
            src_ref=src,
            dst_ref=dst,
            send_sem=w_send.at[i],
            recv_sem=w_recv.at[i],
            device_id=(me, 1 - core),
            device_id_type=MESH,
        )
        for i, (src, dst) in enumerate(((win_ref, wi2_ref), (wout_ref, wo2_ref)))
    ]
    for half in halves:
        half.start()

    need(0)
    x = tok_ref[...].astype(F32)
    ms1 = jnp.mean(x * x, axis=-1, keepdims=True)
    na = (x * lax.rsqrt(ms1 + EPSILON) * ga_ref[...][None]).astype(BF16)
    nat_ref[...] = na.T
    need(1)
    qt_ref[...] = dot(na, wq_ref[...]).astype(BF16).T
    need(2)
    keys = dot(na, wk_ref[...]).astype(BF16)
    k_ref[...] = keys
    kt_ref[...] = keys.T
    need(3)
    values = dot(na, wv_ref[...]).astype(BF16)
    v_ref[...] = values
    vt_ref[...] = values.T
    save(nat_ref, nat_hbm)
    save(qt_ref, qt_hbm)
    save(kt_ref, kt_hbm)
    save(v_ref, v_hbm)
    band_ref[...] = dot(rel_ref[...], band_onehot(), 1, 0, HIGH)
    lower_half = iota((LANES, count), 0) < HEAD_DIM
    blocks = count // LANES

    def save_probs(pair):
        heads = pl.ds(2 * pair, 2)
        return pltpu.make_async_copy(p_ref.at[heads], p_hbm.at[heads], probs_sem.at[pair])

    @pl.loop(0, HEADS // 2)
    def _(pair):
        lanes = pl.ds(pl.multiple_of(pair * LANES, LANES), LANES)
        both = qt_ref[lanes, :]
        for sub in range(2):
            head = 2 * pair + sub
            mask = lower_half if sub == 0 else jnp.logical_not(lower_half)
            query = jnp.where(mask, both, jnp.zeros_like(both))
            line = band_ref[pl.ds(head, 1), :]
            band = pltpu.roll(
                jnp.broadcast_to(line, (LANES, 4 * LANES)), 0, 1, stride=1, stride_axis=0
            )
            before = jnp.broadcast_to(line[:, 255:256], (LANES, LANES))
            after = jnp.broadcast_to(line[:, 257:258], (LANES, LANES))
            by_gap = {
                0: band[:, :LANES],
                -1: band[:, LANES : 2 * LANES],
                1: band[:, 3 * LANES :],
            }
            scores = []
            for row in range(blocks):
                bias = jnp.concatenate(
                    [
                        by_gap.get(row - col, after if row > col else before)
                        for col in range(blocks)
                    ],
                    axis=1,
                )
                made = dot(k_ref[row * LANES : (row + 1) * LANES, lanes], query)
                scores.append(made + bias)
            scores = jnp.concatenate(scores, axis=0)
            peak = jnp.max(scores, axis=0, keepdims=True)
            expo = jnp.exp(scores - peak)
            total = jnp.sum(expo, axis=0, keepdims=True)
            probs = (expo * (1.0 / total)).astype(BF16)
            p_ref[head] = probs
            features = pl.ds(pl.multiple_of(head * HEAD_DIM, HEAD_DIM), HEAD_DIM)
            mixt_ref[features, :] = dot(vt_ref[features, :], probs).astype(BF16)
        save_probs(pair).start()

    save(mixt_ref, mixt_hbm)
    need(4)
    hidden = tok_ref[...].astype(F32) + dot(mixt_ref[...].T, wo_ref[...])
    hid_ref[...] = hidden
    save(hid_ref, hid_hbm)
    ms2 = jnp.mean(hidden * hidden, axis=-1, keepdims=True)
    nf = (hidden * lax.rsqrt(ms2 + EPSILON) * gf_ref[...][None]).astype(BF16)
    nf_ref[...] = nf
    save(nf_ref, nf_hbm)
    logits = dot(wrt_ref[...], nf, 1, 1)
    top = jnp.max(logits, axis=0, keepdims=True)
    raised = jnp.exp(logits - top)
    router = raised / jnp.sum(raised, axis=0, keepdims=True)
    pr_ref[...] = router
    gate = jnp.sum(router * chosen, axis=0, keepdims=True)
    gcol_ref[...] = jnp.broadcast_to(gate, (LANES, count)).T
    roots = jnp.concatenate(
        [
            jnp.broadcast_to(jnp.sqrt(ms + EPSILON), (count, LANES)).T[:4]
            for ms in (ms1, ms2)
        ],
        axis=0,
    )
    rms_ref[...] = roots
    parts = pieces(gate)

    @pl.loop(0, rows_all // 256)
    def _(block):
        start = pl.multiple_of(block * 256, 256)
        hot = s_ref[pl.ds(start, 256), :]
        xd_ref[pl.ds(start, 256), :] = dot(hot, nf_ref[...]).astype(BF16)
        split = dot(parts, hot, 1, 1)
        gs_ref[:, pl.ds(start, 256)] = jnp.broadcast_to(
            jnp.sum(split, axis=0, keepdims=True), split.shape
        )
        st_ref[:, pl.ds(start, 256)] = hot.T

    save(xd_ref, xd_hbm)
    save(st_ref, st_hbm)
    for pair in range(HEADS // 2):
        save_probs(pair).wait()
    for copied in saves:
        copied.wait()
    own.wait()
    for half in halves:
        half.wait()
    each(n, lambda k: copy(k).wait())


def attend(n, slots, pad, tokens, ga, wq, wk, wv, wo, rel, gf, wrt, routes, cap, cot, win, wout):
    count, width = tokens.shape
    rows = n * pad
    half = win.shape[-1]
    vmem = pl.BlockSpec(memory_space=pltpu.VMEM)
    anywhere = pl.BlockSpec(memory_space=pl.ANY)
    smem = pl.BlockSpec(memory_space=pltpu.SMEM)
    shapes = (
        ((rows, width), BF16, anywhere),
        ((width, half), BF16, anywhere),
        ((half, width), BF16, anywhere),
        ((rows, width), BF16, anywhere),
        ((8, rows), F32, vmem),
        ((count, rows), BF16, anywhere),
        ((width, count), BF16, anywhere),
        ((width, count), BF16, anywhere),
        ((width, count), BF16, anywhere),
        ((count, width), BF16, anywhere),
        ((HEADS, count, count), BF16, anywhere),
        ((width, count), BF16, anywhere),
        ((count, width), F32, anywhere),
        ((count, width), BF16, anywhere),
        ((n, count), F32, vmem),
        ((count, LANES), F32, vmem),
        ((8, count), F32, vmem),
    )
    return pl.pallas_call(
        functools.partial(attend_kernel, n, slots, pad),
        out_shape=[jax.ShapeDtypeStruct(shape, dtype) for shape, dtype, _ in shapes],
        in_specs=[anywhere, vmem] + [anywhere] * 4 + [vmem] * 4 + [smem, vmem, anywhere, anywhere],
        out_specs=[space for _, _, space in shapes],
        scratch_shapes=[
            pltpu.VMEM((rows, width), BF16),
            pltpu.VMEM((rows, count), BF16),
            pltpu.VMEM((count, width), BF16),
            pltpu.VMEM((width, count), BF16),
            pltpu.VMEM((HEADS, 4 * LANES), F32),
            pltpu.SemaphoreType.DMA((n,)),
            pltpu.SemaphoreType.DMA((n,)),
            pltpu.SemaphoreType.DMA,
            pltpu.SemaphoreType.DMA((2,)),
            pltpu.SemaphoreType.DMA((2,)),
            pltpu.VMEM((count, width), BF16),
            *[pltpu.VMEM((width, width), BF16)] * 4,
            pltpu.VMEM((rows, width), BF16),
            pltpu.VMEM((count, rows), BF16),
            *[pltpu.VMEM((width, count), BF16)] * 3,
            pltpu.VMEM((count, width), BF16),
            pltpu.VMEM((HEADS, count, count), BF16),
            pltpu.VMEM((width, count), BF16),
            pltpu.VMEM((count, width), F32),
            pltpu.VMEM((count, width), BF16),
            pltpu.SemaphoreType.DMA((5,)),
            pltpu.SemaphoreType.DMA((9,)),
            pltpu.SemaphoreType.DMA((HEADS // 2,)),
        ],
        compiler_params=pltpu.CompilerParams(
            collective_id=0, has_side_effects=True, vmem_limit_bytes=60 * 1024 * 1024
        ),
        name="attend",
    )(tokens, ga, wq, wk, wv, wo, rel, gf, wrt, routes, cap, cot, win, wout)
RSQRT2 = 2.0 ** (-0.5)
RSQRT2PI = 0.3989422804014327
ROWS = 256
HIDDEN = 512


def lane_mask(pad, offset):
    return iota((pad, LANES), 1) == iota((pad, LANES), 0) + offset


def expert_kernel(
    n, pad,
    xd_ref, cr_hbm, gs_ref, win_ref, wout_ref, win2_ref, wout2_ref,
    gx_ref, gg_ref, p_hbm, own_in, own_out, got_in, got_out,
    xr_ref, gr_ref, gc_ref, wi_ref, wo_ref, act_ref, gi_ref, gxs_ref, ggs_ref, sum_gx, sum_p, sum_gg, gate_ref,
    x_send, x_recv, g_send, g_recv, gx_send, gx_recv, gg_send, gg_recv, w_sem, own_sem, dw_send, dw_recv, dw_sem,
    cr_ref, p_ref, local_sem, p_sem,
):
    me = lax.axis_index("expert")
    core = lax.axis_index("ffn")
    half = win_ref.shape[1]
    parts = half // HIDDEN
    rows_all = n * pad
    barrier = greet(n, me, core, True)
    mine = pltpu.make_async_copy(cr_hbm, cr_ref, local_sem.at[0])
    mine.start()
    loads = []
    for j, (first, second) in enumerate(((win_ref, wout_ref), (win2_ref, wout2_ref))):
        for i in range(parts):
            at = j * parts + i
            cut = pl.ds(i * HIDDEN, HIDDEN)
            loads.append(pltpu.make_async_copy(first.at[:, cut], wi_ref.at[at], w_sem.at[2 * at]))
            loads.append(
                pltpu.make_async_copy(second.at[cut, :], wo_ref.at[at], w_sem.at[2 * at + 1])
            )
    for load in loads:
        load.start()

    def rows_of(e):
        return pl.ds(pl.multiple_of(e * pad, pad), pad)

    def tile_of(e):
        return pl.ds(pl.multiple_of(e * pad // LANES * LANES, LANES), LANES)

    def send(k, src, dst, sends, recvs):
        return pltpu.make_async_remote_copy(
            src_ref=src,
            dst_ref=dst,
            send_sem=sends.at[k],
            recv_sem=recvs.at[k],
            device_id=(partner(n, me, k), core),
            device_id_type=MESH,
        )

    def token_copy(k):
        target = partner(n, me, k)
        return send(k, xd_ref.at[rows_of(target)], xr_ref.at[rows_of(me)], x_send, x_recv)

    def gate_copy(k):
        target = partner(n, me, k)
        return send(k, gs_ref.at[:, tile_of(target)], gr_ref.at[me], g_send, g_recv)

    def grad_copy(k):
        target = partner(n, me, k)
        return send(k, gxs_ref.at[rows_of(target)], gx_ref.at[rows_of(me)], gx_send, gx_recv)

    def mark_copy(k):
        target = partner(n, me, k)
        return send(k, ggs_ref.at[target], gg_ref.at[me], gg_send, gg_recv)

    pl.semaphore_wait(barrier, n)

    def start_tokens(k):
        gate_copy(k).start()
        token_copy(k).start()

    each(n, start_tokens)
    held = pltpu.make_async_copy(xd_ref.at[rows_of(me)], xr_ref.at[rows_of(me)], local_sem.at[1])
    held.start()
    gr_ref[me] = gs_ref[:, tile_of(me)]
    offset = lax.rem(me * pad, LANES)
    mask = lane_mask(pad, offset)
    for load in [*loads, mine, held]:
        load.wait()
    per = ROWS // pad
    row_blocks = rows_all // ROWS

    @pl.loop(0, row_blocks)
    def _(step):
        group = step
        if n == 16:
            group = jnp.where(step == 0, 3, jnp.where(step == 1, 0, jnp.where(step == 2, 2, 1)))
        block = block_at(n, me, group, per, row_blocks)
        rows = pl.ds(pl.multiple_of(block * ROWS, ROWS), ROWS)
        columns = []
        for u in range(per):
            source = block * per + u
            k = index_between(n, source, me, group)

            @pl.when(source != me)
            def _():
                gate_copy(k).wait_recv()
                token_copy(k).wait_recv()

            line = jnp.broadcast_to(gr_ref[source][:1], (pad, LANES))
            columns.append(jnp.sum(jnp.where(mask, line, 0.0), axis=1, keepdims=True))
        gates = jnp.concatenate(columns, axis=0)
        gate_ref[...] = jnp.broadcast_to(gates, gate_ref.shape)
        gc_ref[rows, :] = (gates * cr_ref[rows, :].astype(F32)).astype(BF16)
        sum_gx[...] = jnp.zeros_like(sum_gx)
        sum_p[...] = jnp.zeros_like(sum_p)
        sum_gg[...] = jnp.zeros_like(sum_gg)

        @pl.loop(0, 2 * parts, unroll=2 * parts)
        def _(i):
            inner = dot(xr_ref[rows, :], wi_ref[i])
            raw = dot(cr_ref[rows, :], wo_ref[i], 1, 1)
            normal = 0.5 * (1.0 + lax.erf(inner * RSQRT2))
            density = jnp.exp(-0.5 * inner * inner) * RSQRT2PI
            active = (inner * normal).astype(BF16)
            act_ref[i, rows, :] = active
            weighed = active.astype(F32) * raw
            folded = weighed[:, :LANES]
            for c in range(1, HIDDEN // LANES):
                folded = folded + weighed[:, c * LANES : (c + 1) * LANES]
            sum_gg[...] += folded
            grad = (gate_ref[:, :1] * raw * (normal + inner * density)).astype(BF16)
            gi_ref[i, rows, :] = grad
            sum_gx[...] += dot(grad, wi_ref[i], 1, 1)
            sum_p[...] += dot(active, wo_ref[i])

        gxs_ref[rows, :] = sum_gx[...].astype(BF16)
        p_ref[rows, :] = sum_p[...].astype(BF16)
        pltpu.make_async_copy(p_ref.at[rows], p_hbm.at[rows], p_sem.at[block]).start()
        marks = jnp.sum(sum_gg[...], axis=1, keepdims=True)
        for u in range(per):
            source = block * per + u
            k = index_between(n, me, source, group)
            line = jnp.sum(
                jnp.where(mask, marks[u * pad : (u + 1) * pad], 0.0), axis=0, keepdims=True
            )
            ggs_ref[source] = jnp.broadcast_to(line, (8, LANES))

            @pl.when(source != me)
            def _():
                mark_copy(k).start()
                grad_copy(k).start()

    own = pltpu.make_async_copy(gxs_ref.at[rows_of(me)], gx_ref.at[rows_of(me)], own_sem)
    own.start()
    gg_ref[me] = ggs_ref[me]

    def wait_sent(k):
        token_copy(k).wait_send()
        gate_copy(k).wait_send()

    each(n, wait_sent)

    moves = []
    for j in (1, 0):
        for i in range(parts):
            at = j * parts + i
            cut = pl.ds(i * HIDDEN, HIDDEN)
            wi_ref[at] = dot(xr_ref[...], gi_ref[at], 0, 0).astype(BF16)
            wo_ref[at] = dot(act_ref[at], gc_ref[...], 0, 0).astype(BF16)
            for q, (src, dst) in enumerate(
                (
                    (wi_ref.at[at], (got_in if j else own_in).at[:, cut]),
                    (wo_ref.at[at], (got_out if j else own_out).at[cut, :]),
                )
            ):
                if j:
                    moves.append(
                        pltpu.make_async_remote_copy(
                            src_ref=src,
                            dst_ref=dst,
                            send_sem=dw_send.at[2 * i + q],
                            recv_sem=dw_recv.at[2 * i + q],
                            device_id=(me, 1 - core),
                            device_id_type=MESH,
                        )
                    )
                else:
                    moves.append(pltpu.make_async_copy(src, dst, dw_sem.at[2 * i + q]))
                moves[-1].start()
    for move in moves:
        move.wait()

    @pl.loop(0, row_blocks)
    def _(block):
        rows = pl.ds(pl.multiple_of(block * ROWS, ROWS), ROWS)
        pltpu.make_async_copy(p_ref.at[rows], p_hbm.at[rows], p_sem.at[block]).wait()

    own.wait()

    def finish(k):
        mark_copy(k).wait()
        grad_copy(k).wait()

    each(n, finish)


def run_experts(n, pad, xd, cr, gs, win, wout, win2, wout2):
    rows, width = xd.shape
    half = win.shape[1]
    parts = half // HIDDEN
    vmem = pl.BlockSpec(memory_space=pltpu.VMEM)
    anywhere = pl.BlockSpec(memory_space=pl.ANY)
    shapes = (
        ((rows, width), BF16, anywhere),
        ((n, 8, LANES), F32, vmem),
        ((rows, width), BF16, anywhere),
        ((width, half), BF16, anywhere),
        ((half, width), BF16, anywhere),
        ((width, half), BF16, anywhere),
        ((half, width), BF16, anywhere),
    )
    return pl.pallas_call(
        functools.partial(expert_kernel, n, pad),
        out_shape=[jax.ShapeDtypeStruct(shape, dtype) for shape, dtype, _ in shapes],
        in_specs=[anywhere, anywhere, vmem] + [anywhere] * 4,
        out_specs=[space for _, _, space in shapes],
        scratch_shapes=[
            pltpu.VMEM((rows, width), BF16),
            pltpu.VMEM((n, 8, LANES), F32),
            pltpu.VMEM((rows, width), BF16),
            pltpu.VMEM((2 * parts, width, HIDDEN), BF16),
            pltpu.VMEM((2 * parts, HIDDEN, width), BF16),
            pltpu.VMEM((2 * parts, rows, HIDDEN), BF16),
            pltpu.VMEM((2 * parts, rows, HIDDEN), BF16),
            pltpu.VMEM((rows, width), BF16),
            pltpu.VMEM((n, 8, LANES), F32),
            pltpu.VMEM((ROWS, width), F32),
            pltpu.VMEM((ROWS, width), F32),
            pltpu.VMEM((ROWS, LANES), F32),
            pltpu.VMEM((ROWS, LANES), F32),
        ]
        + [pltpu.SemaphoreType.DMA((n,))] * 8
        + [
            pltpu.SemaphoreType.DMA((4 * parts,)),
            pltpu.SemaphoreType.DMA,
            pltpu.SemaphoreType.DMA((2 * parts,)),
            pltpu.SemaphoreType.DMA((2 * parts,)),
            pltpu.SemaphoreType.DMA((2 * parts,)),
            pltpu.VMEM((rows, width), BF16),
            pltpu.VMEM((rows, width), BF16),
            pltpu.SemaphoreType.DMA((2,)),
            pltpu.SemaphoreType.DMA((rows // ROWS,)),
        ],
        compiler_params=pltpu.CompilerParams(
            collective_id=1, has_side_effects=True, vmem_limit_bytes=60 * 1024 * 1024
        ),
        name="experts",
    )(xd, cr, gs, win, wout, win2, wout2)
def unit_rows(n, rows):
    return -(-rows // (n * 16)) * 16


def reduce_rows(n, width):
    return [n * unit_rows(n, 3 * width)] * 4 + [n * unit_rows(n, 3 * n + 32)]


def reduce_shapes(n, width):
    stages = n.bit_length() - 1
    scratch = []
    for rows in reduce_rows(n, width):
        scratch.append(pltpu.VMEM((rows, LANES), BF16))
        scratch += [pltpu.VMEM((rows >> (s + 1), LANES), BF16) for s in range(stages)]
    return scratch + [pltpu.SemaphoreType.DMA((5, 2 * stages + 2))] * 2


def reduce_peer(me, core, s):
    distance = (1 + core, 2 - core)[s] if s < 2 else 2**s
    side = lax.rem(me // distance, 2)
    return me + distance * (1 - 2 * side), side


def reduce_steps(n, me, core, j, part, arrived, halves, total, sends, recvs, finish):
    stages = n.bit_length() - 1
    unit = part.shape[1] // n
    sides, peers, starts = [], [], [0]
    for s in range(stages):
        peer, side = reduce_peer(me, core, s)
        peers.append(peer)
        sides.append(side)
        starts.append(starts[-1] + side * (n >> (s + 1)))

    def region(start, units):
        return pl.ds(pl.multiple_of(start * unit, unit), units * unit)

    def copy(step, src, dst, device):
        return pltpu.make_async_remote_copy(
            src_ref=src,
            dst_ref=dst,
            send_sem=sends.at[j, step],
            recv_sem=recvs.at[j, step],
            device_id=device,
            device_id_type=MESH,
        )

    def transfer(step):
        if step == 0:
            return copy(step, part.at[1 - core], arrived, (me, 1 - core))
        if step <= stages:
            s = step - 1
            size = n >> (s + 1)
            away = starts[s] + (1 - sides[s]) * size
            return copy(step, part.at[core, region(away, size)], halves[s], (peers[s], core))
        if step <= 2 * stages:
            s = 2 * stages - step
            held = total.at[core, region(starts[s + 1], n >> (s + 1))]
            return copy(step, held, held, (peers[s], core))
        return copy(step, total.at[core], total.at[core], (me, 1 - core))

    def add(step):
        if step == 0:
            part[core] = (part[core].astype(F32) + arrived[...].astype(F32)).astype(BF16)
        elif step <= stages:
            s = step - 1
            mine = region(starts[s + 1], n >> (s + 1))
            summed = (part[core, mine, :].astype(F32) + halves[s][...].astype(F32)).astype(BF16)
            if step == stages:
                total[core, mine, :] = summed
            else:
                part[core, mine, :] = summed

    last = 2 * stages + 1

    def run(step):
        if step > 0:
            transfer(step - 1).wait_recv()
            add(step - 1)
        if step <= last:
            transfer(step).start()
        else:
            finish(j)
            for done in range(last + 1):
                transfer(done).wait_send()

    return [functools.partial(run, step) for step in range(last + 2)]


def reducers(n, me, core, parts, totals, scratch, finish):
    stages = n.bit_length() - 1
    size = stages + 1
    sends, recvs = scratch[-2:]
    return [
        reduce_steps(
            n, me, core, j, parts[j], scratch[j * size],
            scratch[j * size + 1 : (j + 1) * size], totals[j], sends, recvs, finish,
        )
        for j in range(5)
    ]


def unroll_band(band):
    wide = band.shape[1]
    folded = band[:8]
    for g in range(1, band.shape[0] // 8):
        folded = folded + pltpu.roll(band[8 * g : 8 * g + 8], wide - 8 * g, 1)
    line = folded[:1]
    for s in range(1, 8):
        line = line + pltpu.roll(folded, wide - s, 1)[s : s + 1]
    return line


PLAN = (
    (0,),
    ((), (), (), (), (), ()),
    ((1, 0), (2, 1, 0), (3, 2, 1, 0)),
    (0, 1, 2, 3),
    (0, 1, 2, 3, 4),
)


def back_kernel(
    n, pad,
    tok_hbm, ga_ref, wq_hbm, wk_hbm, wv_hbm, wo_hbm, gf_ref, wrt_ref, routes_ref, cot_hbm, st_hbm, gx_hbm, gg_ref, p_ref,
    nat_hbm, qt_hbm, kt_hbm, v_hbm, probs_hbm, mixt_hbm, hid_hbm, nf_hbm, pr_ref, gcol_ref,
    out_hbm, dx_hbm, total0_hbm, totals_hbm, total4_hbm,
    got_ref, probs_ref, gmt_ref, gqt_ref, gkt_ref, gvt_ref, lines_ref,
    send_sem, recv_sem, probs_sem, own_sem, part0, part1, part2, part3, part4,
    tok_ref, wq_ref, wk_ref, wv_ref, wo_ref, cot_ref, st_ref, gx_ref, nat_ref, qt_ref, kt_ref, v_ref, mixt_ref, hid_ref, nf_ref,
    out_ref, dx_ref, total0, totals, total4, load_sem, save_sem, *reduce_scratch,
):
    me = lax.axis_index("expert")
    core = lax.axis_index("ffn")
    count, width = tok_ref.shape
    rows_all = n * pad
    barrier = greet(n, me, core, True)
    need = fetch(
        load_sem,
        (st_hbm, st_ref), (gx_hbm, gx_ref), (nf_hbm, nf_ref), (hid_hbm, hid_ref), (cot_hbm, cot_ref), (mixt_hbm, mixt_ref),
        (wo_hbm, wo_ref), (v_hbm, v_ref), (kt_hbm, kt_ref), (qt_hbm, qt_ref), (nat_hbm, nat_ref), (wq_hbm, wq_ref),
        (wk_hbm, wk_ref), (wv_hbm, wv_ref), (tok_hbm, tok_ref),
    )

    def load(pair):
        return pltpu.make_async_copy(
            probs_hbm.at[pl.ds(2 * pair, 2)], probs_ref.at[pair % 2], probs_sem.at[pair % 2]
        )

    load(0).start()
    load(1).start()

    def rows_of(e):
        return pl.ds(pl.multiple_of(e * pad, pad), pad)

    def copy(k):
        target = partner(n, me, k)
        return pltpu.make_async_remote_copy(
            src_ref=p_ref.at[rows_of(target)],
            dst_ref=got_ref.at[rows_of(me)],
            send_sem=send_sem.at[k],
            recv_sem=recv_sem.at[k],
            device_id=(target, core),
            device_id_type=MESH,
        )

    pl.semaphore_wait(barrier, n)
    each(n, lambda k: copy(k).start())
    own = pltpu.make_async_copy(p_ref.at[rows_of(me)], got_ref.at[rows_of(me)], own_sem)
    own.start()
    parts = (part0, part1, part2, part3, part4)
    queue = reducers(
        n, me, core, parts, [total0, totals.at[0], totals.at[1], totals.at[2], total4], reduce_scratch,
        lambda j: kept[j].start(),
    )
    done = [0] * 5
    kept = [pltpu.make_async_copy(total0, total0_hbm, save_sem.at[0])]
    for g in range(3):
        kept.append(pltpu.make_async_copy(totals.at[g], totals_hbm.at[g], save_sem.at[g + 1]))
    kept.append(pltpu.make_async_copy(total4, total4_hbm, save_sem.at[4]))
    kept.append(pltpu.make_async_copy(dx_ref, dx_hbm, save_sem.at[5]))
    kept.append(pltpu.make_async_copy(out_ref, out_hbm, save_sem.at[6]))

    def tick(*chosen):
        for j in chosen:
            if done[j] < len(queue[j]):
                queue[j][done[j]]()
                done[j] += 1

    base = 3 * width
    for part, filled in zip(parts, [base] * 4 + [3 * n + 32]):
        if part.shape[1] > filled:
            part[:, filled:, :] = jnp.zeros((2, part.shape[1] - filled, LANES), BF16)

    share = LANES // pad
    tiles = []
    for t in range(n // share):
        tile = gg_ref[t * share][:1]
        for u in range(1, share):
            tile = tile + gg_ref[t * share + u][:1]
        tiles.append(tile)
    marks = jnp.concatenate(tiles, axis=1)
    need(0)
    grad_gate = jnp.sum(dot(pieces(marks), st_ref[...], 1, 1), axis=0, keepdims=True)
    chosen = (iota((n, count), 0) == routes_ref[...]).astype(F32)
    router = pr_ref[...]
    grad_probs = chosen * grad_gate
    grad_logits = router * (grad_probs - jnp.sum(router * grad_probs, axis=0, keepdims=True))
    grad_logits = grad_logits.astype(BF16)
    need(1, 2)
    grad_router = dot(nf_ref[...], grad_logits, 0, 1).T
    grad_nf = dot(st_ref[...], gx_ref[...]) + dot(grad_logits, wrt_ref[...], 0, 0)
    need(3, 4)
    hidden = hid_ref[...]
    scale = lax.rsqrt(jnp.mean(hidden * hidden, axis=-1, keepdims=True) + EPSILON)
    weighted = grad_nf * gf_ref[...][None]
    grad_gain_ffn = jnp.sum(grad_nf * hidden * scale, axis=0, keepdims=True)
    inner = jnp.mean(weighted * hidden, axis=-1, keepdims=True)
    grad_hidden = (
        cot_ref[...].astype(F32) + scale * weighted - hidden * (scale * scale * scale * inner)
    )
    dx_ref[...] = grad_hidden
    branch = grad_hidden.astype(BF16)
    need(5)
    for t in range(width // LANES):
        cut = slice(t * LANES, (t + 1) * LANES)
        rows = slice(t % 3 * width, (t % 3 + 1) * width)
        part0[t // 3, rows, :] = dot(mixt_ref[...], branch[:, cut]).astype(BF16)
    tick(*PLAN[0])
    need(6)
    gmt_ref[...] = dot(wo_ref[...], branch, 1, 1).astype(BF16)
    need(7, 8, 9)
    lines_ref[...] = jnp.zeros_like(lines_ref)
    lower_half = iota((LANES, count), 0) < HEAD_DIM
    blocks = count // LANES
    place = iota((1, 4 * LANES), 1)

    def run_pair(pair):
        load(pair).wait()
        lanes = pl.ds(pair * LANES, LANES)
        both = gmt_ref[lanes, :]
        for sub in range(2):
            head = 2 * pair + sub
            mask = lower_half if sub == 0 else jnp.logical_not(lower_half)
            chunk = jnp.where(mask, both, jnp.zeros_like(both))
            features = pl.ds(head * HEAD_DIM, HEAD_DIM)
            grad_mixed = gmt_ref[features, :]
            delta = jnp.sum(
                grad_mixed.astype(F32) * mixt_ref[features, :].astype(F32), axis=0, keepdims=True
            )
            probs = probs_ref[pair % 2, sub]
            grad_probs = dot(v_ref[:, lanes], chunk)
            scores = probs.astype(F32) * (grad_probs - delta)
            low = scores.astype(BF16)
            gqt_ref[features, :] = dot(kt_ref[features, :], low).astype(BF16)
            gkt_ref[features, :] = dot(qt_ref[features, :], low, 1, 1).astype(BF16)
            gvt_ref[features, :] = dot(grad_mixed, probs, 1, 1).astype(BF16)
            near = {0: None, -1: None, 1: None}
            far = {-1: None, 1: None}
            for row in range(blocks):
                for col in range(blocks):
                    block = scores[
                        row * LANES : (row + 1) * LANES, col * LANES : (col + 1) * LANES
                    ]
                    gap = row - col
                    if gap in near:
                        near[gap] = block if near[gap] is None else near[gap] + block
                    else:
                        side = 1 if gap > 0 else -1
                        far[side] = block if far[side] is None else far[side] + block
            band = jnp.concatenate([near[0], near[-1], jnp.zeros_like(near[0]), near[1]], axis=1)
            line = unroll_band(band)
            for side, lane in ((-1, 255), (1, 257)):
                total = jnp.sum(jnp.sum(far[side], axis=0, keepdims=True), axis=1, keepdims=True)
                line = line + jnp.where(place == lane, total, 0.0)
            lines_ref[pl.ds(head, 1), :] = line
        if pair + 2 < HEADS // 2:
            load(pair + 2).start()

    for group, part in enumerate((part1, part2, part3)):
        for pair in (2 * group, 2 * group + 1):
            run_pair(pair)
            tick(*PLAN[1][pair])
        if group == 0:
            need(10)
        for i, grad in enumerate((gqt_ref, gkt_ref, gvt_ref)):
            columns = grad[group * 2 * LANES : (group + 1) * 2 * LANES, :]
            made = dot(nat_ref[...], columns, 1, 1).astype(BF16)
            for c in range(2):
                part[c, i * width : (i + 1) * width, :] = made[:, c * LANES : (c + 1) * LANES]
        tick(*PLAN[2][group])
    need(11, 12, 13, 14)
    grad_na = (
        dot(wq_ref[...], gqt_ref[...])
        + dot(wk_ref[...], gkt_ref[...])
        + dot(wv_ref[...], gvt_ref[...])
    ).T
    x = tok_ref[...].astype(F32)
    scale = lax.rsqrt(jnp.mean(x * x, axis=-1, keepdims=True) + EPSILON)
    weighted = grad_na * ga_ref[...][None]
    grad_gain_attn = jnp.sum(grad_na * x * scale, axis=0, keepdims=True)
    inner = jnp.mean(weighted * x, axis=-1, keepdims=True)
    tick(*PLAN[3])
    dx_ref[...] = dx_ref[...] + scale * weighted - x * (scale * scale * scale * inner)
    kept[5].start()
    grad_bias = dot(band_onehot(), lines_ref[...], 1, 1, HIGH)
    gains = jnp.concatenate([grad_gain_attn, grad_gain_ffn, jnp.zeros((14, width), F32)], axis=0)
    for c in range(2):
        for t in range(3):
            cut = slice((3 * c + t) * LANES, (3 * c + t + 1) * LANES)
            part4[c, t * n : (t + 1) * n, :] = grad_router[:, cut].astype(BF16)
        rows = slice(3 * n, 3 * n + 16)
        sums = [gains[:, (3 * c + t) * LANES : (3 * c + t + 1) * LANES][:2] for t in range(3)]
        part4[c, rows, :] = jnp.concatenate(sums + [jnp.zeros((10, LANES), F32)], axis=0).astype(BF16)
        rows = slice(3 * n + 16, 3 * n + 32)
        wide = jnp.concatenate(
            [grad_bias[16 * c : 16 * c + 16], jnp.zeros((16, LANES - 16), F32)], axis=1
        )
        part4[c, rows, :] = wide.astype(BF16)
    tick(*PLAN[4])
    own.wait()
    each(n, lambda k: copy(k).wait())
    picked = dot(st_ref[...], got_ref[...])
    out_ref[...] = (hid_ref[...] + gcol_ref[:, :1] * picked).astype(BF16)
    kept[6].start()
    while any(done[j] < len(queue[j]) for j in range(5)):
        tick(3, 2, 4, 1, 0)
    for copied in kept:
        copied.wait()


def run_back(n, pad, tokens, *rest):
    count, width = tokens.shape
    rows = n * pad
    vmem = pl.BlockSpec(memory_space=pltpu.VMEM)
    anywhere = pl.BlockSpec(memory_space=pl.ANY)
    shapes = (
        ((count, width), BF16, anywhere),
        ((count, width), F32, anywhere),
        ((2, reduce_rows(n, width)[0], LANES), BF16, anywhere),
        ((3, 2, reduce_rows(n, width)[0], LANES), BF16, anywhere),
        ((2, reduce_rows(n, width)[4], LANES), BF16, anywhere),
    )
    return pl.pallas_call(
        functools.partial(back_kernel, n, pad),
        out_shape=[jax.ShapeDtypeStruct(shape, dtype) for shape, dtype, _ in shapes],
        in_specs=[anywhere, vmem]
        + [anywhere] * 4
        + [vmem] * 3
        + [anywhere] * 3
        + [vmem]
        + [anywhere] * 9
        + [vmem] * 2,
        out_specs=[space for _, _, space in shapes],
        scratch_shapes=[
            pltpu.VMEM((rows, width), BF16),
            pltpu.VMEM((2, 2, count, count), BF16),
            pltpu.VMEM((width, count), BF16),
            pltpu.VMEM((width, count), BF16),
            pltpu.VMEM((width, count), BF16),
            pltpu.VMEM((width, count), BF16),
            pltpu.VMEM((16, 4 * LANES), F32),
            pltpu.SemaphoreType.DMA((n,)),
            pltpu.SemaphoreType.DMA((n,)),
            pltpu.SemaphoreType.DMA((2,)),
            pltpu.SemaphoreType.DMA,
            *(pltpu.VMEM((2, part, LANES), BF16) for part in reduce_rows(n, width)),
            pltpu.VMEM((count, width), BF16),
            *[pltpu.VMEM((width, width), BF16)] * 4,
            pltpu.VMEM((count, width), BF16),
            pltpu.VMEM((count, rows), BF16),
            pltpu.VMEM((rows, width), BF16),
            *[pltpu.VMEM((width, count), BF16)] * 3,
            pltpu.VMEM((count, width), BF16),
            pltpu.VMEM((width, count), BF16),
            pltpu.VMEM((count, width), F32),
            pltpu.VMEM((count, width), BF16),
            *[pltpu.VMEM(shape, dtype) for shape, dtype, _ in shapes],
            pltpu.SemaphoreType.DMA((15,)),
            pltpu.SemaphoreType.DMA((7,)),
            *reduce_shapes(n, width),
        ],
        compiler_params=pltpu.CompilerParams(
            collective_id=2, has_side_effects=True, vmem_limit_bytes=63 * 1024 * 1024
        ),
        name="attend_back",
    )(tokens, *rest)


def finish_kernel(
    n,
    first0, first1, first2, q_ref, k_ref, v_ref, small_ref, own_in, got_in, own_out, got_out, out_ref, dx_ref, rms_ref,
    go_ref, gq_ref, gk_ref, gv_ref, gi_ref, gw_ref, router_ref, gain_a, gain_f, bias_ref, output_ref, grad_ref, roots_ref,
):
    for t in range(6):
        cut = slice(t * LANES, (t + 1) * LANES)
        go_ref[:, cut] = (first0, first1, first2)[t % 3][t // 3].astype(F32)
        for made, grad in ((gq_ref, q_ref), (gk_ref, k_ref), (gv_ref, v_ref)):
            made[:, cut] = grad[t // 2, t % 2].astype(F32)
    gi_ref[...] = own_in[...].astype(F32) + got_in[...].astype(F32)
    gw_ref[...] = own_out[...].astype(F32) + got_out[...].astype(F32)
    output_ref[...] = out_ref[...]
    grad_ref[...] = dx_ref[...]

    @pl.when(pl.program_id(0) == 0)
    def _():
        roots_ref[...] = rms_ref[3:5, :]
        small = small_ref[...].astype(F32)
        for t in range(6):
            c, at = t // 3, t % 3
            cut = slice(t * LANES, (t + 1) * LANES)
            router_ref[:, cut] = small[c, at * n : (at + 1) * n]
            gain_a[cut] = small[c, 3 * n + 2 * at]
            gain_f[cut] = small[c, 3 * n + 2 * at + 1]
        bias = jnp.concatenate([small[c, 3 * n + 16 : 3 * n + 32] for c in range(2)], axis=0)
        bias_ref[...] = bias.T[:HEADS]


def run_finish(n, first, groups, smalls, own_in, got_in, own_out, got_out, out, dx, rms):
    width, half = own_in.shape
    count = out.shape[0]
    steps = width // LANES
    whole = lambda *shape: pl.BlockSpec(shape, lambda t: (0,) * len(shape))
    by_rows = lambda rows, columns: pl.BlockSpec((rows, columns), lambda t: (t, 0))
    out_part = lambda i: pl.BlockSpec((2, LANES, LANES), lambda t: (0, i * steps + t, 0))
    weight = lambda i: pl.BlockSpec((3, 2, LANES, LANES), lambda t: (0, 0, i * steps + t, 0))
    grad_shape = jax.ShapeDtypeStruct((width, width), F32)
    some = pl.BlockSpec((count // 4, width), lambda t: (jnp.minimum(t, 3), 0))
    rows_in, rows_out = by_rows(LANES, half), by_rows(half // steps, width)
    return pl.pallas_call(
        functools.partial(finish_kernel, n),
        grid=(steps,),
        out_shape=[
            grad_shape,
            grad_shape,
            grad_shape,
            grad_shape,
            jax.ShapeDtypeStruct((width, half), F32),
            jax.ShapeDtypeStruct((half, width), F32),
            jax.ShapeDtypeStruct((n, width), F32),
            jax.ShapeDtypeStruct((width,), F32),
            jax.ShapeDtypeStruct((width,), F32),
            jax.ShapeDtypeStruct((HEADS, BUCKETS), F32),
            jax.ShapeDtypeStruct((count, width), BF16),
            jax.ShapeDtypeStruct((count, width), F32),
            jax.ShapeDtypeStruct((2, count), F32),
        ],
        in_specs=[out_part(i) for i in range(3)]
        + [weight(i) for i in range(3)]
        + [whole(*smalls.shape), rows_in, rows_in, rows_out, rows_out, some, some, whole(8, count)],
        out_specs=[by_rows(LANES, width)] * 4
        + [rows_in, rows_out]
        + [whole(n, width), whole(width), whole(width), whole(HEADS, BUCKETS)]
        + [some, some, whole(2, count)],
        compiler_params=pltpu.CompilerParams(vmem_limit_bytes=60 * 1024 * 1024),
        name="finish",
    )(first, first, first, groups, groups, groups, smalls, own_in, got_in, own_out, got_out, out, dx, rms)


def per_device(
    tokens, gain_attn, query_weight, key_weight, value_weight, out_weight, rel_bias, gain_ffn, router_weight,
    expert_in, expert_out, routes, capacity, cotangent,
):
    count, width = tokens.shape
    n = lax.axis_size("expert")
    experts = router_weight.shape[1]
    assert experts == n and count == SEQ
    slots = 2 * count // experts
    pad = -(-slots // 16) * 16
    router_rows = router_weight.T
    routes = routes.reshape(1, count)
    (
        cots, in_other, out_other, dispatched, gates, slots_t, normed_t, query_t, key_t, values, probs, mixed_t,
        hidden, normed_ffn, router_t, gate_col, roots,
    ) = attend(
        n, slots, pad, tokens, gain_attn, query_weight, key_weight, value_weight, out_weight, rel_bias.T, gain_ffn,
        router_rows, routes, capacity, cotangent, expert_in[0], expert_out[0],
    )
    grad_rows, marks, produced, own_in, own_out, got_in, got_out = run_experts(
        n, pad, dispatched, cots, gates, expert_in[0], expert_out[0], in_other, out_other
    )
    output, input_grad, first, groups, smalls = run_back(
        n, pad, tokens, gain_attn, query_weight, key_weight, value_weight, out_weight, gain_ffn, router_rows, routes,
        cotangent, slots_t, grad_rows, marks, produced, normed_t, query_t, key_t, values, probs, mixed_t, hidden,
        normed_ffn, router_t, gate_col,
    )
    (
        grad_out, grad_query, grad_key, grad_value, grad_in, grad_expert, grad_router, grad_gain_attn, grad_gain_ffn,
        grad_bias, output, input_grad, rms_values,
    ) = run_finish(n, first, groups, smalls, own_in, got_in, own_out, got_out, output, input_grad, roots)
    return (
        output,
        input_grad,
        grad_gain_attn,
        grad_query,
        grad_key,
        grad_value,
        grad_out,
        grad_bias.T,
        grad_gain_ffn,
        grad_router.T,
        grad_in[None],
        grad_expert[None],
        rms_values,
    )


def solution(mesh):
    placed = (
        P(("expert", "ffn"), None),
        P(),
        P(),
        P(),
        P(),
        P(),
        P(),
        P(),
        P(),
        P("expert", None, "ffn"),
        P("expert", "ffn", None),
        P(("expert", "ffn"), None),
        P(("expert", "ffn")),
        P(("expert", "ffn"), None),
    )
    return jax.shard_map(
        per_device,
        mesh=mesh,
        in_specs=placed,
        out_specs=(
            P(("expert", "ffn"), None),
            P(("expert", "ffn"), None),
            P(),
            P(),
            P(),
            P(),
            P(),
            P(),
            P(),
            P(),
            P("expert", None, "ffn"),
            P("expert", "ffn", None),
            P(None, ("expert", "ffn")),
        ),
        check_vma=False,
    )
```

```python
import functools
import jax
import jax.numpy as jnp
from jax import lax
from jax.experimental import pallas as pl
from jax.experimental.pallas import tpu as pltpu
from jax.sharding import PartitionSpec as P

HEADS = 12
HEAD_DIM = 64
BUCKETS = 32
SEQ = 512
EPSILON = 1e-06
THRESHOLDS = (12, 16, 23, 32, 46, 64, 91)
HIGH = lax.Precision.HIGHEST
F32 = jnp.float32
BF16 = jnp.bfloat16
MESH = pl.DeviceIdType.MESH
LANES = 128


def dot(a, b, ca=1, cb=0, precision=None):
    return lax.dot_general(
        a, b, (((ca,), (cb,)), ((), ())), precision=precision, preferred_element_type=F32
    )


def iota(shape, dim):
    return lax.broadcasted_iota(jnp.int32, shape, dim)


def div(a, b):
    return a // b if isinstance(a, int) else lax.div(a, jnp.int32(b))


def rem(a, b):
    return a % b if isinstance(a, int) else lax.rem(a, jnp.int32(b))


def block_at(n, me, step, per, blocks):
    if n != 16:
        return rem(div(me, per) + step, blocks)
    layer = div(me, 4)
    low = rem(rem(layer, 2) + div(step + 1, 2), 2)
    return 2 * rem(div(layer, 2) + 1 - div(step, 2), 2) + low


def partner(n, me, k):
    if n != 16:
        return rem(me + k, n)
    return 4 * block_at(n, me, div(k, 4), 4, 4) + rem(rem(me, 4) + rem(k, 4), 4)


def index_between(n, sender, receiver, step):
    if n != 16:
        return rem(receiver - sender + n, n)
    return 4 * step + rem(rem(receiver, 4) - rem(sender, 4) + 4, 4)


def each(n, body):
    if n == 16:
        for k in range(n):
            if k != 12:
                body(k)
    else:

        def step(k, carry):
            body(k)
            return carry

        lax.fori_loop(1, n, step, 0)


def greet(n, me, core, sibling):
    barrier = pltpu.get_barrier_semaphore()

    def signal(k):
        pl.semaphore_signal(
            barrier, inc=1, device_id=(partner(n, me, k), core), device_id_type=MESH
        )

    each(n, signal)
    if sibling:
        pl.semaphore_signal(barrier, inc=1, device_id=(me, 1 - core), device_id_type=MESH)
    return barrier


def band_onehot():
    place = iota((BUCKETS, 4 * LANES), 1)
    offset = jnp.where(place < 2 * LANES, -place, 4 * LANES - place)
    distance = jnp.abs(offset)
    larger = jnp.full(distance.shape, 8, jnp.int32)
    for limit in THRESHOLDS:
        larger = larger + (distance >= limit).astype(jnp.int32)
    bucket = jnp.where(distance < 8, distance, larger) + jnp.where(offset > 0, 16, 0)
    return (bucket == iota(bucket.shape, 0)).astype(F32)


def pieces(row):
    high = row.astype(BF16)
    rest = row - high.astype(F32)
    middle = rest.astype(BF16)
    low = (rest - middle.astype(F32)).astype(BF16)
    filler = jnp.zeros((5, row.shape[1]), BF16)
    return jnp.concatenate([high, middle, low, filler], axis=0)


def fetch(sem, *pairs):
    copies = [pltpu.make_async_copy(src, dst, sem.at[i]) for i, (src, dst) in enumerate(pairs)]
    for copy in copies:
        copy.start()

    def need(*which):
        for i in which:
            copies[i].wait()

    return need


def attend_kernel(
    n, slots, pad,
    tok_hbm, ga_ref, wq_hbm, wk_hbm, wv_hbm, wo_hbm, rel_ref, gf_ref, wrt_ref, routes_ref, cap_ref, cot_ref, win_ref, wout_ref,
    cr_ref, wi2_ref, wo2_ref, xd_hbm, gs_ref, st_hbm, nat_hbm, qt_hbm, kt_hbm, v_hbm, p_hbm, mixt_hbm, hid_hbm, nf_hbm, pr_ref, gcol_ref, rms_ref,
    cd_ref, s_ref, k_ref, vt_ref, band_ref, send_sem, recv_sem, own_sem, w_send, w_recv,
    tok_ref, wq_ref, wk_ref, wv_ref, wo_ref, xd_ref, st_ref, nat_ref, qt_ref, kt_ref, v_ref, p_ref, mixt_ref, hid_ref, nf_ref,
    load_sem, save_sem, probs_sem,
):
    me = lax.axis_index("expert")
    core = lax.axis_index("ffn")
    count, width = tok_ref.shape
    rows_all = n * pad
    barrier = greet(n, me, core, True)
    need = fetch(
        load_sem,
        (tok_hbm, tok_ref), (wq_hbm, wq_ref), (wk_hbm, wk_ref), (wv_hbm, wv_ref), (wo_hbm, wo_ref),
    )
    saves = []

    def save(src, dst):
        saves.append(pltpu.make_async_copy(src, dst, save_sem.at[len(saves)]))
        saves[-1].start()


    routes = routes_ref[...]
    chosen = (iota((n, count), 0) == routes).astype(F32)
    upper = (iota((count, count), 0) < iota((count, count), 1)).astype(F32).astype(BF16)
    earlier = dot(chosen.astype(BF16), upper)
    position = jnp.sum(earlier * chosen, axis=0, keepdims=True)
    live = (cap_ref[0] * count // n).astype(F32)
    slot = jnp.where(position < live, routes * pad + position.astype(jnp.int32), rows_all)

    @pl.loop(0, rows_all // 256)
    def _(block):
        start = pl.multiple_of(block * 256, 256)
        hot = (iota((256, count), 0) + start == slot).astype(F32).astype(BF16)
        s_ref[pl.ds(start, 256), :] = hot
        cd_ref[pl.ds(start, 256), :] = dot(hot, cot_ref[...]).astype(BF16)

    pl.semaphore_wait(barrier, n)

    def rows_of(e):
        return pl.ds(pl.multiple_of(e * pad, pad), pad)

    def copy(k):
        target = partner(n, me, k)
        return pltpu.make_async_remote_copy(
            src_ref=cd_ref.at[rows_of(target)],
            dst_ref=cr_ref.at[rows_of(me)],
            send_sem=send_sem.at[k],
            recv_sem=recv_sem.at[k],
            device_id=(target, core),
            device_id_type=MESH,
        )

    each(n, lambda k: copy(k).start())
    own = pltpu.make_async_copy(cd_ref.at[rows_of(me)], cr_ref.at[rows_of(me)], own_sem)
    own.start()
    halves = [
        pltpu.make_async_remote_copy(
            src_ref=src,
            dst_ref=dst,
            send_sem=w_send.at[i],
            recv_sem=w_recv.at[i],
            device_id=(me, 1 - core),
            device_id_type=MESH,
        )
        for i, (src, dst) in enumerate(((win_ref, wi2_ref), (wout_ref, wo2_ref)))
    ]
    for half in halves:
        half.start()

    need(0)
    x = tok_ref[...].astype(F32)
    ms1 = jnp.mean(x * x, axis=-1, keepdims=True)
    na = (x * lax.rsqrt(ms1 + EPSILON) * ga_ref[...][None]).astype(BF16)
    nat_ref[...] = na.T
    need(1)
    qt_ref[...] = dot(na, wq_ref[...]).astype(BF16).T
    need(2)
    keys = dot(na, wk_ref[...]).astype(BF16)
    k_ref[...] = keys
    kt_ref[...] = keys.T
    need(3)
    values = dot(na, wv_ref[...]).astype(BF16)
    v_ref[...] = values
    vt_ref[...] = values.T
    save(nat_ref, nat_hbm)
    save(qt_ref, qt_hbm)
    save(kt_ref, kt_hbm)
    save(v_ref, v_hbm)
    band_ref[...] = dot(rel_ref[...], band_onehot(), 1, 0, HIGH)
    lower_half = iota((LANES, count), 0) < HEAD_DIM
    blocks = count // LANES

    def save_probs(pair):
        heads = pl.ds(2 * pair, 2)
        return pltpu.make_async_copy(p_ref.at[heads], p_hbm.at[heads], probs_sem.at[pair])

    @pl.loop(0, HEADS // 2)
    def _(pair):
        lanes = pl.ds(pl.multiple_of(pair * LANES, LANES), LANES)
        both = qt_ref[lanes, :]
        for sub in range(2):
            head = 2 * pair + sub
            mask = lower_half if sub == 0 else jnp.logical_not(lower_half)
            query = jnp.where(mask, both, jnp.zeros_like(both))
            line = band_ref[pl.ds(head, 1), :]
            band = pltpu.roll(
                jnp.broadcast_to(line, (LANES, 4 * LANES)), 0, 1, stride=1, stride_axis=0
            )
            before = jnp.broadcast_to(line[:, 255:256], (LANES, LANES))
            after = jnp.broadcast_to(line[:, 257:258], (LANES, LANES))
            by_gap = {
                0: band[:, :LANES],
                -1: band[:, LANES : 2 * LANES],
                1: band[:, 3 * LANES :],
            }
            scores = []
            for row in range(blocks):
                bias = jnp.concatenate(
                    [
                        by_gap.get(row - col, after if row > col else before)
                        for col in range(blocks)
                    ],
                    axis=1,
                )
                made = dot(k_ref[row * LANES : (row + 1) * LANES, lanes], query)
                scores.append(made + bias)
            scores = jnp.concatenate(scores, axis=0)
            peak = jnp.max(scores, axis=0, keepdims=True)
            expo = jnp.exp(scores - peak)
            total = jnp.sum(expo, axis=0, keepdims=True)
            probs = (expo * (1.0 / total)).astype(BF16)
            p_ref[head] = probs
            features = pl.ds(pl.multiple_of(head * HEAD_DIM, HEAD_DIM), HEAD_DIM)
            mixt_ref[features, :] = dot(vt_ref[features, :], probs).astype(BF16)
        save_probs(pair).start()

    save(mixt_ref, mixt_hbm)
    need(4)
    hidden = tok_ref[...].astype(F32) + dot(mixt_ref[...].T, wo_ref[...])
    hid_ref[...] = hidden
    save(hid_ref, hid_hbm)
    ms2 = jnp.mean(hidden * hidden, axis=-1, keepdims=True)
    nf = (hidden * lax.rsqrt(ms2 + EPSILON) * gf_ref[...][None]).astype(BF16)
    nf_ref[...] = nf
    save(nf_ref, nf_hbm)
    logits = dot(wrt_ref[...], nf, 1, 1)
    top = jnp.max(logits, axis=0, keepdims=True)
    raised = jnp.exp(logits - top)
    router = raised / jnp.sum(raised, axis=0, keepdims=True)
    pr_ref[...] = router
    gate = jnp.sum(router * chosen, axis=0, keepdims=True)
    gcol_ref[...] = jnp.broadcast_to(gate, (LANES, count)).T
    roots = jnp.concatenate(
        [
            jnp.broadcast_to(jnp.sqrt(ms + EPSILON), (count, LANES)).T[:4]
            for ms in (ms1, ms2)
        ],
        axis=0,
    )
    rms_ref[...] = roots
    parts = pieces(gate)

    @pl.loop(0, rows_all // 256)
    def _(block):
        start = pl.multiple_of(block * 256, 256)
        hot = s_ref[pl.ds(start, 256), :]
        xd_ref[pl.ds(start, 256), :] = dot(hot, nf_ref[...]).astype(BF16)
        split = dot(parts, hot, 1, 1)
        gs_ref[:, pl.ds(start, 256)] = jnp.broadcast_to(
            jnp.sum(split, axis=0, keepdims=True), split.shape
        )
        st_ref[:, pl.ds(start, 256)] = hot.T

    save(xd_ref, xd_hbm)
    save(st_ref, st_hbm)
    for pair in range(HEADS // 2):
        save_probs(pair).wait()
    for copied in saves:
        copied.wait()
    own.wait()
    for half in halves:
        half.wait()
    each(n, lambda k: copy(k).wait())


def attend(n, slots, pad, tokens, ga, wq, wk, wv, wo, rel, gf, wrt, routes, cap, cot, win, wout):
    count, width = tokens.shape
    rows = n * pad
    half = win.shape[-1]
    vmem = pl.BlockSpec(memory_space=pltpu.VMEM)
    anywhere = pl.BlockSpec(memory_space=pl.ANY)
    smem = pl.BlockSpec(memory_space=pltpu.SMEM)
    shapes = (
        ((rows, width), BF16, anywhere),
        ((width, half), BF16, anywhere),
        ((half, width), BF16, anywhere),
        ((rows, width), BF16, anywhere),
        ((8, rows), F32, vmem),
        ((count, rows), BF16, anywhere),
        ((width, count), BF16, anywhere),
        ((width, count), BF16, anywhere),
        ((width, count), BF16, anywhere),
        ((count, width), BF16, anywhere),
        ((HEADS, count, count), BF16, anywhere),
        ((width, count), BF16, anywhere),
        ((count, width), F32, anywhere),
        ((count, width), BF16, anywhere),
        ((n, count), F32, vmem),
        ((count, LANES), F32, vmem),
        ((8, count), F32, vmem),
    )
    return pl.pallas_call(
        functools.partial(attend_kernel, n, slots, pad),
        out_shape=[jax.ShapeDtypeStruct(shape, dtype) for shape, dtype, _ in shapes],
        in_specs=[anywhere, vmem] + [anywhere] * 4 + [vmem] * 4 + [smem, vmem, anywhere, anywhere],
        out_specs=[space for _, _, space in shapes],
        scratch_shapes=[
            pltpu.VMEM((rows, width), BF16),
            pltpu.VMEM((rows, count), BF16),
            pltpu.VMEM((count, width), BF16),
            pltpu.VMEM((width, count), BF16),
            pltpu.VMEM((HEADS, 4 * LANES), F32),
            pltpu.SemaphoreType.DMA((n,)),
            pltpu.SemaphoreType.DMA((n,)),
            pltpu.SemaphoreType.DMA,
            pltpu.SemaphoreType.DMA((2,)),
            pltpu.SemaphoreType.DMA((2,)),
            pltpu.VMEM((count, width), BF16),
            *[pltpu.VMEM((width, width), BF16)] * 4,
            pltpu.VMEM((rows, width), BF16),
            pltpu.VMEM((count, rows), BF16),
            *[pltpu.VMEM((width, count), BF16)] * 3,
            pltpu.VMEM((count, width), BF16),
            pltpu.VMEM((HEADS, count, count), BF16),
            pltpu.VMEM((width, count), BF16),
            pltpu.VMEM((count, width), F32),
            pltpu.VMEM((count, width), BF16),
            pltpu.SemaphoreType.DMA((5,)),
            pltpu.SemaphoreType.DMA((9,)),
            pltpu.SemaphoreType.DMA((HEADS // 2,)),
        ],
        compiler_params=pltpu.CompilerParams(
            collective_id=0, has_side_effects=True, vmem_limit_bytes=60 * 1024 * 1024
        ),
        name="attend",
    )(tokens, ga, wq, wk, wv, wo, rel, gf, wrt, routes, cap, cot, win, wout)
RSQRT2 = 2.0 ** (-0.5)
RSQRT2PI = 0.3989422804014327
ROWS = 256
HIDDEN = 512


def lane_mask(pad, offset):
    return iota((pad, LANES), 1) == iota((pad, LANES), 0) + offset


def expert_kernel(
    n, pad,
    xd_ref, cr_hbm, gs_ref, win_ref, wout_ref, win2_ref, wout2_ref,
    gx_ref, gg_ref, p_hbm, own_in, own_out, got_in, got_out,
    xr_ref, gr_ref, gc_ref, wi_ref, wo_ref, act_ref, gi_ref, gxs_ref, ggs_ref, sum_gx, sum_p, sum_gg, gate_ref,
    x_send, x_recv, g_send, g_recv, gx_send, gx_recv, gg_send, gg_recv, w_sem, own_sem, dw_send, dw_recv, dw_sem,
    cr_ref, p_ref, local_sem, p_sem,
):
    me = lax.axis_index("expert")
    core = lax.axis_index("ffn")
    half = win_ref.shape[1]
    parts = half // HIDDEN
    rows_all = n * pad
    barrier = greet(n, me, core, True)
    mine = pltpu.make_async_copy(cr_hbm, cr_ref, local_sem.at[0])
    mine.start()
    loads = []
    for j, (first, second) in enumerate(((win_ref, wout_ref), (win2_ref, wout2_ref))):
        for i in range(parts):
            at = j * parts + i
            cut = pl.ds(i * HIDDEN, HIDDEN)
            loads.append(pltpu.make_async_copy(first.at[:, cut], wi_ref.at[at], w_sem.at[2 * at]))
            loads.append(
                pltpu.make_async_copy(second.at[cut, :], wo_ref.at[at], w_sem.at[2 * at + 1])
            )
    for load in loads:
        load.start()

    def rows_of(e):
        return pl.ds(pl.multiple_of(e * pad, pad), pad)

    def tile_of(e):
        return pl.ds(pl.multiple_of(e * pad // LANES * LANES, LANES), LANES)

    def send(k, src, dst, sends, recvs):
        return pltpu.make_async_remote_copy(
            src_ref=src,
            dst_ref=dst,
            send_sem=sends.at[k],
            recv_sem=recvs.at[k],
            device_id=(partner(n, me, k), core),
            device_id_type=MESH,
        )

    def token_copy(k):
        target = partner(n, me, k)
        return send(k, xd_ref.at[rows_of(target)], xr_ref.at[rows_of(me)], x_send, x_recv)

    def gate_copy(k):
        target = partner(n, me, k)
        return send(k, gs_ref.at[:, tile_of(target)], gr_ref.at[me], g_send, g_recv)

    def grad_copy(k):
        target = partner(n, me, k)
        return send(k, gxs_ref.at[rows_of(target)], gx_ref.at[rows_of(me)], gx_send, gx_recv)

    def mark_copy(k):
        target = partner(n, me, k)
        return send(k, ggs_ref.at[target], gg_ref.at[me], gg_send, gg_recv)

    pl.semaphore_wait(barrier, n)

    def start_tokens(k):
        gate_copy(k).start()
        token_copy(k).start()

    each(n, start_tokens)
    held = pltpu.make_async_copy(xd_ref.at[rows_of(me)], xr_ref.at[rows_of(me)], local_sem.at[1])
    held.start()
    gr_ref[me] = gs_ref[:, tile_of(me)]
    offset = lax.rem(me * pad, LANES)
    mask = lane_mask(pad, offset)
    for load in [*loads, mine, held]:
        load.wait()
    per = ROWS // pad
    row_blocks = rows_all // ROWS

    @pl.loop(0, row_blocks)
    def _(step):
        group = step
        if n == 16:
            group = jnp.where(step == 0, 3, jnp.where(step == 1, 0, jnp.where(step == 2, 2, 1)))
        block = block_at(n, me, group, per, row_blocks)
        rows = pl.ds(pl.multiple_of(block * ROWS, ROWS), ROWS)
        columns = []
        for u in range(per):
            source = block * per + u
            k = index_between(n, source, me, group)

            @pl.when(source != me)
            def _():
                gate_copy(k).wait_recv()
                token_copy(k).wait_recv()

            line = jnp.broadcast_to(gr_ref[source][:1], (pad, LANES))
            columns.append(jnp.sum(jnp.where(mask, line, 0.0), axis=1, keepdims=True))
        gates = jnp.concatenate(columns, axis=0)
        gate_ref[...] = jnp.broadcast_to(gates, gate_ref.shape)
        gc_ref[rows, :] = (gates * cr_ref[rows, :].astype(F32)).astype(BF16)
        sum_gx[...] = jnp.zeros_like(sum_gx)
        sum_p[...] = jnp.zeros_like(sum_p)
        sum_gg[...] = jnp.zeros_like(sum_gg)

        @pl.loop(0, 2 * parts, unroll=2 * parts)
        def _(i):
            inner = dot(xr_ref[rows, :], wi_ref[i])
            raw = dot(cr_ref[rows, :], wo_ref[i], 1, 1)
            normal = 0.5 * (1.0 + lax.erf(inner * RSQRT2))
            density = jnp.exp(-0.5 * inner * inner) * RSQRT2PI
            active = (inner * normal).astype(BF16)
            act_ref[i, rows, :] = active
            weighed = active.astype(F32) * raw
            folded = weighed[:, :LANES]
            for c in range(1, HIDDEN // LANES):
                folded = folded + weighed[:, c * LANES : (c + 1) * LANES]
            sum_gg[...] += folded
            grad = (gate_ref[:, :1] * raw * (normal + inner * density)).astype(BF16)
            gi_ref[i, rows, :] = grad
            sum_gx[...] += dot(grad, wi_ref[i], 1, 1)
            sum_p[...] += dot(active, wo_ref[i])

        gxs_ref[rows, :] = sum_gx[...].astype(BF16)
        p_ref[rows, :] = sum_p[...].astype(BF16)
        pltpu.make_async_copy(p_ref.at[rows], p_hbm.at[rows], p_sem.at[block]).start()
        marks = jnp.sum(sum_gg[...], axis=1, keepdims=True)
        for u in range(per):
            source = block * per + u
            k = index_between(n, me, source, group)
            line = jnp.sum(
                jnp.where(mask, marks[u * pad : (u + 1) * pad], 0.0), axis=0, keepdims=True
            )
            ggs_ref[source] = jnp.broadcast_to(line, (8, LANES))

            @pl.when(source != me)
            def _():
                mark_copy(k).start()
                grad_copy(k).start()

    own = pltpu.make_async_copy(gxs_ref.at[rows_of(me)], gx_ref.at[rows_of(me)], own_sem)
    own.start()
    gg_ref[me] = ggs_ref[me]

    def wait_sent(k):
        token_copy(k).wait_send()
        gate_copy(k).wait_send()

    each(n, wait_sent)

    moves = []
    for j in (1, 0):
        for i in range(parts):
            at = j * parts + i
            cut = pl.ds(i * HIDDEN, HIDDEN)
            wi_ref[at] = dot(xr_ref[...], gi_ref[at], 0, 0).astype(BF16)
            wo_ref[at] = dot(act_ref[at], gc_ref[...], 0, 0).astype(BF16)
            for q, (src, dst) in enumerate(
                (
                    (wi_ref.at[at], (got_in if j else own_in).at[:, cut]),
                    (wo_ref.at[at], (got_out if j else own_out).at[cut, :]),
                )
            ):
                if j:
                    moves.append(
                        pltpu.make_async_remote_copy(
                            src_ref=src,
                            dst_ref=dst,
                            send_sem=dw_send.at[2 * i + q],
                            recv_sem=dw_recv.at[2 * i + q],
                            device_id=(me, 1 - core),
                            device_id_type=MESH,
                        )
                    )
                else:
                    moves.append(pltpu.make_async_copy(src, dst, dw_sem.at[2 * i + q]))
                moves[-1].start()
    for move in moves:
        move.wait()

    @pl.loop(0, row_blocks)
    def _(block):
        rows = pl.ds(pl.multiple_of(block * ROWS, ROWS), ROWS)
        pltpu.make_async_copy(p_ref.at[rows], p_hbm.at[rows], p_sem.at[block]).wait()

    own.wait()

    def finish(k):
        mark_copy(k).wait()
        grad_copy(k).wait()

    each(n, finish)


def run_experts(n, pad, xd, cr, gs, win, wout, win2, wout2):
    rows, width = xd.shape
    half = win.shape[1]
    parts = half // HIDDEN
    vmem = pl.BlockSpec(memory_space=pltpu.VMEM)
    anywhere = pl.BlockSpec(memory_space=pl.ANY)
    shapes = (
        ((rows, width), BF16, anywhere),
        ((n, 8, LANES), F32, vmem),
        ((rows, width), BF16, anywhere),
        ((width, half), BF16, anywhere),
        ((half, width), BF16, anywhere),
        ((width, half), BF16, anywhere),
        ((half, width), BF16, anywhere),
    )
    return pl.pallas_call(
        functools.partial(expert_kernel, n, pad),
        out_shape=[jax.ShapeDtypeStruct(shape, dtype) for shape, dtype, _ in shapes],
        in_specs=[anywhere, anywhere, vmem] + [anywhere] * 4,
        out_specs=[space for _, _, space in shapes],
        scratch_shapes=[
            pltpu.VMEM((rows, width), BF16),
            pltpu.VMEM((n, 8, LANES), F32),
            pltpu.VMEM((rows, width), BF16),
            pltpu.VMEM((2 * parts, width, HIDDEN), BF16),
            pltpu.VMEM((2 * parts, HIDDEN, width), BF16),
            pltpu.VMEM((2 * parts, rows, HIDDEN), BF16),
            pltpu.VMEM((2 * parts, rows, HIDDEN), BF16),
            pltpu.VMEM((rows, width), BF16),
            pltpu.VMEM((n, 8, LANES), F32),
            pltpu.VMEM((ROWS, width), F32),
            pltpu.VMEM((ROWS, width), F32),
            pltpu.VMEM((ROWS, LANES), F32),
            pltpu.VMEM((ROWS, LANES), F32),
        ]
        + [pltpu.SemaphoreType.DMA((n,))] * 8
        + [
            pltpu.SemaphoreType.DMA((4 * parts,)),
            pltpu.SemaphoreType.DMA,
            pltpu.SemaphoreType.DMA((2 * parts,)),
            pltpu.SemaphoreType.DMA((2 * parts,)),
            pltpu.SemaphoreType.DMA((2 * parts,)),
            pltpu.VMEM((rows, width), BF16),
            pltpu.VMEM((rows, width), BF16),
            pltpu.SemaphoreType.DMA((2,)),
            pltpu.SemaphoreType.DMA((rows // ROWS,)),
        ],
        compiler_params=pltpu.CompilerParams(
            collective_id=1, has_side_effects=True, vmem_limit_bytes=60 * 1024 * 1024
        ),
        name="experts",
    )(xd, cr, gs, win, wout, win2, wout2)
def reduce_rows(n, width):
    return [-(-rows // (n * 16)) * 16 * n for rows in [3 * width] * 4 + [3 * n + 32]]


def reduce_stages(n, core):
    if n == 16:
        return [(1 + core, 2), (2 - core, 2), (4, 4)]
    return [(1 + core, 2), (2 - core, 2)] + [(2**s, 2) for s in range(2, n.bit_length() - 1)]


def reduce_shapes(n, width):
    stages = reduce_stages(n, 0)
    scratch = []
    for rows in reduce_rows(n, width):
        scratch.append(pltpu.VMEM((rows, LANES), BF16))
        for _, radix in stages:
            rows //= radix
            scratch.append(pltpu.VMEM((radix - 1, rows, LANES), BF16))
        scratch += [pltpu.SemaphoreType.DMA((2 * len(stages) + 2, 3))] * 2
    return scratch


def reduce_steps(n, me, core, part, total, scratch, finish):
    stages = reduce_stages(n, core)
    arrived, *halves = scratch[:-2]
    sends, recvs = scratch[-2:]
    unit = part.shape[1] // n
    count = len(stages)
    spots, starts, sizes = [], [0], [n]
    for distance, radix in stages:
        spot = lax.rem(me // distance, radix)
        spots.append(spot)
        sizes.append(sizes[-1] // radix)
        starts.append(starts[-1] + spot * sizes[-1])

    def region(start, units):
        return pl.ds(pl.multiple_of(start * unit, 16), units * unit)

    def copy(step, slot, src, dst, device):
        return pltpu.make_async_remote_copy(
            src_ref=src,
            dst_ref=dst,
            send_sem=sends.at[step, slot],
            recv_sem=recvs.at[step, slot],
            device_id=device,
            device_id_type=MESH,
        )

    def transfers(step):
        sibling = (me, 1 - core)
        if step == 0:
            return [copy(step, 0, part.at[1 - core], arrived, sibling)]
        if step == 2 * count + 1:
            held = total.at[core]
            return [copy(step, 0, held, held, sibling)]
        s = step - 1 if step <= count else 2 * count - step
        distance, radix = stages[s]
        made = []
        for slot in range(radix - 1):
            spot = lax.rem(spots[s] + slot + 1, radix)
            device = (me + distance * (spot - spots[s]), core)
            if step <= count:
                away = part.at[core, region(starts[s] + spot * sizes[s + 1], sizes[s + 1])]
                made.append(copy(step, slot, away, halves[s].at[slot], device))
            else:
                held = total.at[core, region(starts[s + 1], sizes[s + 1])]
                made.append(copy(step, slot, held, held, device))
        return made

    def add(step):
        if step == 0:
            mine, others = slice(None), [arrived[...]]
        elif step <= count:
            s = step - 1
            mine = region(starts[s + 1], sizes[s + 1])
            others = [halves[s][slot] for slot in range(stages[s][1] - 1)]
        else:
            return
        summed = part[core, mine, :].astype(F32)
        for other in others:
            summed = summed + other.astype(F32)
        if step == count:
            total[core, mine, :] = summed.astype(BF16)
        else:
            part[core, mine, :] = summed.astype(BF16)

    last = 2 * count + 1

    def run(step):
        if step > 0:
            for transfer in transfers(step - 1):
                transfer.wait_recv()
            add(step - 1)
        if step <= last:
            for transfer in transfers(step):
                transfer.start()
        else:
            finish()
            for done in range(last + 1):
                for transfer in transfers(done):
                    transfer.wait_send()

    return [functools.partial(run, step) for step in range(last + 2)]


def reducers(n, me, core, parts, totals, scratch, finish):
    size = len(reduce_stages(n, core)) + 3
    return [
        reduce_steps(
            n, me, core, part, total, scratch[j * size : (j + 1) * size], functools.partial(finish, j)
        )
        for j, (part, total) in enumerate(zip(parts, totals))
    ]


def unroll_band(band):
    wide = band.shape[1]
    folded = band[:8]
    for g in range(1, band.shape[0] // 8):
        folded = folded + pltpu.roll(band[8 * g : 8 * g + 8], wide - 8 * g, 1)
    line = folded[:1]
    for s in range(1, 8):
        line = line + pltpu.roll(folded, wide - s, 1)[s : s + 1]
    return line


PLAN = (
    (0,),
    ((), (), (), (), (), ()),
    ((1, 0), (2, 1, 0), (3, 2, 1, 0)),
    (3, 2, 1, 0),
    (4, 3, 2, 1, 0),
)


def back_kernel(
    n, pad,
    tok_hbm, ga_ref, wq_hbm, wk_hbm, wv_hbm, wo_hbm, gf_ref, wrt_ref, routes_ref, cot_hbm, st_hbm, gx_hbm, gg_ref, p_ref,
    nat_hbm, qt_hbm, kt_hbm, v_hbm, probs_hbm, mixt_hbm, hid_hbm, nf_hbm, pr_ref, gcol_ref,
    out_hbm, dx_hbm, total0_hbm, totals_hbm, total4_hbm,
    got_ref, probs_ref, gmt_ref, gqt_ref, gkt_ref, gvt_ref, lines_ref,
    send_sem, recv_sem, probs_sem, own_sem, part0, part1, part2, part3, part4,
    tok_ref, wq_ref, wk_ref, wv_ref, wo_ref, cot_ref, st_ref, gx_ref, nat_ref, qt_ref, kt_ref, v_ref, mixt_ref, hid_ref, nf_ref,
    out_ref, dx_ref, total0, totals, total4, load_sem, save_sem, *reduce_scratch,
):
    me = lax.axis_index("expert")
    core = lax.axis_index("ffn")
    count, width = tok_ref.shape
    rows_all = n * pad
    barrier = greet(n, me, core, True)
    need = fetch(
        load_sem,
        (st_hbm, st_ref), (gx_hbm, gx_ref), (nf_hbm, nf_ref), (hid_hbm, hid_ref), (cot_hbm, cot_ref), (mixt_hbm, mixt_ref),
        (wo_hbm, wo_ref), (v_hbm, v_ref), (kt_hbm, kt_ref), (qt_hbm, qt_ref), (nat_hbm, nat_ref), (wq_hbm, wq_ref),
        (wk_hbm, wk_ref), (wv_hbm, wv_ref), (tok_hbm, tok_ref),
    )

    def load(pair):
        return pltpu.make_async_copy(
            probs_hbm.at[pl.ds(2 * pair, 2)], probs_ref.at[pair % 2], probs_sem.at[pair % 2]
        )

    load(0).start()
    load(1).start()

    def rows_of(e):
        return pl.ds(pl.multiple_of(e * pad, pad), pad)

    def copy(k):
        target = partner(n, me, k)
        return pltpu.make_async_remote_copy(
            src_ref=p_ref.at[rows_of(target)],
            dst_ref=got_ref.at[rows_of(me)],
            send_sem=send_sem.at[k],
            recv_sem=recv_sem.at[k],
            device_id=(target, core),
            device_id_type=MESH,
        )

    pl.semaphore_wait(barrier, n)
    each(n, lambda k: copy(k).start())
    own = pltpu.make_async_copy(p_ref.at[rows_of(me)], got_ref.at[rows_of(me)], own_sem)
    own.start()
    parts = (part0, part1, part2, part3, part4)
    queue = reducers(
        n, me, core, parts, [total0, totals.at[0], totals.at[1], totals.at[2], total4], reduce_scratch,
        lambda j: kept[j].start(),
    )
    done = [0] * 5
    kept = [pltpu.make_async_copy(total0, total0_hbm, save_sem.at[0])]
    for g in range(3):
        kept.append(pltpu.make_async_copy(totals.at[g], totals_hbm.at[g], save_sem.at[g + 1]))
    kept.append(pltpu.make_async_copy(total4, total4_hbm, save_sem.at[4]))
    kept.append(pltpu.make_async_copy(dx_ref, dx_hbm, save_sem.at[5]))
    kept.append(pltpu.make_async_copy(out_ref, out_hbm, save_sem.at[6]))

    def tick(*chosen):
        for j in chosen:
            if done[j] < len(queue[j]):
                queue[j][done[j]]()
                done[j] += 1

    base = 3 * width
    for part, filled in zip(parts, [base] * 4 + [3 * n + 32]):
        if part.shape[1] > filled:
            part[:, filled:, :] = jnp.zeros((2, part.shape[1] - filled, LANES), BF16)

    share = LANES // pad
    tiles = []
    for t in range(n // share):
        tile = gg_ref[t * share][:1]
        for u in range(1, share):
            tile = tile + gg_ref[t * share + u][:1]
        tiles.append(tile)
    marks = jnp.concatenate(tiles, axis=1)
    need(0)
    grad_gate = jnp.sum(dot(pieces(marks), st_ref[...], 1, 1), axis=0, keepdims=True)
    chosen = (iota((n, count), 0) == routes_ref[...]).astype(F32)
    router = pr_ref[...]
    grad_probs = chosen * grad_gate
    grad_logits = router * (grad_probs - jnp.sum(router * grad_probs, axis=0, keepdims=True))
    grad_logits = grad_logits.astype(BF16)
    need(1, 2)
    grad_router = dot(nf_ref[...], grad_logits, 0, 1).T
    grad_nf = dot(st_ref[...], gx_ref[...]) + dot(grad_logits, wrt_ref[...], 0, 0)
    need(3, 4)
    hidden = hid_ref[...]
    scale = lax.rsqrt(jnp.mean(hidden * hidden, axis=-1, keepdims=True) + EPSILON)
    weighted = grad_nf * gf_ref[...][None]
    grad_gain_ffn = jnp.sum(grad_nf * hidden * scale, axis=0, keepdims=True)
    inner = jnp.mean(weighted * hidden, axis=-1, keepdims=True)
    grad_hidden = (
        cot_ref[...].astype(F32) + scale * weighted - hidden * (scale * scale * scale * inner)
    )
    dx_ref[...] = grad_hidden
    branch = grad_hidden.astype(BF16)
    need(5)
    for t in range(width // LANES):
        cut = slice(t * LANES, (t + 1) * LANES)
        rows = slice(t % 3 * width, (t % 3 + 1) * width)
        part0[t // 3, rows, :] = dot(mixt_ref[...], branch[:, cut]).astype(BF16)
    tick(*PLAN[0])
    need(6)
    gmt_ref[...] = dot(wo_ref[...], branch, 1, 1).astype(BF16)
    need(7, 8, 9)
    lines_ref[...] = jnp.zeros_like(lines_ref)
    lower_half = iota((LANES, count), 0) < HEAD_DIM
    blocks = count // LANES
    place = iota((1, 4 * LANES), 1)

    def run_pair(pair):
        load(pair).wait()
        lanes = pl.ds(pair * LANES, LANES)
        both = gmt_ref[lanes, :]
        for sub in range(2):
            head = 2 * pair + sub
            mask = lower_half if sub == 0 else jnp.logical_not(lower_half)
            chunk = jnp.where(mask, both, jnp.zeros_like(both))
            features = pl.ds(head * HEAD_DIM, HEAD_DIM)
            grad_mixed = gmt_ref[features, :]
            delta = jnp.sum(
                grad_mixed.astype(F32) * mixt_ref[features, :].astype(F32), axis=0, keepdims=True
            )
            probs = probs_ref[pair % 2, sub]
            grad_probs = dot(v_ref[:, lanes], chunk)
            scores = probs.astype(F32) * (grad_probs - delta)
            low = scores.astype(BF16)
            gqt_ref[features, :] = dot(kt_ref[features, :], low).astype(BF16)
            gkt_ref[features, :] = dot(qt_ref[features, :], low, 1, 1).astype(BF16)
            gvt_ref[features, :] = dot(grad_mixed, probs, 1, 1).astype(BF16)
            near = {0: None, -1: None, 1: None}
            far = {-1: None, 1: None}
            for row in range(blocks):
                for col in range(blocks):
                    block = scores[
                        row * LANES : (row + 1) * LANES, col * LANES : (col + 1) * LANES
                    ]
                    gap = row - col
                    if gap in near:
                        near[gap] = block if near[gap] is None else near[gap] + block
                    else:
                        side = 1 if gap > 0 else -1
                        far[side] = block if far[side] is None else far[side] + block
            band = jnp.concatenate([near[0], near[-1], jnp.zeros_like(near[0]), near[1]], axis=1)
            line = unroll_band(band)
            for side, lane in ((-1, 255), (1, 257)):
                total = jnp.sum(jnp.sum(far[side], axis=0, keepdims=True), axis=1, keepdims=True)
                line = line + jnp.where(place == lane, total, 0.0)
            lines_ref[pl.ds(head, 1), :] = line
        if pair + 2 < HEADS // 2:
            load(pair + 2).start()

    for group, part in enumerate((part1, part2, part3)):
        for pair in (2 * group, 2 * group + 1):
            run_pair(pair)
            tick(*PLAN[1][pair])
        if group == 0:
            need(10)
        for i, grad in enumerate((gqt_ref, gkt_ref, gvt_ref)):
            columns = grad[group * 2 * LANES : (group + 1) * 2 * LANES, :]
            made = dot(nat_ref[...], columns, 1, 1).astype(BF16)
            for c in range(2):
                part[c, i * width : (i + 1) * width, :] = made[:, c * LANES : (c + 1) * LANES]
        tick(*PLAN[2][group])
    need(11, 12, 13, 14)
    grad_na = (
        dot(wq_ref[...], gqt_ref[...])
        + dot(wk_ref[...], gkt_ref[...])
        + dot(wv_ref[...], gvt_ref[...])
    ).T
    x = tok_ref[...].astype(F32)
    scale = lax.rsqrt(jnp.mean(x * x, axis=-1, keepdims=True) + EPSILON)
    weighted = grad_na * ga_ref[...][None]
    grad_gain_attn = jnp.sum(grad_na * x * scale, axis=0, keepdims=True)
    inner = jnp.mean(weighted * x, axis=-1, keepdims=True)
    tick(*PLAN[3])
    dx_ref[...] = dx_ref[...] + scale * weighted - x * (scale * scale * scale * inner)
    kept[5].start()
    grad_bias = dot(band_onehot(), lines_ref[...], 1, 1, HIGH)
    gains = jnp.concatenate([grad_gain_attn, grad_gain_ffn, jnp.zeros((14, width), F32)], axis=0)
    for c in range(2):
        for t in range(3):
            cut = slice((3 * c + t) * LANES, (3 * c + t + 1) * LANES)
            part4[c, t * n : (t + 1) * n, :] = grad_router[:, cut].astype(BF16)
        rows = slice(3 * n, 3 * n + 16)
        sums = [gains[:, (3 * c + t) * LANES : (3 * c + t + 1) * LANES][:2] for t in range(3)]
        part4[c, rows, :] = jnp.concatenate(sums + [jnp.zeros((10, LANES), F32)], axis=0).astype(BF16)
        rows = slice(3 * n + 16, 3 * n + 32)
        wide = jnp.concatenate(
            [grad_bias[16 * c : 16 * c + 16], jnp.zeros((16, LANES - 16), F32)], axis=1
        )
        part4[c, rows, :] = wide.astype(BF16)
    tick(*PLAN[4])
    own.wait()
    each(n, lambda k: copy(k).wait())
    picked = dot(st_ref[...], got_ref[...])
    out_ref[...] = (hid_ref[...] + gcol_ref[:, :1] * picked).astype(BF16)
    kept[6].start()
    while any(done[j] < len(queue[j]) for j in range(5)):
        tick(4, 3, 2, 1, 0)
    for copied in kept:
        copied.wait()


def run_back(n, pad, tokens, *rest):
    count, width = tokens.shape
    rows = n * pad
    vmem = pl.BlockSpec(memory_space=pltpu.VMEM)
    anywhere = pl.BlockSpec(memory_space=pl.ANY)
    shapes = (
        ((count, width), BF16, anywhere),
        ((count, width), F32, anywhere),
        ((2, reduce_rows(n, width)[0], LANES), BF16, anywhere),
        ((3, 2, reduce_rows(n, width)[0], LANES), BF16, anywhere),
        ((2, reduce_rows(n, width)[4], LANES), BF16, anywhere),
    )
    return pl.pallas_call(
        functools.partial(back_kernel, n, pad),
        out_shape=[jax.ShapeDtypeStruct(shape, dtype) for shape, dtype, _ in shapes],
        in_specs=[anywhere, vmem]
        + [anywhere] * 4
        + [vmem] * 3
        + [anywhere] * 3
        + [vmem]
        + [anywhere] * 9
        + [vmem] * 2,
        out_specs=[space for _, _, space in shapes],
        scratch_shapes=[
            pltpu.VMEM((rows, width), BF16),
            pltpu.VMEM((2, 2, count, count), BF16),
            pltpu.VMEM((width, count), BF16),
            pltpu.VMEM((width, count), BF16),
            pltpu.VMEM((width, count), BF16),
            pltpu.VMEM((width, count), BF16),
            pltpu.VMEM((16, 4 * LANES), F32),
            pltpu.SemaphoreType.DMA((n,)),
            pltpu.SemaphoreType.DMA((n,)),
            pltpu.SemaphoreType.DMA((2,)),
            pltpu.SemaphoreType.DMA,
            *(pltpu.VMEM((2, part, LANES), BF16) for part in reduce_rows(n, width)),
            pltpu.VMEM((count, width), BF16),
            *[pltpu.VMEM((width, width), BF16)] * 4,
            pltpu.VMEM((count, width), BF16),
            pltpu.VMEM((count, rows), BF16),
            pltpu.VMEM((rows, width), BF16),
            *[pltpu.VMEM((width, count), BF16)] * 3,
            pltpu.VMEM((count, width), BF16),
            pltpu.VMEM((width, count), BF16),
            pltpu.VMEM((count, width), F32),
            pltpu.VMEM((count, width), BF16),
            *[pltpu.VMEM(shape, dtype) for shape, dtype, _ in shapes],
            pltpu.SemaphoreType.DMA((15,)),
            pltpu.SemaphoreType.DMA((7,)),
            *reduce_shapes(n, width),
        ],
        compiler_params=pltpu.CompilerParams(
            collective_id=2, has_side_effects=True, vmem_limit_bytes=63 * 1024 * 1024
        ),
        name="attend_back",
    )(tokens, *rest)


def finish_kernel(
    n,
    first0, first1, first2, q_ref, k_ref, v_ref, small_ref, own_in, got_in, own_out, got_out, out_ref, dx_ref, rms_ref,
    go_ref, gq_ref, gk_ref, gv_ref, gi_ref, gw_ref, router_ref, gain_a, gain_f, bias_ref, output_ref, grad_ref, roots_ref,
):
    for t in range(6):
        cut = slice(t * LANES, (t + 1) * LANES)
        go_ref[:, cut] = (first0, first1, first2)[t % 3][t // 3].astype(F32)
        for made, grad in ((gq_ref, q_ref), (gk_ref, k_ref), (gv_ref, v_ref)):
            made[:, cut] = grad[t // 2, t % 2].astype(F32)
    gi_ref[...] = own_in[...].astype(F32) + got_in[...].astype(F32)
    gw_ref[...] = own_out[...].astype(F32) + got_out[...].astype(F32)
    output_ref[...] = out_ref[...]
    grad_ref[...] = dx_ref[...]

    @pl.when(pl.program_id(0) == 0)
    def _():
        roots_ref[...] = rms_ref[3:5, :]
        small = small_ref[...].astype(F32)
        for t in range(6):
            c, at = t // 3, t % 3
            cut = slice(t * LANES, (t + 1) * LANES)
            router_ref[:, cut] = small[c, at * n : (at + 1) * n]
            gain_a[cut] = small[c, 3 * n + 2 * at]
            gain_f[cut] = small[c, 3 * n + 2 * at + 1]
        bias = jnp.concatenate([small[c, 3 * n + 16 : 3 * n + 32] for c in range(2)], axis=0)
        bias_ref[...] = bias.T[:HEADS]


def run_finish(n, first, groups, smalls, own_in, got_in, own_out, got_out, out, dx, rms):
    width, half = own_in.shape
    count = out.shape[0]
    steps = 3
    rows = width // steps
    whole = lambda *shape: pl.BlockSpec(shape, lambda t: (0,) * len(shape))
    by_rows = lambda rows, columns: pl.BlockSpec((rows, columns), lambda t: (t, 0))
    out_part = lambda i: pl.BlockSpec((2, rows, LANES), lambda t: (0, i * steps + t, 0))
    weight = lambda i: pl.BlockSpec((3, 2, rows, LANES), lambda t: (0, 0, i * steps + t, 0))
    grad_shape = jax.ShapeDtypeStruct((width, width), F32)
    some = pl.BlockSpec((count // 2, width), lambda t: (jnp.minimum(t, 1), 0))
    rows_in, rows_out = by_rows(rows, half), by_rows(half // steps, width)
    return pl.pallas_call(
        functools.partial(finish_kernel, n),
        grid=(steps,),
        out_shape=[
            grad_shape,
            grad_shape,
            grad_shape,
            grad_shape,
            jax.ShapeDtypeStruct((width, half), F32),
            jax.ShapeDtypeStruct((half, width), F32),
            jax.ShapeDtypeStruct((n, width), F32),
            jax.ShapeDtypeStruct((width,), F32),
            jax.ShapeDtypeStruct((width,), F32),
            jax.ShapeDtypeStruct((HEADS, BUCKETS), F32),
            jax.ShapeDtypeStruct((count, width), BF16),
            jax.ShapeDtypeStruct((count, width), F32),
            jax.ShapeDtypeStruct((2, count), F32),
        ],
        in_specs=[out_part(i) for i in range(3)]
        + [weight(i) for i in range(3)]
        + [whole(*smalls.shape), rows_in, rows_in, rows_out, rows_out, some, some, whole(8, count)],
        out_specs=[by_rows(rows, width)] * 4
        + [rows_in, rows_out]
        + [whole(n, width), whole(width), whole(width), whole(HEADS, BUCKETS)]
        + [some, some, whole(2, count)],
        compiler_params=pltpu.CompilerParams(vmem_limit_bytes=60 * 1024 * 1024),
        name="finish",
    )(first, first, first, groups, groups, groups, smalls, own_in, got_in, own_out, got_out, out, dx, rms)


def per_device(
    tokens, gain_attn, query_weight, key_weight, value_weight, out_weight, rel_bias, gain_ffn, router_weight,
    expert_in, expert_out, routes, capacity, cotangent,
):
    count, width = tokens.shape
    n = lax.axis_size("expert")
    experts = router_weight.shape[1]
    assert experts == n and count == SEQ
    slots = 2 * count // experts
    pad = -(-slots // 16) * 16
    router_rows = router_weight.T
    routes = routes.reshape(1, count)
    (
        cots, in_other, out_other, dispatched, gates, slots_t, normed_t, query_t, key_t, values, probs, mixed_t,
        hidden, normed_ffn, router_t, gate_col, roots,
    ) = attend(
        n, slots, pad, tokens, gain_attn, query_weight, key_weight, value_weight, out_weight, rel_bias.T, gain_ffn,
        router_rows, routes, capacity, cotangent, expert_in[0], expert_out[0],
    )
    grad_rows, marks, produced, own_in, own_out, got_in, got_out = run_experts(
        n, pad, dispatched, cots, gates, expert_in[0], expert_out[0], in_other, out_other
    )
    output, input_grad, first, groups, smalls = run_back(
        n, pad, tokens, gain_attn, query_weight, key_weight, value_weight, out_weight, gain_ffn, router_rows, routes,
        cotangent, slots_t, grad_rows, marks, produced, normed_t, query_t, key_t, values, probs, mixed_t, hidden,
        normed_ffn, router_t, gate_col,
    )
    (
        grad_out, grad_query, grad_key, grad_value, grad_in, grad_expert, grad_router, grad_gain_attn, grad_gain_ffn,
        grad_bias, output, input_grad, rms_values,
    ) = run_finish(n, first, groups, smalls, own_in, got_in, own_out, got_out, output, input_grad, roots)
    return (
        output,
        input_grad,
        grad_gain_attn,
        grad_query,
        grad_key,
        grad_value,
        grad_out,
        grad_bias.T,
        grad_gain_ffn,
        grad_router.T,
        grad_in[None],
        grad_expert[None],
        rms_values,
    )


def solution(mesh):
    placed = (
        P(("expert", "ffn"), None),
        P(),
        P(),
        P(),
        P(),
        P(),
        P(),
        P(),
        P(),
        P("expert", None, "ffn"),
        P("expert", "ffn", None),
        P(("expert", "ffn"), None),
        P(("expert", "ffn")),
        P(("expert", "ffn"), None),
    )
    return jax.shard_map(
        per_device,
        mesh=mesh,
        in_specs=placed,
        out_specs=(
            P(("expert", "ffn"), None),
            P(("expert", "ffn"), None),
            P(),
            P(),
            P(),
            P(),
            P(),
            P(),
            P(),
            P(),
            P("expert", None, "ffn"),
            P("expert", "ffn", None),
            P(None, ("expert", "ffn")),
        ),
        check_vma=False,
    )
```

```python
import functools
import jax
import jax.numpy as jnp
from jax import lax
from jax.experimental import pallas as pl
from jax.experimental.pallas import tpu as pltpu
from jax.sharding import PartitionSpec as P

HEADS = 12
HEAD_DIM = 64
BUCKETS = 32
SEQ = 512
EPSILON = 1e-06
THRESHOLDS = (12, 16, 23, 32, 46, 64, 91)
HIGH = lax.Precision.HIGHEST
F32 = jnp.float32
BF16 = jnp.bfloat16
MESH = pl.DeviceIdType.MESH
LANES = 128


def dot(a, b, ca=1, cb=0, precision=None):
    return lax.dot_general(
        a, b, (((ca,), (cb,)), ((), ())), precision=precision, preferred_element_type=F32
    )


def iota(shape, dim):
    return lax.broadcasted_iota(jnp.int32, shape, dim)


def div(a, b):
    return a // b if isinstance(a, int) else lax.div(a, jnp.int32(b))


def rem(a, b):
    return a % b if isinstance(a, int) else lax.rem(a, jnp.int32(b))


def block_at(n, me, step, per, blocks):
    if n != 16:
        return rem(div(me, per) + step, blocks)
    layer = div(me, 4)
    low = rem(rem(layer, 2) + div(step + 1, 2), 2)
    return 2 * rem(div(layer, 2) + 1 - div(step, 2), 2) + low


def partner(n, me, k):
    if n != 16:
        return rem(me + k, n)
    return 4 * block_at(n, me, div(k, 4), 4, 4) + rem(rem(me, 4) + rem(k, 4), 4)


def index_between(n, sender, receiver, step):
    if n != 16:
        return rem(receiver - sender + n, n)
    return 4 * step + rem(rem(receiver, 4) - rem(sender, 4) + 4, 4)


def each(n, body):
    if n == 16:
        for k in range(n):
            if k != 12:
                body(k)
    else:

        def step(k, carry):
            body(k)
            return carry

        lax.fori_loop(1, n, step, 0)


def greet(n, me, core, sibling):
    barrier = pltpu.get_barrier_semaphore()

    def signal(k):
        pl.semaphore_signal(
            barrier, inc=1, device_id=(partner(n, me, k), core), device_id_type=MESH
        )

    each(n, signal)
    if sibling:
        pl.semaphore_signal(barrier, inc=1, device_id=(me, 1 - core), device_id_type=MESH)
    return barrier


def band_onehot():
    place = iota((BUCKETS, 4 * LANES), 1)
    offset = jnp.where(place < 2 * LANES, -place, 4 * LANES - place)
    distance = jnp.abs(offset)
    larger = jnp.full(distance.shape, 8, jnp.int32)
    for limit in THRESHOLDS:
        larger = larger + (distance >= limit).astype(jnp.int32)
    bucket = jnp.where(distance < 8, distance, larger) + jnp.where(offset > 0, 16, 0)
    return (bucket == iota(bucket.shape, 0)).astype(F32)


def pieces(row):
    high = row.astype(BF16)
    rest = row - high.astype(F32)
    middle = rest.astype(BF16)
    low = (rest - middle.astype(F32)).astype(BF16)
    filler = jnp.zeros((5, row.shape[1]), BF16)
    return jnp.concatenate([high, middle, low, filler], axis=0)


def fetch(sem, *pairs):
    copies = [pltpu.make_async_copy(src, dst, sem.at[i]) for i, (src, dst) in enumerate(pairs)]
    for copy in copies:
        copy.start()

    def need(*which):
        for i in which:
            copies[i].wait()

    return need


def attend_kernel(
    n, slots, pad,
    tok_hbm, ga_ref, wq_hbm, wk_hbm, wv_hbm, wo_hbm, rel_ref, gf_ref, wrt_ref, routes_ref, cap_ref, cot_ref, win_ref, wout_ref,
    cr_ref, wi2_ref, wo2_ref, xd_hbm, gs_ref, st_hbm, nat_hbm, qt_hbm, kt_hbm, v_hbm, p_hbm, mixt_hbm, hid_hbm, nf_hbm, pr_ref, gcol_ref, rms_ref,
    cd_ref, s_ref, k_ref, vt_ref, band_ref, send_sem, recv_sem, own_sem, w_send, w_recv,
    tok_ref, wq_ref, wk_ref, wv_ref, wo_ref, xd_ref, st_ref, nat_ref, qt_ref, kt_ref, v_ref, p_ref, mixt_ref, hid_ref, nf_ref,
    load_sem, save_sem, probs_sem,
):
    me = lax.axis_index("expert")
    core = lax.axis_index("ffn")
    count, width = tok_ref.shape
    rows_all = n * pad
    barrier = greet(n, me, core, True)
    need = fetch(
        load_sem,
        (tok_hbm, tok_ref), (wq_hbm, wq_ref), (wk_hbm, wk_ref), (wv_hbm, wv_ref), (wo_hbm, wo_ref),
    )
    saves = []

    def save(src, dst):
        saves.append(pltpu.make_async_copy(src, dst, save_sem.at[len(saves)]))
        saves[-1].start()


    routes = routes_ref[...]
    chosen = (iota((n, count), 0) == routes).astype(F32)
    upper = (iota((count, count), 0) < iota((count, count), 1)).astype(F32).astype(BF16)
    earlier = dot(chosen.astype(BF16), upper)
    position = jnp.sum(earlier * chosen, axis=0, keepdims=True)
    live = (cap_ref[0] * count // n).astype(F32)
    slot = jnp.where(position < live, routes * pad + position.astype(jnp.int32), rows_all)

    @pl.loop(0, rows_all // 256)
    def _(block):
        start = pl.multiple_of(block * 256, 256)
        hot = (iota((256, count), 0) + start == slot).astype(F32).astype(BF16)
        s_ref[pl.ds(start, 256), :] = hot
        cd_ref[pl.ds(start, 256), :] = dot(hot, cot_ref[...]).astype(BF16)

    pl.semaphore_wait(barrier, n)

    def rows_of(e):
        return pl.ds(pl.multiple_of(e * pad, pad), pad)

    def copy(k):
        target = partner(n, me, k)
        return pltpu.make_async_remote_copy(
            src_ref=cd_ref.at[rows_of(target)],
            dst_ref=cr_ref.at[rows_of(me)],
            send_sem=send_sem.at[k],
            recv_sem=recv_sem.at[k],
            device_id=(target, core),
            device_id_type=MESH,
        )

    each(n, lambda k: copy(k).start())
    own = pltpu.make_async_copy(cd_ref.at[rows_of(me)], cr_ref.at[rows_of(me)], own_sem)
    own.start()
    halves = [
        pltpu.make_async_remote_copy(
            src_ref=src,
            dst_ref=dst,
            send_sem=w_send.at[i],
            recv_sem=w_recv.at[i],
            device_id=(me, 1 - core),
            device_id_type=MESH,
        )
        for i, (src, dst) in enumerate(((win_ref, wi2_ref), (wout_ref, wo2_ref)))
    ]
    for half in halves:
        half.start()

    need(0)
    x = tok_ref[...].astype(F32)
    ms1 = jnp.mean(x * x, axis=-1, keepdims=True)
    na = (x * lax.rsqrt(ms1 + EPSILON) * ga_ref[...][None]).astype(BF16)
    nat_ref[...] = na.T
    need(1)
    qt_ref[...] = dot(na, wq_ref[...]).astype(BF16).T
    need(2)
    keys = dot(na, wk_ref[...]).astype(BF16)
    k_ref[...] = keys
    kt_ref[...] = keys.T
    need(3)
    values = dot(na, wv_ref[...]).astype(BF16)
    v_ref[...] = values
    vt_ref[...] = values.T
    save(nat_ref, nat_hbm)
    save(qt_ref, qt_hbm)
    save(kt_ref, kt_hbm)
    save(v_ref, v_hbm)
    band_ref[...] = dot(rel_ref[...], band_onehot(), 1, 0, HIGH)
    lower_half = iota((LANES, count), 0) < HEAD_DIM
    blocks = count // LANES

    def save_probs(pair):
        heads = pl.ds(2 * pair, 2)
        return pltpu.make_async_copy(p_ref.at[heads], p_hbm.at[heads], probs_sem.at[pair])

    @pl.loop(0, HEADS // 2)
    def _(pair):
        lanes = pl.ds(pl.multiple_of(pair * LANES, LANES), LANES)
        both = qt_ref[lanes, :]
        for sub in range(2):
            head = 2 * pair + sub
            mask = lower_half if sub == 0 else jnp.logical_not(lower_half)
            query = jnp.where(mask, both, jnp.zeros_like(both))
            line = band_ref[pl.ds(head, 1), :]
            band = pltpu.roll(
                jnp.broadcast_to(line, (LANES, 4 * LANES)), 0, 1, stride=1, stride_axis=0
            )
            before = jnp.broadcast_to(line[:, 255:256], (LANES, LANES))
            after = jnp.broadcast_to(line[:, 257:258], (LANES, LANES))
            by_gap = {
                0: band[:, :LANES],
                -1: band[:, LANES : 2 * LANES],
                1: band[:, 3 * LANES :],
            }
            scores = []
            for row in range(blocks):
                bias = jnp.concatenate(
                    [
                        by_gap.get(row - col, after if row > col else before)
                        for col in range(blocks)
                    ],
                    axis=1,
                )
                made = dot(k_ref[row * LANES : (row + 1) * LANES, lanes], query)
                scores.append(made + bias)
            scores = jnp.concatenate(scores, axis=0)
            peak = jnp.max(scores, axis=0, keepdims=True)
            expo = jnp.exp(scores - peak)
            total = jnp.sum(expo, axis=0, keepdims=True)
            probs = (expo * (1.0 / total)).astype(BF16)
            p_ref[head] = probs
            features = pl.ds(pl.multiple_of(head * HEAD_DIM, HEAD_DIM), HEAD_DIM)
            mixt_ref[features, :] = dot(vt_ref[features, :], probs).astype(BF16)
        save_probs(pair).start()

    save(mixt_ref, mixt_hbm)
    need(4)
    hidden = tok_ref[...].astype(F32) + dot(mixt_ref[...].T, wo_ref[...])
    hid_ref[...] = hidden
    save(hid_ref, hid_hbm)
    ms2 = jnp.mean(hidden * hidden, axis=-1, keepdims=True)
    nf = (hidden * lax.rsqrt(ms2 + EPSILON) * gf_ref[...][None]).astype(BF16)
    nf_ref[...] = nf
    save(nf_ref, nf_hbm)
    logits = dot(wrt_ref[...], nf, 1, 1)
    top = jnp.max(logits, axis=0, keepdims=True)
    raised = jnp.exp(logits - top)
    router = raised / jnp.sum(raised, axis=0, keepdims=True)
    pr_ref[...] = router
    gate = jnp.sum(router * chosen, axis=0, keepdims=True)
    gcol_ref[...] = jnp.broadcast_to(gate, (LANES, count)).T
    roots = jnp.concatenate(
        [
            jnp.broadcast_to(jnp.sqrt(ms + EPSILON), (count, LANES)).T[:4]
            for ms in (ms1, ms2)
        ],
        axis=0,
    )
    rms_ref[...] = roots
    parts = pieces(gate)

    @pl.loop(0, rows_all // 256)
    def _(block):
        start = pl.multiple_of(block * 256, 256)
        hot = s_ref[pl.ds(start, 256), :]
        xd_ref[pl.ds(start, 256), :] = dot(hot, nf_ref[...]).astype(BF16)
        split = dot(parts, hot, 1, 1)
        gs_ref[:, pl.ds(start, 256)] = jnp.broadcast_to(
            jnp.sum(split, axis=0, keepdims=True), split.shape
        )
        st_ref[:, pl.ds(start, 256)] = hot.T

    save(xd_ref, xd_hbm)
    save(st_ref, st_hbm)
    for pair in range(HEADS // 2):
        save_probs(pair).wait()
    for copied in saves:
        copied.wait()
    own.wait()
    for half in halves:
        half.wait()
    each(n, lambda k: copy(k).wait())


def attend(n, slots, pad, tokens, ga, wq, wk, wv, wo, rel, gf, wrt, routes, cap, cot, win, wout):
    count, width = tokens.shape
    rows = n * pad
    half = win.shape[-1]
    vmem = pl.BlockSpec(memory_space=pltpu.VMEM)
    anywhere = pl.BlockSpec(memory_space=pl.ANY)
    smem = pl.BlockSpec(memory_space=pltpu.SMEM)
    shapes = (
        ((rows, width), BF16, anywhere),
        ((width, half), BF16, anywhere),
        ((half, width), BF16, anywhere),
        ((rows, width), BF16, anywhere),
        ((8, rows), F32, vmem),
        ((count, rows), BF16, anywhere),
        ((width, count), BF16, anywhere),
        ((width, count), BF16, anywhere),
        ((width, count), BF16, anywhere),
        ((count, width), BF16, anywhere),
        ((HEADS, count, count), BF16, anywhere),
        ((width, count), BF16, anywhere),
        ((count, width), F32, anywhere),
        ((count, width), BF16, anywhere),
        ((n, count), F32, vmem),
        ((count, LANES), F32, vmem),
        ((8, count), F32, vmem),
    )
    return pl.pallas_call(
        functools.partial(attend_kernel, n, slots, pad),
        out_shape=[jax.ShapeDtypeStruct(shape, dtype) for shape, dtype, _ in shapes],
        in_specs=[anywhere, vmem] + [anywhere] * 4 + [vmem] * 4 + [smem, vmem, anywhere, anywhere],
        out_specs=[space for _, _, space in shapes],
        scratch_shapes=[
            pltpu.VMEM((rows, width), BF16),
            pltpu.VMEM((rows, count), BF16),
            pltpu.VMEM((count, width), BF16),
            pltpu.VMEM((width, count), BF16),
            pltpu.VMEM((HEADS, 4 * LANES), F32),
            pltpu.SemaphoreType.DMA((n,)),
            pltpu.SemaphoreType.DMA((n,)),
            pltpu.SemaphoreType.DMA,
            pltpu.SemaphoreType.DMA((2,)),
            pltpu.SemaphoreType.DMA((2,)),
            pltpu.VMEM((count, width), BF16),
            *[pltpu.VMEM((width, width), BF16)] * 4,
            pltpu.VMEM((rows, width), BF16),
            pltpu.VMEM((count, rows), BF16),
            *[pltpu.VMEM((width, count), BF16)] * 3,
            pltpu.VMEM((count, width), BF16),
            pltpu.VMEM((HEADS, count, count), BF16),
            pltpu.VMEM((width, count), BF16),
            pltpu.VMEM((count, width), F32),
            pltpu.VMEM((count, width), BF16),
            pltpu.SemaphoreType.DMA((5,)),
            pltpu.SemaphoreType.DMA((9,)),
            pltpu.SemaphoreType.DMA((HEADS // 2,)),
        ],
        compiler_params=pltpu.CompilerParams(
            collective_id=0, has_side_effects=True, vmem_limit_bytes=60 * 1024 * 1024
        ),
        name="attend",
    )(tokens, ga, wq, wk, wv, wo, rel, gf, wrt, routes, cap, cot, win, wout)
RSQRT2 = 2.0 ** (-0.5)
RSQRT2PI = 0.3989422804014327
ROWS = 256
HIDDEN = 512


def lane_mask(pad, offset):
    return iota((pad, LANES), 1) == iota((pad, LANES), 0) + offset


def expert_kernel(
    n, pad,
    xd_ref, cr_hbm, gs_ref, win_ref, wout_ref, win2_ref, wout2_ref,
    gx_ref, gg_ref, p_hbm, own_in, own_out, got_in, got_out,
    xr_ref, gr_ref, gc_ref, wi_ref, wo_ref, act_ref, gi_ref, gxs_ref, ggs_ref, gate_ref,
    x_send, x_recv, g_send, g_recv, gx_send, gx_recv, gg_send, gg_recv, w_sem, own_sem, dw_send, dw_recv, dw_sem,
    cr_ref, p_ref, local_sem, p_sem,
):
    me = lax.axis_index("expert")
    core = lax.axis_index("ffn")
    half = win_ref.shape[1]
    parts = half // HIDDEN
    rows_all = n * pad
    barrier = greet(n, me, core, True)
    mine = pltpu.make_async_copy(cr_hbm, cr_ref, local_sem.at[0])
    mine.start()
    loads = []
    for j, (first, second) in enumerate(((win_ref, wout_ref), (win2_ref, wout2_ref))):
        for i in range(parts):
            at = j * parts + i
            cut = pl.ds(i * HIDDEN, HIDDEN)
            loads.append(pltpu.make_async_copy(first.at[:, cut], wi_ref.at[at], w_sem.at[2 * at]))
            loads.append(
                pltpu.make_async_copy(second.at[cut, :], wo_ref.at[at], w_sem.at[2 * at + 1])
            )
    for load in loads:
        load.start()

    def rows_of(e):
        return pl.ds(pl.multiple_of(e * pad, pad), pad)

    def tile_of(e):
        return pl.ds(pl.multiple_of(e * pad // LANES * LANES, LANES), LANES)

    def send(k, src, dst, sends, recvs):
        return pltpu.make_async_remote_copy(
            src_ref=src,
            dst_ref=dst,
            send_sem=sends.at[k],
            recv_sem=recvs.at[k],
            device_id=(partner(n, me, k), core),
            device_id_type=MESH,
        )

    def token_copy(k):
        target = partner(n, me, k)
        return send(k, xd_ref.at[rows_of(target)], xr_ref.at[rows_of(me)], x_send, x_recv)

    def gate_copy(k):
        target = partner(n, me, k)
        return send(k, gs_ref.at[:, tile_of(target)], gr_ref.at[me], g_send, g_recv)

    def grad_copy(k):
        target = partner(n, me, k)
        return send(k, gxs_ref.at[rows_of(target)], gx_ref.at[rows_of(me)], gx_send, gx_recv)

    def mark_copy(k):
        target = partner(n, me, k)
        return send(k, ggs_ref.at[target], gg_ref.at[me], gg_send, gg_recv)

    pl.semaphore_wait(barrier, n)

    def start_tokens(k):
        gate_copy(k).start()
        token_copy(k).start()

    each(n, start_tokens)
    held = pltpu.make_async_copy(xd_ref.at[rows_of(me)], xr_ref.at[rows_of(me)], local_sem.at[1])
    held.start()
    gr_ref[me] = gs_ref[:, tile_of(me)]
    offset = lax.rem(me * pad, LANES)
    mask = lane_mask(pad, offset)
    for load in [*loads, mine, held]:
        load.wait()
    per = ROWS // pad
    row_blocks = rows_all // ROWS

    @pl.loop(0, row_blocks)
    def _(step):
        group = step
        if n == 16:
            group = jnp.where(step == 0, 3, jnp.where(step == 1, 0, jnp.where(step == 2, 2, 1)))
        block = block_at(n, me, group, per, row_blocks)
        rows = pl.ds(pl.multiple_of(block * ROWS, ROWS), ROWS)
        columns = []
        for u in range(per):
            source = block * per + u
            k = index_between(n, source, me, group)

            @pl.when(source != me)
            def _():
                gate_copy(k).wait_recv()
                token_copy(k).wait_recv()

            line = jnp.broadcast_to(gr_ref[source][:1], (pad, LANES))
            columns.append(jnp.sum(jnp.where(mask, line, 0.0), axis=1, keepdims=True))
        gates = jnp.concatenate(columns, axis=0)
        gate_ref[...] = jnp.broadcast_to(gates, gate_ref.shape)
        gc_ref[rows, :] = (gates * cr_ref[rows, :].astype(F32)).astype(BF16)
        total_gx, total_p, total_gg = 0.0, 0.0, 0.0
        for i in range(2 * parts):
            inner = dot(xr_ref[rows, :], wi_ref[i])
            raw = dot(cr_ref[rows, :], wo_ref[i], 1, 1)
            normal = 0.5 * (1.0 + lax.erf(inner * RSQRT2))
            density = jnp.exp(-0.5 * inner * inner) * RSQRT2PI
            active = (inner * normal).astype(BF16)
            act_ref[i, rows, :] = active
            weighed = active.astype(F32) * raw
            folded = weighed[:, :LANES]
            for c in range(1, HIDDEN // LANES):
                folded = folded + weighed[:, c * LANES : (c + 1) * LANES]
            total_gg = total_gg + folded
            grad = (gate_ref[:, :1] * raw * (normal + inner * density)).astype(BF16)
            gi_ref[i, rows, :] = grad
            total_gx = total_gx + dot(grad, wi_ref[i], 1, 1)
            total_p = total_p + dot(active, wo_ref[i])

        gxs_ref[rows, :] = total_gx.astype(BF16)
        p_ref[rows, :] = total_p.astype(BF16)
        pltpu.make_async_copy(p_ref.at[rows], p_hbm.at[rows], p_sem.at[block]).start()
        marks = jnp.sum(total_gg, axis=1, keepdims=True)
        for u in range(per):
            source = block * per + u
            k = index_between(n, me, source, group)
            line = jnp.sum(
                jnp.where(mask, marks[u * pad : (u + 1) * pad], 0.0), axis=0, keepdims=True
            )
            ggs_ref[source] = jnp.broadcast_to(line, (8, LANES))

            @pl.when(source != me)
            def _():
                mark_copy(k).start()
                grad_copy(k).start()

    own = pltpu.make_async_copy(gxs_ref.at[rows_of(me)], gx_ref.at[rows_of(me)], own_sem)
    own.start()
    gg_ref[me] = ggs_ref[me]

    def wait_sent(k):
        token_copy(k).wait_send()
        gate_copy(k).wait_send()

    each(n, wait_sent)

    moves = []
    for j in (1, 0):
        for i in range(parts):
            at = j * parts + i
            cut = pl.ds(i * HIDDEN, HIDDEN)
            wi_ref[at] = dot(xr_ref[...], gi_ref[at], 0, 0).astype(BF16)
            wo_ref[at] = dot(act_ref[at], gc_ref[...], 0, 0).astype(BF16)
            for q, (src, dst) in enumerate(
                (
                    (wi_ref.at[at], (got_in if j else own_in).at[:, cut]),
                    (wo_ref.at[at], (got_out if j else own_out).at[cut, :]),
                )
            ):
                if j:
                    moves.append(
                        pltpu.make_async_remote_copy(
                            src_ref=src,
                            dst_ref=dst,
                            send_sem=dw_send.at[2 * i + q],
                            recv_sem=dw_recv.at[2 * i + q],
                            device_id=(me, 1 - core),
                            device_id_type=MESH,
                        )
                    )
                else:
                    moves.append(pltpu.make_async_copy(src, dst, dw_sem.at[2 * i + q]))
                moves[-1].start()
    for move in moves:
        move.wait()

    @pl.loop(0, row_blocks)
    def _(block):
        rows = pl.ds(pl.multiple_of(block * ROWS, ROWS), ROWS)
        pltpu.make_async_copy(p_ref.at[rows], p_hbm.at[rows], p_sem.at[block]).wait()

    own.wait()

    def finish(k):
        mark_copy(k).wait()
        grad_copy(k).wait()

    each(n, finish)


def run_experts(n, pad, xd, cr, gs, win, wout, win2, wout2):
    rows, width = xd.shape
    half = win.shape[1]
    parts = half // HIDDEN
    vmem = pl.BlockSpec(memory_space=pltpu.VMEM)
    anywhere = pl.BlockSpec(memory_space=pl.ANY)
    shapes = (
        ((rows, width), BF16, anywhere),
        ((n, 8, LANES), F32, vmem),
        ((rows, width), BF16, anywhere),
        ((width, half), BF16, anywhere),
        ((half, width), BF16, anywhere),
        ((width, half), BF16, anywhere),
        ((half, width), BF16, anywhere),
    )
    return pl.pallas_call(
        functools.partial(expert_kernel, n, pad),
        out_shape=[jax.ShapeDtypeStruct(shape, dtype) for shape, dtype, _ in shapes],
        in_specs=[anywhere, anywhere, vmem] + [anywhere] * 4,
        out_specs=[space for _, _, space in shapes],
        scratch_shapes=[
            pltpu.VMEM((rows, width), BF16),
            pltpu.VMEM((n, 8, LANES), F32),
            pltpu.VMEM((rows, width), BF16),
            pltpu.VMEM((2 * parts, width, HIDDEN), BF16),
            pltpu.VMEM((2 * parts, HIDDEN, width), BF16),
            pltpu.VMEM((2 * parts, rows, HIDDEN), BF16),
            pltpu.VMEM((2 * parts, rows, HIDDEN), BF16),
            pltpu.VMEM((rows, width), BF16),
            pltpu.VMEM((n, 8, LANES), F32),
            pltpu.VMEM((ROWS, LANES), F32),
        ]
        + [pltpu.SemaphoreType.DMA((n,))] * 8
        + [
            pltpu.SemaphoreType.DMA((4 * parts,)),
            pltpu.SemaphoreType.DMA,
            pltpu.SemaphoreType.DMA((2 * parts,)),
            pltpu.SemaphoreType.DMA((2 * parts,)),
            pltpu.SemaphoreType.DMA((2 * parts,)),
            pltpu.VMEM((rows, width), BF16),
            pltpu.VMEM((rows, width), BF16),
            pltpu.SemaphoreType.DMA((2,)),
            pltpu.SemaphoreType.DMA((rows // ROWS,)),
        ],
        compiler_params=pltpu.CompilerParams(
            collective_id=1, has_side_effects=True, vmem_limit_bytes=60 * 1024 * 1024
        ),
        name="experts",
    )(xd, cr, gs, win, wout, win2, wout2)
def reduce_rows(n, width):
    return [-(-rows // (n * 16)) * 16 * n for rows in [3 * width] * 4 + [3 * n + 32]]


def reduce_stages(n, core):
    if n == 16:
        return [(1 + core, 2), (2 - core, 2), (4, 4)]
    return [(1 + core, 2), (2 - core, 2)] + [(2**s, 2) for s in range(2, n.bit_length() - 1)]


def reduce_shapes(n, width):
    stages = reduce_stages(n, 0)
    scratch = []
    for rows in reduce_rows(n, width):
        scratch.append(pltpu.VMEM((rows, LANES), BF16))
        for _, radix in stages:
            rows //= radix
            scratch.append(pltpu.VMEM((radix - 1, rows, LANES), BF16))
        scratch += [pltpu.SemaphoreType.DMA((2 * len(stages) + 2, 3))] * 2
    return scratch


def reduce_steps(n, me, core, part, total, scratch, finish):
    stages = reduce_stages(n, core)
    arrived, *halves = scratch[:-2]
    sends, recvs = scratch[-2:]
    unit = part.shape[1] // n
    count = len(stages)
    spots, starts, sizes = [], [0], [n]
    for distance, radix in stages:
        spot = lax.rem(me // distance, radix)
        spots.append(spot)
        sizes.append(sizes[-1] // radix)
        starts.append(starts[-1] + spot * sizes[-1])

    def region(start, units):
        return pl.ds(pl.multiple_of(start * unit, 16), units * unit)

    def copy(step, slot, src, dst, device):
        return pltpu.make_async_remote_copy(
            src_ref=src,
            dst_ref=dst,
            send_sem=sends.at[step, slot],
            recv_sem=recvs.at[step, slot],
            device_id=device,
            device_id_type=MESH,
        )

    def transfers(step):
        sibling = (me, 1 - core)
        if step == 0:
            return [copy(step, 0, part.at[1 - core], arrived, sibling)]
        if step == 2 * count + 1:
            held = total.at[core]
            return [copy(step, 0, held, held, sibling)]
        s = step - 1 if step <= count else 2 * count - step
        distance, radix = stages[s]
        made = []
        for slot in range(radix - 1):
            spot = lax.rem(spots[s] + slot + 1, radix)
            device = (me + distance * (spot - spots[s]), core)
            if step <= count:
                away = part.at[core, region(starts[s] + spot * sizes[s + 1], sizes[s + 1])]
                made.append(copy(step, slot, away, halves[s].at[slot], device))
            else:
                held = total.at[core, region(starts[s + 1], sizes[s + 1])]
                made.append(copy(step, slot, held, held, device))
        return made

    def add(step):
        if step == 0:
            mine, others = slice(None), [arrived[...]]
        elif step <= count:
            s = step - 1
            mine = region(starts[s + 1], sizes[s + 1])
            others = [halves[s][slot] for slot in range(stages[s][1] - 1)]
        else:
            return
        summed = part[core, mine, :].astype(F32)
        for other in others:
            summed = summed + other.astype(F32)
        if step == count:
            total[core, mine, :] = summed.astype(BF16)
        else:
            part[core, mine, :] = summed.astype(BF16)

    last = 2 * count + 1

    def run(step):
        if step > 0:
            for transfer in transfers(step - 1):
                transfer.wait_recv()
            add(step - 1)
        if step <= last:
            for transfer in transfers(step):
                transfer.start()
        else:
            finish()
            for done in range(last + 1):
                for transfer in transfers(done):
                    transfer.wait_send()

    return [functools.partial(run, step) for step in range(last + 2)]


def reducers(n, me, core, parts, totals, scratch, finish):
    size = len(reduce_stages(n, core)) + 3
    return [
        reduce_steps(
            n, me, core, part, total, scratch[j * size : (j + 1) * size], functools.partial(finish, j)
        )
        for j, (part, total) in enumerate(zip(parts, totals))
    ]


def unroll_band(band):
    wide = band.shape[1]
    folded = band[:8]
    for g in range(1, band.shape[0] // 8):
        folded = folded + pltpu.roll(band[8 * g : 8 * g + 8], wide - 8 * g, 1)
    line = folded[:1]
    for s in range(1, 8):
        line = line + pltpu.roll(folded, wide - s, 1)[s : s + 1]
    return line


PLAN = (
    (0,),
    ((), (), (), (), (), ()),
    ((1, 0), (2, 1, 0), (3, 2, 1, 0)),
    (3, 2, 1, 0),
    (4, 3, 2, 1, 0),
)


def back_kernel(
    n, pad,
    tok_hbm, ga_ref, wq_hbm, wk_hbm, wv_hbm, wo_hbm, gf_ref, wrt_ref, routes_ref, cot_hbm, st_hbm, gx_hbm, gg_ref, p_ref,
    nat_hbm, qt_hbm, kt_hbm, v_hbm, probs_hbm, mixt_hbm, hid_hbm, nf_hbm, pr_ref, gcol_ref,
    out_hbm, dx_hbm, total0_hbm, totals_hbm, total4_hbm,
    got_ref, probs_ref, gmt_ref, gqt_ref, gkt_ref, gvt_ref, lines_ref,
    send_sem, recv_sem, probs_sem, own_sem, part0, part1, part2, part3, part4,
    tok_ref, wq_ref, wk_ref, wv_ref, wo_ref, cot_ref, st_ref, gx_ref, nat_ref, qt_ref, kt_ref, v_ref, mixt_ref, hid_ref, nf_ref,
    out_ref, dx_ref, total0, totals, total4, load_sem, save_sem, *reduce_scratch,
):
    me = lax.axis_index("expert")
    core = lax.axis_index("ffn")
    count, width = tok_ref.shape
    rows_all = n * pad
    barrier = greet(n, me, core, True)
    need = fetch(
        load_sem,
        (st_hbm, st_ref), (gx_hbm, gx_ref), (nf_hbm, nf_ref), (hid_hbm, hid_ref), (cot_hbm, cot_ref), (mixt_hbm, mixt_ref),
        (wo_hbm, wo_ref), (v_hbm, v_ref), (kt_hbm, kt_ref), (qt_hbm, qt_ref), (nat_hbm, nat_ref), (wq_hbm, wq_ref),
        (wk_hbm, wk_ref), (wv_hbm, wv_ref), (tok_hbm, tok_ref),
    )

    def load(pair):
        return pltpu.make_async_copy(
            probs_hbm.at[pl.ds(2 * pair, 2)], probs_ref.at[pair % 2], probs_sem.at[pair % 2]
        )

    load(0).start()
    load(1).start()

    def rows_of(e):
        return pl.ds(pl.multiple_of(e * pad, pad), pad)

    def copy(k):
        target = partner(n, me, k)
        return pltpu.make_async_remote_copy(
            src_ref=p_ref.at[rows_of(target)],
            dst_ref=got_ref.at[rows_of(me)],
            send_sem=send_sem.at[k],
            recv_sem=recv_sem.at[k],
            device_id=(target, core),
            device_id_type=MESH,
        )

    pl.semaphore_wait(barrier, n)
    each(n, lambda k: copy(k).start())
    own = pltpu.make_async_copy(p_ref.at[rows_of(me)], got_ref.at[rows_of(me)], own_sem)
    own.start()
    parts = (part0, part1, part2, part3, part4)
    queue = reducers(
        n, me, core, parts, [total0, totals.at[0], totals.at[1], totals.at[2], total4], reduce_scratch,
        lambda j: kept[j].start(),
    )
    done = [0] * 5
    kept = [pltpu.make_async_copy(total0, total0_hbm, save_sem.at[0])]
    for g in range(3):
        kept.append(pltpu.make_async_copy(totals.at[g], totals_hbm.at[g], save_sem.at[g + 1]))
    kept.append(pltpu.make_async_copy(total4, total4_hbm, save_sem.at[4]))
    kept.append(pltpu.make_async_copy(dx_ref, dx_hbm, save_sem.at[5]))
    kept.append(pltpu.make_async_copy(out_ref, out_hbm, save_sem.at[6]))

    def tick(*chosen):
        for j in chosen:
            if done[j] < len(queue[j]):
                queue[j][done[j]]()
                done[j] += 1

    base = 3 * width
    for part, filled in zip(parts, [base] * 4 + [3 * n + 32]):
        if part.shape[1] > filled:
            part[:, filled:, :] = jnp.zeros((2, part.shape[1] - filled, LANES), BF16)

    share = LANES // pad
    tiles = []
    for t in range(n // share):
        tile = gg_ref[t * share][:1]
        for u in range(1, share):
            tile = tile + gg_ref[t * share + u][:1]
        tiles.append(tile)
    marks = jnp.concatenate(tiles, axis=1)
    need(0)
    grad_gate = jnp.sum(dot(pieces(marks), st_ref[...], 1, 1), axis=0, keepdims=True)
    chosen = (iota((n, count), 0) == routes_ref[...]).astype(F32)
    router = pr_ref[...]
    grad_probs = chosen * grad_gate
    grad_logits = router * (grad_probs - jnp.sum(router * grad_probs, axis=0, keepdims=True))
    grad_logits = grad_logits.astype(BF16)
    need(1, 2)
    grad_router = dot(nf_ref[...], grad_logits, 0, 1).T
    grad_nf = dot(st_ref[...], gx_ref[...]) + dot(grad_logits, wrt_ref[...], 0, 0)
    need(3, 4)
    hidden = hid_ref[...]
    scale = lax.rsqrt(jnp.mean(hidden * hidden, axis=-1, keepdims=True) + EPSILON)
    weighted = grad_nf * gf_ref[...][None]
    grad_gain_ffn = jnp.sum(grad_nf * hidden * scale, axis=0, keepdims=True)
    inner = jnp.mean(weighted * hidden, axis=-1, keepdims=True)
    grad_hidden = (
        cot_ref[...].astype(F32) + scale * weighted - hidden * (scale * scale * scale * inner)
    )
    dx_ref[...] = grad_hidden
    branch = grad_hidden.astype(BF16)
    need(5)
    for t in range(width // LANES):
        cut = slice(t * LANES, (t + 1) * LANES)
        rows = slice(t % 3 * width, (t % 3 + 1) * width)
        part0[t // 3, rows, :] = dot(mixt_ref[...], branch[:, cut]).astype(BF16)
    tick(*PLAN[0])
    need(6)
    gmt_ref[...] = dot(wo_ref[...], branch, 1, 1).astype(BF16)
    need(7, 8, 9)
    lines_ref[...] = jnp.zeros_like(lines_ref)
    lower_half = iota((LANES, count), 0) < HEAD_DIM
    blocks = count // LANES
    place = iota((1, 4 * LANES), 1)

    def run_pair(pair):
        load(pair).wait()
        lanes = pl.ds(pair * LANES, LANES)
        both = gmt_ref[lanes, :]
        for sub in range(2):
            head = 2 * pair + sub
            mask = lower_half if sub == 0 else jnp.logical_not(lower_half)
            chunk = jnp.where(mask, both, jnp.zeros_like(both))
            features = pl.ds(head * HEAD_DIM, HEAD_DIM)
            grad_mixed = gmt_ref[features, :]
            delta = jnp.sum(
                grad_mixed.astype(F32) * mixt_ref[features, :].astype(F32), axis=0, keepdims=True
            )
            probs = probs_ref[pair % 2, sub]
            grad_probs = dot(v_ref[:, lanes], chunk)
            scores = probs.astype(F32) * (grad_probs - delta)
            low = scores.astype(BF16)
            gqt_ref[features, :] = dot(kt_ref[features, :], low).astype(BF16)
            gkt_ref[features, :] = dot(qt_ref[features, :], low, 1, 1).astype(BF16)
            gvt_ref[features, :] = dot(grad_mixed, probs, 1, 1).astype(BF16)
            near = {0: None, -1: None, 1: None}
            far = {-1: None, 1: None}
            for row in range(blocks):
                for col in range(blocks):
                    block = scores[
                        row * LANES : (row + 1) * LANES, col * LANES : (col + 1) * LANES
                    ]
                    gap = row - col
                    if gap in near:
                        near[gap] = block if near[gap] is None else near[gap] + block
                    else:
                        side = 1 if gap > 0 else -1
                        far[side] = block if far[side] is None else far[side] + block
            band = jnp.concatenate([near[0], near[-1], jnp.zeros_like(near[0]), near[1]], axis=1)
            line = unroll_band(band)
            for side, lane in ((-1, 255), (1, 257)):
                total = jnp.sum(jnp.sum(far[side], axis=0, keepdims=True), axis=1, keepdims=True)
                line = line + jnp.where(place == lane, total, 0.0)
            lines_ref[pl.ds(head, 1), :] = line
        if pair + 2 < HEADS // 2:
            load(pair + 2).start()

    for group, part in enumerate((part1, part2, part3)):
        for pair in (2 * group, 2 * group + 1):
            run_pair(pair)
            tick(*PLAN[1][pair])
        if group == 0:
            need(10)
        for i, grad in enumerate((gqt_ref, gkt_ref, gvt_ref)):
            columns = grad[group * 2 * LANES : (group + 1) * 2 * LANES, :]
            made = dot(nat_ref[...], columns, 1, 1).astype(BF16)
            for c in range(2):
                part[c, i * width : (i + 1) * width, :] = made[:, c * LANES : (c + 1) * LANES]
        tick(*PLAN[2][group])
    need(11, 12, 13, 14)
    grad_na = (
        dot(wq_ref[...], gqt_ref[...])
        + dot(wk_ref[...], gkt_ref[...])
        + dot(wv_ref[...], gvt_ref[...])
    ).T
    x = tok_ref[...].astype(F32)
    scale = lax.rsqrt(jnp.mean(x * x, axis=-1, keepdims=True) + EPSILON)
    weighted = grad_na * ga_ref[...][None]
    grad_gain_attn = jnp.sum(grad_na * x * scale, axis=0, keepdims=True)
    inner = jnp.mean(weighted * x, axis=-1, keepdims=True)
    tick(*PLAN[3])
    dx_ref[...] = dx_ref[...] + scale * weighted - x * (scale * scale * scale * inner)
    kept[5].start()
    grad_bias = dot(band_onehot(), lines_ref[...], 1, 1, HIGH)
    gains = jnp.concatenate([grad_gain_attn, grad_gain_ffn, jnp.zeros((14, width), F32)], axis=0)
    for c in range(2):
        for t in range(3):
            cut = slice((3 * c + t) * LANES, (3 * c + t + 1) * LANES)
            part4[c, t * n : (t + 1) * n, :] = grad_router[:, cut].astype(BF16)
        rows = slice(3 * n, 3 * n + 16)
        sums = [gains[:, (3 * c + t) * LANES : (3 * c + t + 1) * LANES][:2] for t in range(3)]
        part4[c, rows, :] = jnp.concatenate(sums + [jnp.zeros((10, LANES), F32)], axis=0).astype(BF16)
        rows = slice(3 * n + 16, 3 * n + 32)
        wide = jnp.concatenate(
            [grad_bias[16 * c : 16 * c + 16], jnp.zeros((16, LANES - 16), F32)], axis=1
        )
        part4[c, rows, :] = wide.astype(BF16)
    tick(*PLAN[4])
    own.wait()
    each(n, lambda k: copy(k).wait())
    picked = dot(st_ref[...], got_ref[...])
    out_ref[...] = (hid_ref[...] + gcol_ref[:, :1] * picked).astype(BF16)
    kept[6].start()
    while any(done[j] < len(queue[j]) for j in range(5)):
        tick(4, 3, 2, 1, 0)
    for copied in kept:
        copied.wait()


def run_back(n, pad, tokens, *rest):
    count, width = tokens.shape
    rows = n * pad
    vmem = pl.BlockSpec(memory_space=pltpu.VMEM)
    anywhere = pl.BlockSpec(memory_space=pl.ANY)
    shapes = (
        ((count, width), BF16, anywhere),
        ((count, width), F32, anywhere),
        ((2, reduce_rows(n, width)[0], LANES), BF16, anywhere),
        ((3, 2, reduce_rows(n, width)[0], LANES), BF16, anywhere),
        ((2, reduce_rows(n, width)[4], LANES), BF16, anywhere),
    )
    return pl.pallas_call(
        functools.partial(back_kernel, n, pad),
        out_shape=[jax.ShapeDtypeStruct(shape, dtype) for shape, dtype, _ in shapes],
        in_specs=[anywhere, vmem]
        + [anywhere] * 4
        + [vmem] * 3
        + [anywhere] * 3
        + [vmem]
        + [anywhere] * 9
        + [vmem] * 2,
        out_specs=[space for _, _, space in shapes],
        scratch_shapes=[
            pltpu.VMEM((rows, width), BF16),
            pltpu.VMEM((2, 2, count, count), BF16),
            pltpu.VMEM((width, count), BF16),
            pltpu.VMEM((width, count), BF16),
            pltpu.VMEM((width, count), BF16),
            pltpu.VMEM((width, count), BF16),
            pltpu.VMEM((16, 4 * LANES), F32),
            pltpu.SemaphoreType.DMA((n,)),
            pltpu.SemaphoreType.DMA((n,)),
            pltpu.SemaphoreType.DMA((2,)),
            pltpu.SemaphoreType.DMA,
            *(pltpu.VMEM((2, part, LANES), BF16) for part in reduce_rows(n, width)),
            pltpu.VMEM((count, width), BF16),
            *[pltpu.VMEM((width, width), BF16)] * 4,
            pltpu.VMEM((count, width), BF16),
            pltpu.VMEM((count, rows), BF16),
            pltpu.VMEM((rows, width), BF16),
            *[pltpu.VMEM((width, count), BF16)] * 3,
            pltpu.VMEM((count, width), BF16),
            pltpu.VMEM((width, count), BF16),
            pltpu.VMEM((count, width), F32),
            pltpu.VMEM((count, width), BF16),
            *[pltpu.VMEM(shape, dtype) for shape, dtype, _ in shapes],
            pltpu.SemaphoreType.DMA((15,)),
            pltpu.SemaphoreType.DMA((7,)),
            *reduce_shapes(n, width),
        ],
        compiler_params=pltpu.CompilerParams(
            collective_id=2, has_side_effects=True, vmem_limit_bytes=63 * 1024 * 1024
        ),
        name="attend_back",
    )(tokens, *rest)


def finish_kernel(
    n,
    first0, first1, first2, q_ref, k_ref, v_ref, small_ref, own_in, got_in, own_out, got_out, out_ref, dx_ref, rms_ref,
    go_ref, gq_ref, gk_ref, gv_ref, gi_ref, gw_ref, router_ref, gain_a, gain_f, bias_ref, output_ref, grad_ref, roots_ref,
):
    for t in range(6):
        cut = slice(t * LANES, (t + 1) * LANES)
        go_ref[:, cut] = (first0, first1, first2)[t % 3][t // 3].astype(F32)
        for made, grad in ((gq_ref, q_ref), (gk_ref, k_ref), (gv_ref, v_ref)):
            made[:, cut] = grad[t // 2, t % 2].astype(F32)
    gi_ref[...] = own_in[...].astype(F32) + got_in[...].astype(F32)
    gw_ref[...] = own_out[...].astype(F32) + got_out[...].astype(F32)
    output_ref[...] = out_ref[...]
    grad_ref[...] = dx_ref[...]

    @pl.when(pl.program_id(0) == 0)
    def _():
        roots_ref[...] = rms_ref[3:5, :]
        small = small_ref[...].astype(F32)
        for t in range(6):
            c, at = t // 3, t % 3
            cut = slice(t * LANES, (t + 1) * LANES)
            router_ref[:, cut] = small[c, at * n : (at + 1) * n]
            gain_a[cut] = small[c, 3 * n + 2 * at]
            gain_f[cut] = small[c, 3 * n + 2 * at + 1]
        bias = jnp.concatenate([small[c, 3 * n + 16 : 3 * n + 32] for c in range(2)], axis=0)
        bias_ref[...] = bias.T[:HEADS]


def run_finish(n, first, groups, smalls, own_in, got_in, own_out, got_out, out, dx, rms):
    width, half = own_in.shape
    count = out.shape[0]
    steps = 3
    rows = width // steps
    whole = lambda *shape: pl.BlockSpec(shape, lambda t: (0,) * len(shape))
    by_rows = lambda rows, columns: pl.BlockSpec((rows, columns), lambda t: (t, 0))
    out_part = lambda i: pl.BlockSpec((2, rows, LANES), lambda t: (0, i * steps + t, 0))
    weight = lambda i: pl.BlockSpec((3, 2, rows, LANES), lambda t: (0, 0, i * steps + t, 0))
    grad_shape = jax.ShapeDtypeStruct((width, width), F32)
    some = pl.BlockSpec((count // 2, width), lambda t: (jnp.minimum(t, 1), 0))
    rows_in, rows_out = by_rows(rows, half), by_rows(half // steps, width)
    return pl.pallas_call(
        functools.partial(finish_kernel, n),
        grid=(steps,),
        out_shape=[
            grad_shape,
            grad_shape,
            grad_shape,
            grad_shape,
            jax.ShapeDtypeStruct((width, half), F32),
            jax.ShapeDtypeStruct((half, width), F32),
            jax.ShapeDtypeStruct((n, width), F32),
            jax.ShapeDtypeStruct((width,), F32),
            jax.ShapeDtypeStruct((width,), F32),
            jax.ShapeDtypeStruct((HEADS, BUCKETS), F32),
            jax.ShapeDtypeStruct((count, width), BF16),
            jax.ShapeDtypeStruct((count, width), F32),
            jax.ShapeDtypeStruct((2, count), F32),
        ],
        in_specs=[out_part(i) for i in range(3)]
        + [weight(i) for i in range(3)]
        + [whole(*smalls.shape), rows_in, rows_in, rows_out, rows_out, some, some, whole(8, count)],
        out_specs=[by_rows(rows, width)] * 4
        + [rows_in, rows_out]
        + [whole(n, width), whole(width), whole(width), whole(HEADS, BUCKETS)]
        + [some, some, whole(2, count)],
        compiler_params=pltpu.CompilerParams(vmem_limit_bytes=60 * 1024 * 1024),
        name="finish",
    )(first, first, first, groups, groups, groups, smalls, own_in, got_in, own_out, got_out, out, dx, rms)


def per_device(
    tokens, gain_attn, query_weight, key_weight, value_weight, out_weight, rel_bias, gain_ffn, router_weight,
    expert_in, expert_out, routes, capacity, cotangent,
):
    count, width = tokens.shape
    n = lax.axis_size("expert")
    experts = router_weight.shape[1]
    assert experts == n and count == SEQ
    slots = 2 * count // experts
    pad = -(-slots // 16) * 16
    router_rows = router_weight.T
    routes = routes.reshape(1, count)
    (
        cots, in_other, out_other, dispatched, gates, slots_t, normed_t, query_t, key_t, values, probs, mixed_t,
        hidden, normed_ffn, router_t, gate_col, roots,
    ) = attend(
        n, slots, pad, tokens, gain_attn, query_weight, key_weight, value_weight, out_weight, rel_bias.T, gain_ffn,
        router_rows, routes, capacity, cotangent, expert_in[0], expert_out[0],
    )
    grad_rows, marks, produced, own_in, own_out, got_in, got_out = run_experts(
        n, pad, dispatched, cots, gates, expert_in[0], expert_out[0], in_other, out_other
    )
    output, input_grad, first, groups, smalls = run_back(
        n, pad, tokens, gain_attn, query_weight, key_weight, value_weight, out_weight, gain_ffn, router_rows, routes,
        cotangent, slots_t, grad_rows, marks, produced, normed_t, query_t, key_t, values, probs, mixed_t, hidden,
        normed_ffn, router_t, gate_col,
    )
    (
        grad_out, grad_query, grad_key, grad_value, grad_in, grad_expert, grad_router, grad_gain_attn, grad_gain_ffn,
        grad_bias, output, input_grad, rms_values,
    ) = run_finish(n, first, groups, smalls, own_in, got_in, own_out, got_out, output, input_grad, roots)
    return (
        output,
        input_grad,
        grad_gain_attn,
        grad_query,
        grad_key,
        grad_value,
        grad_out,
        grad_bias.T,
        grad_gain_ffn,
        grad_router.T,
        grad_in[None],
        grad_expert[None],
        rms_values,
    )


def solution(mesh):
    placed = (
        P(("expert", "ffn"), None),
        P(),
        P(),
        P(),
        P(),
        P(),
        P(),
        P(),
        P(),
        P("expert", None, "ffn"),
        P("expert", "ffn", None),
        P(("expert", "ffn"), None),
        P(("expert", "ffn")),
        P(("expert", "ffn"), None),
    )
    return jax.shard_map(
        per_device,
        mesh=mesh,
        in_specs=placed,
        out_specs=(
            P(("expert", "ffn"), None),
            P(("expert", "ffn"), None),
            P(),
            P(),
            P(),
            P(),
            P(),
            P(),
            P(),
            P(),
            P("expert", None, "ffn"),
            P("expert", "ffn", None),
            P(None, ("expert", "ffn")),
        ),
        check_vma=False,
    )
```
